32 devices in a mesh: level: 4 (over z), blocks: 8 (over y, x, core).
Axes of the slice: x: 2, y: 2, z: 4, core: 2. Of those that a mesh axis runs over, the one named last changes fastest.
Arguments:
- populations: float32 [4, 19, 64, 1024], P('level', None, 'blocks'), may hold values from 0.3 to 2, as said below
- solid: int32 [4, 64, 1024], P('level', 'blocks'), may hold values from 0 to 1, as said below
Outputs:
- evolved: float32 [4, 19, 64, 1024], P('level', None, 'blocks')
The draws below stay inside these ranges and needn't reach their ends.
Inputs may be any that keep to these rules, and one draw needn't show every extreme that they name: Normalized populations of a state near equilibrium. `solid`: 1 marks a cell of a level whose centre lies inside one of 32 large or 64 small spheres, radii in the ratio 8, the same spheres on every level.
All inputs are finite; a program needn't handle non-finite values.
Results may differ from the reference program's by a relative error of at most 0.0001.
Values sent between devices are 32-bit elements; how exact they have to be, the bound alone decides.
No kernel may reach another device: no remote copies, remote signals or barrier semaphores. Data moves between devices by JAX's collectives and lax.ppermute only.
A program may use at most 192 MiB of HBM per device.

```python
import jax
import jax.numpy as jnp
import numpy as np
from jax import lax

NY = 32
NZ = 32
LEVELS = 4
NXS = 64
PLANE = 1024
BIG_SPHERES = 32
SMALL_SPHERES = 64


VELOCITY = ((0, 0, 0), (1, 0, 0), (-1, 0, 0), (0, 1, 0), (0, -1, 0), (0, 0, 1), (0, 0, -1), (1, 1, 0), (-1, -1, 0), (1, -1, 0), (-1, 1, 0), (1, 0, 1), (-1, 0, -1), (1, 0, -1), (-1, 0, 1), (0, 1, 1), (0, -1, -1), (0, 1, -1), (0, -1, 1))


def draw_populations(key, part):
    key = jax.random.fold_in(key, 11)
    subkeys = jax.random.split(key, 5)
    grid_shape = (LEVELS, NXS, PLANE)
    density = 1.0 + jnp.clip(0.04 * jax.random.normal(subkeys[0], grid_shape, jnp.float32), -0.1, 0.1)
    speeds = [jnp.clip(0.03 * jax.random.normal(subkeys[1 + component], grid_shape, jnp.float32), -0.08, 0.08) for component in range(3)]
    jitter = jnp.clip(0.02 * jax.random.normal(subkeys[4], (LEVELS, 19, NXS, PLANE), jnp.float32), -0.05, 0.05)
    speed_sq = speeds[0] ** 2 + speeds[1] ** 2 + speeds[2] ** 2
    result = []
    for direction in range(19):
        projection = VELOCITY[direction][0] * speeds[0] + VELOCITY[direction][1] * speeds[1] + VELOCITY[direction][2] * speeds[2]
        result.append(density * (1.0 + 3.0 * projection + 4.5 * projection * projection - 1.5 * speed_sq))
    return (jnp.stack(result, axis=1) + jitter).astype(jnp.float32)


def draw_solid(key, part):
    key = jax.random.fold_in(key, 23)
    subkeys = jax.random.split(key, 3)
    sphere_count = BIG_SPHERES + SMALL_SPHERES
    centre_x = jax.random.randint(subkeys[0], (sphere_count,), 0, NXS * 16)
    centre_y = jax.random.randint(subkeys[1], (sphere_count,), 4 * NY, 12 * NY)
    centre_z = jax.random.randint(subkeys[2], (sphere_count,), 0, NZ // 4)
    radius = jnp.where(jnp.arange(sphere_count) < BIG_SPHERES, 32, 4).astype(jnp.int32)
    level_masks = []
    for level_id in range(LEVELS):
        half_cell = 2 ** (3 - level_id)
        rows_level = NXS * 2 ** level_id
        nz_level = NZ // 2 ** level_id
        plane_level = PLANE // 2 ** level_id
        anchor = 8 * NY - 8 * NY // 2 ** level_id
        x_centres = (2 * jnp.arange(rows_level, dtype=jnp.int32) + 1) * half_cell
        positions = jnp.arange(plane_level, dtype=jnp.int32)
        y_centres = anchor + (2 * (positions // nz_level) + 1) * half_cell
        z_centres = (2 * (positions % nz_level) + 1) * half_cell

        def add_sphere(sphere_id, inside):
            x_gap = (x_centres - centre_x[sphere_id]) ** 2
            yz_gap = (y_centres - centre_y[sphere_id]) ** 2 + (z_centres - centre_z[sphere_id]) ** 2
            return inside | (x_gap[:, None] + yz_gap[None, :] <= radius[sphere_id] ** 2)
        inside = lax.fori_loop(0, sphere_count, add_sphere, jnp.zeros((rows_level, plane_level), jnp.bool_))
        level_masks.append(inside.astype(jnp.int32).reshape(NXS, PLANE))
    return jnp.stack(level_masks)


def setup_inputs(seed: int = 0) -> dict:
    streams_of = jax.random.split(jax.random.key(seed), 3)
    populations = draw_populations(jax.random.fold_in(streams_of[2], 71), 0)
    solid = draw_solid(jax.random.fold_in(streams_of[2], 71), 0)
    return dict(populations=populations, solid=solid)


VELOCITY = ((0, 0, 0), (1, 0, 0), (-1, 0, 0), (0, 1, 0), (0, -1, 0), (0, 0, 1), (0, 0, -1),
            (1, 1, 0), (-1, -1, 0), (1, -1, 0), (-1, 1, 0), (1, 0, 1), (-1, 0, -1), (1, 0, -1),
            (-1, 0, 1), (0, 1, 1), (0, -1, -1), (0, 1, -1), (0, -1, 1))
WEIGHTS = (1.0 / 3.0,) + (1.0 / 18.0,) * 6 + (1.0 / 36.0,) * 12
OPPOSITE = (0, 2, 1, 4, 3, 6, 5, 8, 7, 10, 9, 12, 11, 14, 13, 16, 15, 18, 17)
TAU_BASE = 1.0


def relaxation(level_id):
    return (2.0 ** level_id) * (TAU_BASE - 0.5) + 0.5


def equilibrium(values):
    density = sum(WEIGHTS[direction] * values[direction] for direction in range(19))
    velocity_list = []
    for component in range(3):
        momentum = sum(WEIGHTS[direction] * VELOCITY[direction][component] * values[direction]
                       for direction in range(19) if VELOCITY[direction][component] != 0)
        velocity_list.append(momentum / density)
    speed_sq = velocity_list[0] ** 2 + velocity_list[1] ** 2 + velocity_list[2] ** 2
    result = []
    for direction in range(19):
        projection = sum(VELOCITY[direction][component] * velocity_list[component]
                         for component in range(3) if VELOCITY[direction][component] != 0)
        result.append(density * (1.0 + 3.0 * projection + 4.5 * projection * projection - 1.5 * speed_sq))
    return jnp.stack(result)


def collide(values, solid_level, tau_value):
    balance = equilibrium(values)
    relaxed = values + (balance - values) / tau_value
    flipped = jnp.stack([values[OPPOSITE[direction]] for direction in range(19)])
    return jnp.where(solid_level[None] == 1, flipped, relaxed)


def finish_stream(sources, collided, ny_cells, nz_level):
    positions = jnp.arange(ny_cells * nz_level, dtype=jnp.int32)
    y_index = positions // nz_level
    z_index = positions % nz_level
    result = []
    for direction in range(19):
        step_y = VELOCITY[direction][1]
        step_z = VELOCITY[direction][2]
        shifted = jnp.roll(sources[direction], step_y * nz_level + step_z, axis=1)
        inside = (y_index - step_y >= 0) & (y_index - step_y < ny_cells) & (z_index - step_z >= 0) & (z_index - step_z < nz_level)
        result.append(jnp.where(inside[None, :], shifted, collided[OPPOSITE[direction]]))
    return jnp.stack(result)


def interface_plan(ny_cells, child_nz):
    quarter = child_nz // 2
    targets = list(range(child_nz)) + list(range((ny_cells - 1) * child_nz, ny_cells * child_nz))
    targets += [y_row * child_nz + child_nz - 1 for y_row in range(1, ny_cells - 1)]
    picks = [z_row // 2 for z_row in range(child_nz)] + [quarter + z_row // 2 for z_row in range(child_nz)]
    picks += [2 * quarter + y_row // 2 for y_row in range(1, ny_cells - 1)]
    return np.array(targets, np.int32), np.array(picks, np.int32)


def make_packet(level_field, ny_cells, parent_nz, level_id):
    grid_view = level_field.reshape(19, level_field.shape[1], ny_cells, parent_nz)
    quarter = parent_nz // 4
    rim_values = jnp.concatenate([grid_view[:, :, ny_cells // 4, :quarter],
                                  grid_view[:, :, 3 * ny_cells // 4 - 1, :quarter],
                                  grid_view[:, :, ny_cells // 4:3 * ny_cells // 4, quarter - 1]], axis=2)
    balance = equilibrium(rim_values)
    scaling = relaxation(level_id + 1) / (2.0 * relaxation(level_id))
    return balance + scaling * (rim_values - balance)


def apply_interface(level_field, packet, ny_cells, child_nz):
    targets, picks = interface_plan(ny_cells, child_nz)
    widened = jnp.repeat(packet, 2, axis=1)
    return level_field.at[:, :, targets].set(widened[:, :, picks])


def restrict_packet(level_field, ny_cells, child_nz, level_id):
    parent_rows = level_field.shape[1] // 2
    grid_view = level_field.reshape(19, parent_rows, 2, ny_cells // 2, 2, child_nz // 2, 2)
    averaged = grid_view.sum(axis=(2, 4, 6)) / 8.0
    balance = equilibrium(averaged)
    scaling = 2.0 * relaxation(level_id - 1) / relaxation(level_id)
    restored = balance + scaling * (averaged - balance)
    return restored.reshape(19, parent_rows, (ny_cells // 2) * (child_nz // 2))


def overwrite(level_field, packet, ny_cells, parent_nz):
    parent_rows = level_field.shape[1]
    quarter = parent_nz // 4
    grid_view = level_field.reshape(19, parent_rows, ny_cells, parent_nz)
    grid_view = grid_view.at[:, :, ny_cells // 4:3 * ny_cells // 4, :quarter].set(
        packet.reshape(19, parent_rows, ny_cells // 2, quarter))
    return grid_view.reshape(19, parent_rows, ny_cells * parent_nz)


def roster(level_id, level_count):
    events = [("step", level_id)]
    if level_id + 1 < level_count:
        for repeat in range(2):
            events += roster(level_id + 1, level_count)
        events.append(("restrict", level_id + 1))
    return events


def reference(populations, solid):
    fields = [populations[level_id].reshape(19, NXS * 2 ** level_id, PLANE // 2 ** level_id) for level_id in range(LEVELS)]
    solid_levels = [solid[level_id].reshape(NXS * 2 ** level_id, PLANE // 2 ** level_id) for level_id in range(LEVELS)]
    packets = {}
    for event_kind, level_id in roster(0, LEVELS):
        nz_level = NZ // 2 ** level_id
        if event_kind == "step":
            level_field = fields[level_id]
            if level_id > 0:
                level_field = apply_interface(level_field, packets[level_id], NY, nz_level)
            collided = collide(level_field, solid_levels[level_id], relaxation(level_id))
            sources = [jnp.roll(collided[direction], VELOCITY[direction][0], axis=0) for direction in range(19)]
            level_field = finish_stream(sources, collided, NY, nz_level)
            fields[level_id] = level_field
            if level_id + 1 < LEVELS:
                packets[level_id + 1] = make_packet(level_field, NY, nz_level, level_id)
        else:
            packet = restrict_packet(fields[level_id], NY, nz_level, level_id)
            fields[level_id - 1] = overwrite(fields[level_id - 1], packet, NY, 2 * nz_level)
    return jnp.stack([fields[level_id].reshape(19, NXS, PLANE) for level_id in range(LEVELS)])
```

```python
import jax
import jax.numpy as jnp
import numpy as np
from jax import lax
from jax.experimental import pallas as pl
from jax.experimental.pallas import tpu as pltpu
from jax.sharding import PartitionSpec as P

NY = 32
NZ = 32
LEVELS = 4
SLAB = 8
LANES = 128
VELOCITY = (
    (0, 0, 0),
    (1, 0, 0),
    (-1, 0, 0),
    (0, 1, 0),
    (0, -1, 0),
    (0, 0, 1),
    (0, 0, -1),
    (1, 1, 0),
    (-1, -1, 0),
    (1, -1, 0),
    (-1, 1, 0),
    (1, 0, 1),
    (-1, 0, -1),
    (1, 0, -1),
    (-1, 0, 1),
    (0, 1, 1),
    (0, -1, -1),
    (0, 1, -1),
    (0, -1, 1),
)
OPPOSITE = (0, 2, 1, 4, 3, 6, 5, 8, 7, 10, 9, 12, 11, 14, 13, 16, 15, 18, 17)
TAU_BASE = 1.0
F32 = jnp.float32
BF16 = jnp.bfloat16

PAD = 8
MARGIN = (8, 8, 8, 16)
FACTOR = (1, 2, 4, 8)
CHUNKS = (8, 4, 2, 1)
DEPTH = (32, 16, 8, 4)
OWN = tuple(SLAB * f for f in FACTOR)
ROW0 = tuple(PAD + m for m in MARGIN)
ROWS = tuple(OWN[l] + 2 * ROW0[l] for l in range(LEVELS))

Y_LOW = NY // 4
Y_HIGH = 3 * NY // 4 - 1


def zone_lane(level, y, z):
    if level == 0:
        return (y - 8) * 8 + z
    if level == 1:
        return z * 20 + y - 6
    return z * 25 + y - 4


ZONE_CELLS = (
    [(y, z) for y in range(8, 24) for z in range(8)],
    [(y, z) for y in range(6, 26) for z in range(6)],
    [(y, z) for y in range(5, 27) for z in range(5)],
)
ZONE_PITCH = (None, 20, 25)


def level_lane(level, y, z):
    return y * DEPTH[level] + z


def one_hot(pairs, inputs, outputs, weight=1.0):
    m = np.zeros((inputs, outputs), np.float32)
    for i, o in pairs:
        m[i, o] = weight
    return m


def pack_matrix(level):
    return one_hot(
        [(level_lane(level, y, z), zone_lane(level, y, z)) for y, z in ZONE_CELLS[level]],
        CHUNKS[level] * LANES,
        LANES,
    )


def interface_matrix(child):
    nz = DEPTH[child]
    pairs = [
        (zone_lane(child - 1, 8 + y // 2, z // 2), level_lane(child, y, z))
        for y in range(NY)
        for z in range(nz)
        if y in (0, NY - 1) or z == nz - 1
    ]
    return one_hot(pairs, LANES, CHUNKS[child] * LANES)


def restrict_matrix(child):
    pairs = [
        (level_lane(child, y, z), zone_lane(child - 1, 8 + y // 2, z // 2))
        for y in range(NY)
        for z in range(DEPTH[child])
    ]
    return one_hot(pairs, CHUNKS[child] * LANES, LANES, 0.125)


def compact_matrix():
    m = np.zeros((4, LANES, LANES), np.float32)
    for i in range(4):
        for y in range(NY):
            for z in range(4):
                m[i, level_lane(3, y, z), 32 * i + (y // 2) * 2 + z // 2] = 0.125
    return m


def spread_matrix():
    m = np.zeros((LANES, 4, 2 * LANES), np.float32)
    for i in range(4):
        for y in range(16):
            for z in range(2):
                m[32 * i + y * 2 + z, i, level_lane(2, 8 + y, z)] = 1.0
    return m.reshape(LANES, 4 * 2 * LANES)


Z_OUT = (5, 11, 14, 15, 18)
Y_DOWN = (4, 8, 9, 16, 18)
Y_UP = (3, 7, 10, 15, 17)
FLOW_DIRECTIONS = tuple(sorted(set(Z_OUT + Y_DOWN + Y_UP)))


def flow_cells(q):
    cells = {}
    if q in Z_OUT:
        for y in range(8, 24):
            cells[(y, 1)] = 16 * Z_OUT.index(q) + y - 8
    for group, y, first in ((Y_DOWN, 8, 80), (Y_UP, 23, 85)):
        if q in group:
            for z in range(2):
                cells.setdefault((y, z), first + group.index(q) + 25 * z)
    return cells


def flow_matrix():
    m = np.zeros((LANES, len(FLOW_DIRECTIONS), 2 * LANES), np.float32)
    for k, q in enumerate(FLOW_DIRECTIONS):
        for (y, z), lane in flow_cells(q).items():
            m[lane, k, level_lane(2, y, z)] = 1.0
    return m.reshape(LANES, -1)


def spread_zone_matrix():
    pairs = [
        (zone_lane(1, y, z), level_lane(1, y, z)) for y in range(7, 25) for z in range(5)
    ]
    return one_hot(pairs, LANES, 4 * LANES)


def relaxation(level_id):
    return 2.0**level_id * (TAU_BASE - 0.5) + 0.5


def parent_scale(child):
    return relaxation(child) / (2.0 * relaxation(child - 1))


def child_scale(child):
    return 2.0 * relaxation(child - 1) / relaxation(child)


def relax(v, a, b):
    s = [None] + [v[2 * k - 1] + v[2 * k] for k in range(1, 10)]
    d = [None] + [v[2 * k - 1] - v[2 * k] for k in range(1, 10)]
    rho = (
        (1.0 / 3.0) * v[0]
        + (1.0 / 18.0) * (s[1] + s[2] + s[3])
        + (1.0 / 36.0) * ((s[4] + s[5]) + (s[6] + s[7]) + (s[8] + s[9]))
    )
    mx = (1.0 / 18.0) * d[1] + (1.0 / 36.0) * ((d[4] + d[5]) + (d[6] + d[7]))
    my = (1.0 / 18.0) * d[2] + (1.0 / 36.0) * ((d[4] - d[5]) + (d[8] + d[9]))
    mz = (1.0 / 18.0) * d[3] + (1.0 / 36.0) * ((d[6] - d[7]) + (d[8] - d[9]))
    inv = 1.0 / rho
    ux, uy, uz = mx * inv, my * inv, mz * inv
    ra = a * rho
    base = ra - (1.5 * ra) * (ux * ux + uy * uy + uz * uz)
    r45 = 4.5 * ra
    ra3 = 3.0 * ra

    def kept(q):
        return v[q] if b == 1.0 else b * v[q]

    out = [base if b == 0.0 else base + kept(0)]
    cus = (ux, uy, uz, ux + uy, ux - uy, ux + uz, ux - uz, uy + uz, uy - uz)
    for k in range(1, 10):
        cu = cus[k - 1]
        even = base + r45 * (cu * cu)
        odd = ra3 * cu
        plus, minus = even + odd, even - odd
        if b != 0.0:
            plus, minus = plus + kept(2 * k - 1), minus + kept(2 * k)
        out += [plus, minus]
    return out


def collided(v, solid, level):
    inv_tau = 1.0 / relaxation(level)
    relaxed = relax(v, inv_tau, 1.0 - inv_tau)
    flag = solid != 0.0
    return [jnp.where(flag, v[OPPOSITE[q]], relaxed[q]) for q in range(19)]


def lanes():
    return lax.broadcasted_iota(jnp.int32, (8, LANES), 1)


def interface_mask(level, c):
    lane = lanes()
    nz = DEPTH[level]
    mask = (lane & (nz - 1)) == nz - 1
    if c == 0:
        mask = mask | (lane < nz)
    if c == CHUNKS[level] - 1:
        mask = mask | (lane >= LANES - nz)
    return mask


def pulled(post, level, row, c):
    lane = lanes()
    nz, count = DEPTH[level], CHUNKS[level]
    out = []
    for q in range(19):
        cx, cy, cz = VELOCITY[q]
        shift = cy * nz + cz
        value = post[q, c, pl.ds(row - cx, 8), :]
        if shift != 0:
            value = pltpu.roll(value, shift % LANES, 1)
            outside = None
            if cy == 1:
                if c > 0:
                    other = pltpu.roll(post[q, c - 1, pl.ds(row - cx, 8), :], shift, 1)
                    value = jnp.where(lane < shift, other, value)
                else:
                    outside = lane < nz
            if cy == -1:
                if c < count - 1:
                    other = pltpu.roll(post[q, c + 1, pl.ds(row - cx, 8), :], shift % LANES, 1)
                    value = jnp.where(lane >= LANES + shift, other, value)
                else:
                    outside = lane >= LANES - nz
            if cz != 0:
                edge = (lane & (nz - 1)) == (0 if cz == 1 else nz - 1)
                outside = edge if outside is None else outside | edge
            if outside is not None:
                value = jnp.where(outside, post[OPPOSITE[q], c, pl.ds(row, 8), :], value)
        out.append(value)
    return out


def zone_pulled(post, level, row):
    lane = lanes()
    pitch = ZONE_PITCH[level]
    out = []
    for q in range(19):
        cx, cy, cz = VELOCITY[q]
        shift = cz * pitch + cy
        value = post[q, pl.ds(row - cx, 8), :]
        if shift != 0:
            value = pltpu.roll(value, shift % LANES, 1)
            if cz == 1:
                value = jnp.where(lane < pitch, post[OPPOSITE[q], pl.ds(row, 8), :], value)
        out.append(value)
    return out


def zone_masks(level, reach):
    lane = lanes()
    pitch, first = ZONE_PITCH[level], 6 if level == 1 else 4
    top = DEPTH[level] // 4 - 1
    inside = None
    rim = None
    for z in range(top + reach + 1):
        start = z * pitch - first
        row = (lane >= start + Y_LOW - reach) & (lane <= start + Y_HIGH + reach)
        inside = row if inside is None else inside | row
        if z < top:
            row = (lane == start + Y_LOW) | (lane == start + Y_HIGH)
        elif z == top:
            row = (lane >= start + Y_LOW) & (lane <= start + Y_HIGH)
        else:
            continue
        rim = row if rim is None else rim | row
    return inside, rim


def loop(count, body):
    def step(i, carry):
        body(i)
        return carry

    lax.fori_loop(0, count, step, 0)


def row_loop(start, count, body):
    loop(count, lambda i: body(pl.multiple_of(start + 8 * i, 8)))


def moved(value, matrix):
    high = value.astype(BF16)
    rest = value - high.astype(F32)
    mid = rest.astype(BF16)
    low = (rest - mid.astype(F32)).astype(BF16)

    def product(part):
        return jnp.dot(part, matrix, preferred_element_type=F32)

    return product(high) + (product(mid) + product(low))


def load_level(level, own, solid, low, high, buf):
    factor, count, row0 = FACTOR[level], CHUNKS[level], ROW0[level]
    n = OWN[level]

    def one(q, source):
        for j in range(8):
            buf[q, j % count, pl.ds(row0 + j // count, 8, stride=factor), :] = source(j)
        if low is not None:
            for c in range(count):
                rows = pl.ds(c, 2 * factor, stride=count) if count > 1 else pl.ds(0, 2 * factor)
                buf[q, c, pl.ds(row0 - 2 * factor, 2 * factor), :] = low[q, rows, :]
                buf[q, c, pl.ds(row0 + n, 2 * factor), :] = high[q, rows, :]

    loop(19, lambda q: one(q, lambda j: own[q, :, pl.ds(j * LANES, LANES)]))
    one(19, lambda j: solid[:, pl.ds(j * LANES, LANES)].astype(F32))


def store_level(level, buf, row0, out):
    factor, count = FACTOR[level], CHUNKS[level]

    def one(q):
        for j in range(8):
            out[q, :, pl.ds(j * LANES, LANES)] = buf[
                q, j % count, pl.ds(row0 + j // count, 8, stride=factor), :
            ]

    loop(19, one)


def collide_rows(level, source, solid, wide, dest, start, groups):
    masks = [interface_mask(level, c) for c in range(CHUNKS[level])]

    def body(row):
        for c in range(CHUNKS[level]):
            v = [source[q, c, pl.ds(row, 8), :] for q in range(19)]
            if wide is not None:
                v = [jnp.where(masks[c], wide[q, c, pl.ds(row, 8), :], v[q]) for q in range(19)]
            post = collided(v, solid[19, c, pl.ds(row, 8), :], level)
            for q in range(19):
                dest[q, c, pl.ds(row, 8), :] = post[q]

    row_loop(start, groups, body)


def pull_rows(level, post, dest, start, groups):
    def body(row):
        for c in range(CHUNKS[level]):
            v = pulled(post, level, row, c)
            for q in range(19):
                dest[q, c, pl.ds(row, 8), :] = v[q]

    row_loop(start, groups, body)


def load_zone(level, zone, zero_row, center, left, right):
    n = OWN[level]
    zone[...] = jnp.zeros(zone.shape, F32)
    for q in range(20):
        zone[q, pl.ds(zero_row - 1, n + 2), :] = center[pl.ds(q * 34, n + 2), :]
        zone[q, pl.ds(zero_row - 7, 8), :] += left[q]
        zone[q, pl.ds(zero_row + n - 1, 8), :] += right[q]


def convert_zone(level, zone, start, groups, rim, out):
    scale = parent_scale(level + 1)

    def body(i):
        row = pl.multiple_of(8 * i, 8)
        v = [zone[q, pl.ds(start + row, 8), :] for q in range(19)]
        v = relax(v, 1.0 - scale, scale)
        for q in range(19):
            out[q, pl.ds(row, 8), :] = v[q] if rim is None else jnp.where(rim, v[q], 0.0)

    loop(groups, body)


def widen(converted, matrix, child, skip, count, wide, spread, first):
    rows = converted.shape[1]
    value = moved(converted[...].reshape(19 * rows, LANES), matrix[...])
    for c in range(CHUNKS[child]):
        part = value[:, c * LANES : (c + 1) * LANES].reshape(19, rows, LANES)
        spread[...] = part
        for q in range(19):
            t = spread[q, pl.ds(skip, count), :]
            wide[q, c, pl.ds(first, count, stride=2), :] = t
            wide[q, c, pl.ds(first + 1, count, stride=2), :] = t


def start_kernel(own, solid, pack0, pack1, pack2, to_right, to_left, center, to_zone_right, to_zone_left):
    me = lax.axis_index("level")

    def halo(q, source):
        for j in range(8):
            to_left[q, pl.ds(j, 2, stride=8), :] = source(pl.ds(0, 2), j)
            to_right[q, pl.ds(j, 2, stride=8), :] = source(pl.ds(SLAB - 2, 2), j)

    loop(19, lambda q: halo(q, lambda rows, j: own[q, rows, pl.ds(j * LANES, LANES)]))
    halo(19, lambda rows, j: solid[rows, pl.ds(j * LANES, LANES)].astype(F32))

    for level, pack in enumerate((pack0, pack1, pack2)):

        def push(level=level, pack=pack):
            n, row0, count, rows = OWN[level], ROW0[level], CHUNKS[level], ROWS[level]

            def scoped(buf, post, packed):
                post[...] = jnp.zeros(post.shape, F32)
                buf[19] = jnp.zeros(buf.shape[1:], F32)
                load_level(level, own, solid, None, None, buf)
                collide_rows(level, buf, buf, None, post, row0, n // 8)
                pull_rows(level, post, buf, row0 - 8, n // 8 + 2)
                total = None
                for c in range(count):
                    part = buf[:, c, pl.ds(row0 - 8, n + 16), :].reshape(20 * (n + 16), LANES)
                    part = moved(part, pack[pl.ds(c * LANES, LANES), :])
                    total = part if total is None else total + part
                packed[...] = total.reshape(20, n + 16, LANES)
                for q in range(20):
                    center[pl.ds(q * 34, n + 2), :] = packed[q, pl.ds(7, n + 2), :]
                    to_zone_right[q] = packed[q, pl.ds(n + 1, 8), :]
                    to_zone_left[q] = packed[q, pl.ds(7, 8), :]

            pl.run_scoped(
                scoped,
                pltpu.VMEM((20, count, rows, LANES), F32),
                pltpu.VMEM((19, count, rows, LANES), F32),
                pltpu.VMEM((20, n + 16, LANES), F32),
            )

        pl.when(me == level)(push)


def pack_flows(post, start, out, first):
    lane = lanes()

    def body(i):
        row = pl.multiple_of(8 * i, 8)
        total = jnp.zeros((8, LANES), F32)
        for k, q in enumerate(Z_OUT):
            v = pltpu.roll(post[q, pl.ds(start + row, 8), :], (16 * k - zone_lane(2, 8, 1)) % LANES, 1)
            total = jnp.where((lane >= 16 * k) & (lane < 16 * k + 16), v, total)
        for group, y, base in ((Y_DOWN, 8, 80), (Y_UP, 23, 85)):
            for k, q in enumerate(group):
                lane0 = base + k
                v = pltpu.roll(post[q, pl.ds(start + row, 8), :], (lane0 - zone_lane(2, y, 0)) % LANES, 1)
                total = jnp.where((lane == lane0) | (lane == lane0 + 25), v, total)
        out[pl.ds(first + row, 8), :] = total

    loop(6, body)


def finest_role(own, solid, low, high, center, left, right, widen3, restrict3, compact, state, message):
    level, row0, n = 3, ROW0[3], OWN[3]

    def scoped(g, pa, pb, wide, zone, zpost, flat, spread):
        load_level(level, own, solid, low, high, g)
        load_zone(2, zone, 16, center, left, right)
        covered, rim = zone_masks(2, 0)
        mask = interface_mask(level, 0)

        def substep(v, row, dest):
            v = [jnp.where(mask, wide[q, 0, pl.ds(row, 8), :], v[q]) for q in range(19)]
            post = collided(v, g[19, 0, pl.ds(row, 8), :], level)
            for q in range(19):
                dest[q, 0, pl.ds(row, 8), :] = post[q]

        for cycle in range(4):
            if cycle > 0:

                def zone_collide(row):
                    v = [zone[q, pl.ds(row, 8), :] for q in range(19)]
                    post = collided(v, zone[19, pl.ds(row, 8), :], 2)
                    for q in range(19):
                        zpost[q, pl.ds(row, 8), :] = post[q]

                def zone_pull(row):
                    v = zone_pulled(zpost, 2, row)
                    for q in range(19):
                        zone[q, pl.ds(row, 8), :] = v[q]

                row_loop(8, 6, zone_collide)
                pack_flows(zpost, 8, message, 48 * (cycle - 1))
                row_loop(8, 6, zone_pull)
            convert_zone(2, zone, 8, 6, rim, flat)
            widen(flat, widen3, 3, 0, 48, wide, spread, PAD)
            first, groups = (PAD, 12) if cycle < 2 else (PAD + 8, 10)

            def step_one(row):
                substep([g[q, 0, pl.ds(row, 8), :] for q in range(19)], row, pa)

            def step_two(row):
                substep(pulled(pa, level, row, 0), row, pb)

            def step_out(row):
                v = pulled(pb, level, row, 0)
                for q in range(19):
                    g[q, 0, pl.ds(row, 8), :] = v[q]

            row_loop(first, groups, step_one)
            row_loop(first, groups, step_two)
            if cycle < 3:
                row_loop(first, groups, step_out)
                for q in range(19):
                    flat[q] = (
                        g[q, 0, pl.ds(PAD, 48, stride=2), :] + g[q, 0, pl.ds(PAD + 1, 48, stride=2), :]
                    )
                spread[...] = moved(flat[...].reshape(19 * 48, LANES), restrict3[...]).reshape(19, 48, LANES)
                scale = child_scale(3)

                def restrict(i):
                    row = pl.multiple_of(8 * i, 8)
                    v = relax([spread[q, pl.ds(row, 8), :] for q in range(19)], 1.0 - scale, scale)
                    for q in range(19):
                        old = zone[q, pl.ds(8 + row, 8), :]
                        zone[q, pl.ds(8 + row, 8), :] = jnp.where(covered, v[q], old)

                loop(6, restrict)
            else:
                row_loop(row0, n // 8, step_out)
                store_level(level, g, row0, state)
                for q in range(19):
                    flat[q, pl.ds(0, 32), :] = (
                        g[q, 0, pl.ds(row0, 32, stride=2), :] + g[q, 0, pl.ds(row0 + 1, 32, stride=2), :]
                    )
                flat[:, pl.ds(32, 8), :] = jnp.zeros((19, 8, LANES), F32)
                total = None
                for i in range(4):
                    part = jnp.concatenate(
                        [flat[q, pl.ds(8 * i, 8), :] for q in range(19)] + [jnp.zeros((8, LANES), F32)], axis=0
                    )
                    part = moved(part, compact[i])
                    total = part if total is None else total + part
                scale = child_scale(3)
                v = relax([total[8 * q : 8 * q + 8] for q in range(19)], 1.0 - scale, scale)
                for q in range(19):
                    message[pl.ds(144 + 8 * q, 8), :] = v[q]
                message[pl.ds(296, 8), :] = jnp.zeros((8, LANES), F32)

    rows = ROWS[3]
    pl.run_scoped(
        scoped,
        pltpu.VMEM((20, 1, rows, LANES), F32),
        pltpu.VMEM((19, 1, rows, LANES), F32),
        pltpu.VMEM((19, 1, rows, LANES), F32),
        pltpu.VMEM((19, 1, rows, LANES), F32),
        pltpu.VMEM((20, 64, LANES), F32),
        pltpu.VMEM((19, 64, LANES), F32),
        pltpu.VMEM((19, 48, LANES), F32),
        pltpu.VMEM((19, 48, LANES), F32),
    )


def restrict_pairs(level, g, first, count, skip, flat, matrix):
    flat[...] = jnp.zeros(flat.shape, F32)
    for q in range(19):
        for c in range(CHUNKS[level]):
            flat[q, c, pl.ds(skip, count), :] = (
                g[q, c, pl.ds(first, count, stride=2), :] + g[q, c, pl.ds(first + 1, count, stride=2), :]
            )
    rows = flat.shape[2]
    total = None
    for c in range(CHUNKS[level]):
        part = moved(flat[:, c].reshape(flat.shape[0] * rows, LANES), matrix[pl.ds(c * LANES, LANES), :])
        total = part if total is None else total + part
    return total.reshape(flat.shape[0], rows, LANES)


def second_role(own, solid, low, high, center, left, right, widen2, restrict2, keep_post, keep_wide, keep_zone):
    level, row0 = 2, ROW0[2]
    first = row0 - 8

    def scoped(g, wide, zone, zpost, conv, spread, flat):
        load_level(level, own, solid, low, high, g)
        load_zone(1, zone, 16, center, left, right)
        covered, rim = zone_masks(1, 0)
        keep_post[19] = g[19]
        convert_zone(1, zone, 8, 4, rim, conv)
        widen(conv, widen2, 2, 4, 24, wide, spread, first)
        collide_rows(level, g, g, wide, keep_post, first, 6)
        pull_rows(level, keep_post, g, first, 6)
        collide_rows(level, g, g, wide, keep_post, first, 6)
        pull_rows(level, keep_post, g, first, 6)
        spread[...] = restrict_pairs(level, g, first, 24, 4, flat, restrict2)
        scale = child_scale(2)

        def restrict(i):
            row = pl.multiple_of(8 * i, 8)
            v = relax([spread[q, pl.ds(row, 8), :] for q in range(19)], 1.0 - scale, scale)
            v = [jnp.where(covered, v[q], zone[q, pl.ds(8 + row, 8), :]) for q in range(19)]
            post = collided(v, zone[19, pl.ds(8 + row, 8), :], 1)
            for q in range(19):
                zpost[q, pl.ds(8 + row, 8), :] = post[q]

        loop(4, restrict)

        def zone_pull(row):
            v = zone_pulled(zpost, 1, row)
            for q in range(19):
                zone[q, pl.ds(row, 8), :] = v[q]

        row_loop(8, 4, zone_pull)
        convert_zone(1, zone, 8, 4, rim, conv)
        widen(conv, widen2, 2, 4, 24, keep_wide, spread, first)
        for q in range(19):
            keep_zone[q] = zone[q, pl.ds(16, 16), :]

    pl.run_scoped(
        scoped,
        pltpu.VMEM((20, 2, ROWS[2], LANES), F32),
        pltpu.VMEM((19, 2, ROWS[2], LANES), F32),
        pltpu.VMEM((20, 48, LANES), F32),
        pltpu.VMEM((19, 48, LANES), F32),
        pltpu.VMEM((19, 32, LANES), F32),
        pltpu.VMEM((19, 32, LANES), F32),
        pltpu.VMEM((19, 2, 32, LANES), F32),
    )


def first_role(own, solid, low, high, center, left, right, widen1, mean1, state, partial):
    level, row0, n = 1, ROW0[1], OWN[1]
    first = row0 - 8

    def scoped(g, post, wide, zone, conv, spread, flat):
        load_level(level, own, solid, low, high, g)
        load_zone(0, zone, 12, center, left, right)
        convert_zone(0, zone, 8, 2, None, conv)
        widen(conv, widen1, 1, 0, 16, wide, spread, first)
        collide_rows(level, g, g, wide, post, first, 4)
        pull_rows(level, post, g, first, 4)
        collide_rows(level, g, g, wide, post, first, 4)
        pull_rows(level, post, g, row0, n // 8)
        store_level(level, g, row0, state)
        total = None
        for c in range(CHUNKS[1]):
            part = moved(g[pl.ds(0, 19), c, pl.ds(row0, n), :].reshape(19 * n, LANES), mean1[pl.ds(c * LANES, LANES), :])
            total = part if total is None else total + part
        flat[...] = total.reshape(19, n, LANES)
        for q in range(19):
            partial[q] = flat[q, pl.ds(0, 8, stride=2), :] + flat[q, pl.ds(1, 8, stride=2), :]

    pl.run_scoped(
        scoped,
        pltpu.VMEM((20, 4, ROWS[1], LANES), F32),
        pltpu.VMEM((19, 4, ROWS[1], LANES), F32),
        pltpu.VMEM((19, 4, ROWS[1], LANES), F32),
        pltpu.VMEM((20, 32, LANES), F32),
        pltpu.VMEM((19, 16, LANES), F32),
        pltpu.VMEM((19, 16, LANES), F32),
        pltpu.VMEM((19, n, LANES), F32),
    )


def coarse_role(own, solid, low, high, state):
    level, row0 = 0, ROW0[0]

    def scoped(g, post):
        load_level(level, own, solid, low, high, g)
        collide_rows(level, g, g, None, post, row0 - 8, 3)
        pull_rows(level, post, g, row0, 1)
        store_level(level, g, row0, state)

    pl.run_scoped(
        scoped,
        pltpu.VMEM((20, 8, ROWS[0], LANES), F32),
        pltpu.VMEM((19, 8, ROWS[0], LANES), F32),
    )


def main_kernel(
    own, solid, low, high, center, left, right, widen1, widen2, widen3, restrict2, restrict3, compact, mean1,
    state, message, keep_post, keep_wide, keep_zone, partial,
):
    me = lax.axis_index("level")

    @pl.when(me == 3)
    def _():
        finest_role(own, solid, low, high, center, left, right, widen3, restrict3, compact, state, message)

    @pl.when(me == 2)
    def _():
        second_role(own, solid, low, high, center, left, right, widen2, restrict2, keep_post, keep_wide, keep_zone)

    @pl.when(me == 1)
    def _():
        first_role(own, solid, low, high, center, left, right, widen1, mean1, state, partial)

    @pl.when(me == 0)
    def _():
        coarse_role(own, solid, low, high, state)


def return_kernel(
    message, old_state, keep_post, keep_wide, keep_zone, partial, flows, spread2, restrict2, mean_zone,
    state, to_first, to_coarse,
):
    me = lax.axis_index("level")
    level, row0 = 2, ROW0[2]
    first = row0 - 8

    @pl.when(me == 2)
    def _():
        def scoped(g, post, override, back, flat, means, zone):
            total = moved(message[pl.ds(0, 144), :], flows[...])
            for k in range(len(FLOW_DIRECTIONS)):
                for c in range(2):
                    start = (2 * k + c) * LANES
                    override[k, c] = total[:, start : start + LANES]

            def overridden(c, row, cycle, v):
                lane = lanes() + c * LANES
                y, z = lane >> 3, lane & 7
                v = list(v)
                for k, q in enumerate(FLOW_DIRECTIONS):
                    mask = None
                    if q in Z_OUT:
                        mask = (z == 1) & (y >= Y_LOW) & (y <= Y_HIGH)
                    if q in Y_DOWN:
                        edge = (y == Y_LOW) & (z <= 1)
                        mask = edge if mask is None else mask | edge
                    if q in Y_UP:
                        edge = (y == Y_HIGH) & (z <= 1)
                        mask = edge if mask is None else mask | edge
                    v[q] = jnp.where(mask, override[k, c, pl.ds(48 * cycle + row - first, 8), :], v[q])
                return v

            masks = [interface_mask(level, c) for c in range(2)]

            def begin(row):
                for c in range(2):
                    v = overridden(c, row, 0, [keep_post[q, c, pl.ds(row, 8), :] for q in range(19)])
                    for q in range(19):
                        post[q, c, pl.ds(row, 8), :] = v[q]

            row_loop(first, 6, begin)
            for cycle in (1, 2):
                pull_rows(level, post, g, first, 6)

                def body(row, cycle=cycle):
                    for c in range(2):
                        v = [
                            jnp.where(masks[c], keep_wide[q, c, pl.ds(row, 8), :], g[q, c, pl.ds(row, 8), :])
                            for q in range(19)
                        ]
                        v = collided(v, keep_post[19, c, pl.ds(row, 8), :], level)
                        v = overridden(c, row, cycle, v)
                        for q in range(19):
                            post[q, c, pl.ds(row, 8), :] = v[q]

                row_loop(first, 6, body)
            pull_rows(level, post, g, row0, 4)
            total = moved(message[pl.ds(144, 160), :], spread2[...])
            for i in range(4):
                for c in range(2):
                    start = (2 * i + c) * LANES
                    back[i, c] = total[:, start : start + LANES].reshape(20, 8, LANES)
            for c in range(2):
                lane = lanes() + c * LANES
                y, z = lane >> 3, lane & 7
                covered = (y >= Y_LOW) & (y <= Y_HIGH) & (z <= 1)
                for i in range(4):
                    for q in range(19):
                        rows = pl.ds(row0 + 8 * i, 8)
                        g[q, c, rows, :] = jnp.where(covered, back[i, c, q], g[q, c, rows, :])
            store_level(level, g, row0, state)
            means[...] = restrict_pairs(level, g, row0, 16, 0, flat, restrict2)
            scale = child_scale(2)
            covered, _ = zone_masks(1, 0)
            near, _ = zone_masks(1, 1)
            for i in range(2):
                rows = pl.ds(8 * i, 8)
                v = relax([means[q, rows, :] for q in range(19)], 1.0 - scale, scale)
                for q in range(19):
                    value = jnp.where(covered, v[q], keep_zone[q, rows, :])
                    to_first[q, rows, :] = jnp.where(near, value, 0.0)
            zone[...] = moved(to_first[...].reshape(19 * 16, LANES), mean_zone[...]).reshape(19, 16, LANES)
            for q in range(19):
                to_coarse[q] = zone[q, pl.ds(0, 8, stride=2), :] + zone[q, pl.ds(1, 8, stride=2), :]

        pl.run_scoped(
            scoped,
            pltpu.VMEM((19, 2, ROWS[2], LANES), F32),
            pltpu.VMEM((19, 2, ROWS[2], LANES), F32),
            pltpu.VMEM((len(FLOW_DIRECTIONS), 2, 144, LANES), F32),
            pltpu.VMEM((4, 2, 20, 8, LANES), F32),
            pltpu.VMEM((19, 2, 16, LANES), F32),
            pltpu.VMEM((19, 16, LANES), F32),
            pltpu.VMEM((19, 16, LANES), F32),
        )

    @pl.when(me != 2)
    def _():
        state[...] = old_state[...]

    @pl.when(me == 1)
    def _():
        to_first[:, pl.ds(0, 8), :] = partial[...]


def finish_kernel(old_state, from_near, from_far, spread1, spread0, state):
    me = lax.axis_index("level")

    @pl.when(me >= 2)
    def _():
        state[...] = old_state[...]

    @pl.when(me == 1)
    def _():
        def scoped(wide):
            total = moved(from_near[...].reshape(19 * 16, LANES), spread1[...])
            for c in range(4):
                wide[:, c] = total[:, c * LANES : (c + 1) * LANES].reshape(19, 16, LANES)

            def one(q):
                for j in range(8):
                    c = j % 4
                    lane = lanes() + c * LANES
                    y, z = lane >> 4, lane & 15
                    near = (y >= Y_LOW - 1) & (y <= Y_HIGH + 1) & (z <= 4)
                    columns = pl.ds(j * LANES, LANES)
                    value = wide[q, c, pl.ds(j // 4, 8, stride=2), :]
                    state[q, :, columns] = jnp.where(near, value, old_state[q, :, columns])

            loop(19, one)

        pl.run_scoped(scoped, pltpu.VMEM((19, 4, 16, LANES), F32))

    @pl.when(me == 0)
    def _():
        def scoped(value):
            scale = child_scale(1)
            v = relax(
                [from_near[q, pl.ds(0, 8), :] + from_far[q] for q in range(19)], 1.0 - scale, scale
            )
            for q in range(19):
                value[q] = v[q]
            value[19] = jnp.zeros((8, LANES), F32)
            total = moved(value[...].reshape(160, LANES), spread0[...])
            for q in range(19):
                for j in range(8):
                    columns = pl.ds(j * LANES, LANES)
                    if j in (0, 1, 6, 7):
                        state[q, :, columns] = old_state[q, :, columns]
                    else:
                        covered = (lanes() & 31) < 8
                        part = total[8 * q : 8 * q + 8, j * LANES : (j + 1) * LANES]
                        state[q, :, columns] = jnp.where(covered, part, old_state[q, :, columns])

        pl.run_scoped(scoped, pltpu.VMEM((20, 8, LANES), F32))


def call(kernel, shapes, args):
    return pl.pallas_call(
        kernel,
        out_shape=[jax.ShapeDtypeStruct(s, F32) for s in shapes],
        in_specs=[pl.BlockSpec(memory_space=pltpu.VMEM)] * len(args),
        out_specs=[pl.BlockSpec(memory_space=pltpu.VMEM)] * len(shapes),
        compiler_params=pltpu.CompilerParams(vmem_limit_bytes=48 * 1024 * 1024),
    )(*args)


def weights(matrix):
    return jnp.asarray(matrix, BF16)


def shards(populations, solid):
    own, flags = populations[0], solid[0]
    if own.shape != (19, SLAB, NY * NZ):
        raise ValueError("unexpected slab")
    blocks = lax.axis_size("blocks")
    forward = [(i, (i + 1) % blocks) for i in range(blocks)]
    backward = [(i, (i - 1) % blocks) for i in range(blocks)]
    down = [(i, i + 1) for i in range(LEVELS - 1)]

    def diagonal(step):
        return [
            (level * blocks + b, (level + 1) * blocks + (b + step) % blocks)
            for level in range(LEVELS - 1)
            for b in range(blocks)
        ]

    both = ("level", "blocks")
    to_right, to_left, center, zone_right, zone_left = call(
        start_kernel,
        [(20, 16, LANES), (20, 16, LANES), (680, LANES), (20, 8, LANES), (20, 8, LANES)],
        [own, flags] + [weights(pack_matrix(level)) for level in range(3)],
    )
    center = lax.ppermute(center, "level", down)
    left = lax.ppermute(zone_right, both, diagonal(1))
    right = lax.ppermute(zone_left, both, diagonal(-1))
    low = lax.ppermute(to_right, "blocks", forward)
    high = lax.ppermute(to_left, "blocks", backward)

    mean1 = one_hot(
        [
            (level_lane(1, y, z), zone_lane(0, 8 + y // 2, z // 2))
            for y in range(NY)
            for z in range(16)
            if not (7 <= y <= 24 and z <= 4)
        ],
        4 * LANES,
        LANES,
        0.125,
    )
    mean_zone = one_hot(
        [
            (zone_lane(1, y, z), zone_lane(0, 8 + y // 2, z // 2))
            for y in range(7, 25)
            for z in range(5)
        ],
        LANES,
        LANES,
        0.125,
    )
    spread0 = one_hot(
        [(zone_lane(0, y, z), level_lane(0, y, z)) for y, z in ZONE_CELLS[0]], LANES, 8 * LANES
    )
    restrict2 = weights(restrict_matrix(2))
    state, message, keep_post, keep_wide, keep_zone, partial = call(
        main_kernel,
        [
            (19, SLAB, NY * NZ),
            (304, LANES),
            (20, 2, ROWS[2], LANES),
            (19, 2, ROWS[2], LANES),
            (19, 16, LANES),
            (19, 8, LANES),
        ],
        [own, flags, low, high, center, left, right]
        + [weights(interface_matrix(child)) for child in (1, 2, 3)]
        + [restrict2, weights(restrict_matrix(3)), weights(compact_matrix()), weights(mean1)],
    )
    message = lax.ppermute(message, "level", [(3, 2)])
    state, to_first, to_coarse = call(
        return_kernel,
        [(19, SLAB, NY * NZ), (19, 16, LANES), (19, 8, LANES)],
        [message, state, keep_post, keep_wide, keep_zone, partial]
        + [weights(flow_matrix()), weights(spread_matrix()), restrict2, weights(mean_zone)],
    )
    near = lax.ppermute(to_first, "level", [(2, 1), (1, 0)])
    far = lax.ppermute(to_coarse, "level", [(2, 0)])
    (state,) = call(
        finish_kernel,
        [(19, SLAB, NY * NZ)],
        [state, near, far, weights(spread_zone_matrix()), weights(spread0)],
    )
    return state[None]


def solution(mesh):
    in_specs = (P("level", None, "blocks", None), P("level", "blocks", None))
    out_specs = P("level", None, "blocks", None)
    return jax.shard_map(shards, mesh=mesh, in_specs=in_specs, out_specs=out_specs, check_vma=False)
```

```python
import jax
import jax.numpy as jnp
from jax import lax
from jax.experimental import pallas as pl
from jax.experimental.pallas import tpu as pltpu
from jax.sharding import PartitionSpec as P

NY = 32
NZ = 32
LEVELS = 4
SLAB = 8
LANES = 128
VELOCITY = (
    (0, 0, 0),
    (1, 0, 0),
    (-1, 0, 0),
    (0, 1, 0),
    (0, -1, 0),
    (0, 0, 1),
    (0, 0, -1),
    (1, 1, 0),
    (-1, -1, 0),
    (1, -1, 0),
    (-1, 1, 0),
    (1, 0, 1),
    (-1, 0, -1),
    (1, 0, -1),
    (-1, 0, 1),
    (0, 1, 1),
    (0, -1, -1),
    (0, 1, -1),
    (0, -1, 1),
)
OPPOSITE = (0, 2, 1, 4, 3, 6, 5, 8, 7, 10, 9, 12, 11, 14, 13, 16, 15, 18, 17)
TAU_BASE = 1.0
F32 = jnp.float32
BF16 = jnp.bfloat16

PAD = 8
MARGIN = (8, 8, 8, 16)
FACTOR = (1, 2, 4, 8)
CHUNKS = (8, 4, 2, 1)
DEPTH = (32, 16, 8, 4)
OWN = tuple(SLAB * f for f in FACTOR)
ROW0 = tuple(PAD + m for m in MARGIN)
ROWS = tuple(OWN[l] + 2 * ROW0[l] for l in range(LEVELS))

Y_LOW = NY // 4
Y_HIGH = 3 * NY // 4 - 1


def zone_lane(level, y, z):
    if level == 0:
        return (y - 8) * 8 + z
    if level == 1:
        return z * 20 + y - 6
    return z * 25 + y - 4


ZONE_CELLS = (
    [(y, z) for y in range(8, 24) for z in range(8)],
    [(y, z) for y in range(6, 26) for z in range(6)],
    [(y, z) for y in range(5, 27) for z in range(5)],
)
ZONE_PITCH = (None, 20, 25)


def level_lane(level, y, z):
    return y * DEPTH[level] + z


def made(columns, weight, holds):
    row = lax.broadcasted_iota(jnp.int32, (LANES, columns), 0)
    column = lax.broadcasted_iota(jnp.int32, (LANES, columns), 1)
    matrix = jnp.where(holds(row, column), weight, 0.0).astype(BF16)
    return jnp.concatenate([matrix, matrix], axis=0)


def cell_of(level, lane):
    return lane >> (DEPTH[level].bit_length() - 1), lane & (DEPTH[level] - 1)


def pack_chunk(level, c):
    ys, zs = zip(*ZONE_CELLS[level])

    def holds(row, column):
        y, z = cell_of(level, row + c * LANES)
        inside = (y >= min(ys)) & (y <= max(ys)) & (z <= max(zs))
        return inside & (column == zone_lane(level, y, z))

    return made(LANES, 1.0, holds)


def widen_matrix(child):
    def holds(row, column):
        y, z = cell_of(child, column)
        edge = (y == 0) | (y == NY - 1) | (z == DEPTH[child] - 1)
        return edge & (row == zone_lane(child - 1, 8 + (y >> 1), z >> 1))

    return made(CHUNKS[child] * LANES, 1.0, holds)


def restrict_chunk(child, c):
    def holds(row, column):
        y, z = cell_of(child, row + c * LANES)
        return column == zone_lane(child - 1, 8 + (y >> 1), z >> 1)

    return made(LANES, 0.125, holds)


def compact_chunk(i):
    def holds(row, column):
        y, z = cell_of(3, row)
        return column == 32 * i + (y >> 1) * 2 + (z >> 1)

    return made(LANES, 0.125, holds)


def spread_chunk(i):
    def holds(row, column):
        y, z = cell_of(2, column)
        return (y >= Y_LOW) & (y <= Y_HIGH) & (z <= 1) & (row == 32 * i + (y - Y_LOW) * 2 + z)

    return made(2 * LANES, 1.0, holds)


def near_first(y, z):
    return (y >= Y_LOW - 1) & (y <= Y_HIGH + 1) & (z <= 4)


def mean_chunk(c):
    def holds(row, column):
        y, z = cell_of(1, row + c * LANES)
        return jnp.logical_not(near_first(y, z)) & (column == zone_lane(0, 8 + (y >> 1), z >> 1))

    return made(LANES, 0.125, holds)


def mean_zone_matrix():
    def holds(row, column):
        z = sum((row >= 20 * k).astype(jnp.int32) for k in range(1, 6))
        y = row - 20 * z + 6
        return near_first(y, z) & (column == zone_lane(0, 8 + (y >> 1), z >> 1))

    return made(LANES, 0.125, holds)


def spread_zone_matrix():
    def holds(row, column):
        y, z = cell_of(1, column)
        return near_first(y, z) & (row == zone_lane(1, y, z))

    return made(4 * LANES, 1.0, holds)


def spread_covered_matrix():
    def holds(row, column):
        y, z = cell_of(0, column + 2 * LANES)
        return (z < 8) & (row == zone_lane(0, y, z))

    return made(4 * LANES, 1.0, holds)


Z_OUT = (5, 11, 14, 15, 18)
Y_DOWN = (4, 8, 9, 16, 18)
Y_UP = (3, 7, 10, 15, 17)
FLOW_DIRECTIONS = tuple(sorted(set(Z_OUT + Y_DOWN + Y_UP)))


def flow_mask(q, y, z):
    mask = None
    if q in Z_OUT:
        mask = (z == 1) & (y >= Y_LOW) & (y <= Y_HIGH)
    for group, edge in ((Y_DOWN, Y_LOW), (Y_UP, Y_HIGH)):
        if q in group:
            cells = (y == edge) & (z <= 1)
            mask = cells if mask is None else mask | cells
    return mask


def flow_chunk(q):
    def holds(row, column):
        y, z = cell_of(2, column)
        source = None
        if q in Y_DOWN:
            source = 80 + Y_DOWN.index(q) + 25 * z
        if q in Y_UP:
            source = 85 + Y_UP.index(q) + 25 * z
        if q in Z_OUT:
            over = 16 * Z_OUT.index(q) + y - Y_LOW
            source = over if source is None else jnp.where(z == 1, over, source)
        return flow_mask(q, y, z) & (row == source)

    return made(2 * LANES, 1.0, holds)


def relaxation(level_id):
    return 2.0**level_id * (TAU_BASE - 0.5) + 0.5


def parent_scale(child):
    return relaxation(child) / (2.0 * relaxation(child - 1))


def child_scale(child):
    return 2.0 * relaxation(child - 1) / relaxation(child)


def relax(v, a, b):
    s = [None] + [v[2 * k - 1] + v[2 * k] for k in range(1, 10)]
    d = [None] + [v[2 * k - 1] - v[2 * k] for k in range(1, 10)]
    rho = (
        (1.0 / 3.0) * v[0]
        + (1.0 / 18.0) * (s[1] + s[2] + s[3])
        + (1.0 / 36.0) * ((s[4] + s[5]) + (s[6] + s[7]) + (s[8] + s[9]))
    )
    mx = (1.0 / 18.0) * d[1] + (1.0 / 36.0) * ((d[4] + d[5]) + (d[6] + d[7]))
    my = (1.0 / 18.0) * d[2] + (1.0 / 36.0) * ((d[4] - d[5]) + (d[8] + d[9]))
    mz = (1.0 / 18.0) * d[3] + (1.0 / 36.0) * ((d[6] - d[7]) + (d[8] - d[9]))
    inv = 1.0 / rho
    ux, uy, uz = mx * inv, my * inv, mz * inv
    ra = a * rho
    base = ra - (1.5 * ra) * (ux * ux + uy * uy + uz * uz)
    r45 = 4.5 * ra
    ra3 = 3.0 * ra

    def kept(q):
        return v[q] if b == 1.0 else b * v[q]

    out = [base if b == 0.0 else base + kept(0)]
    cus = (ux, uy, uz, ux + uy, ux - uy, ux + uz, ux - uz, uy + uz, uy - uz)
    for k in range(1, 10):
        cu = cus[k - 1]
        even = base + r45 * (cu * cu)
        odd = ra3 * cu
        plus, minus = even + odd, even - odd
        if b != 0.0:
            plus, minus = plus + kept(2 * k - 1), minus + kept(2 * k)
        out += [plus, minus]
    return out


def collided(v, solid, level):
    inv_tau = 1.0 / relaxation(level)
    relaxed = relax(v, inv_tau, 1.0 - inv_tau)
    flag = solid != 0.0
    return [jnp.where(flag, v[OPPOSITE[q]], relaxed[q]) for q in range(19)]


def lanes():
    return lax.broadcasted_iota(jnp.int32, (8, LANES), 1)


def interface_mask(level, c):
    lane = lanes()
    nz = DEPTH[level]
    mask = (lane & (nz - 1)) == nz - 1
    if c == 0:
        mask = mask | (lane < nz)
    if c == CHUNKS[level] - 1:
        mask = mask | (lane >= LANES - nz)
    return mask


def pulled(post, level, row, c):
    lane = lanes()
    nz, count = DEPTH[level], CHUNKS[level]
    out = []
    for q in range(19):
        cx, cy, cz = VELOCITY[q]
        shift = cy * nz + cz
        value = post[q, c, pl.ds(row - cx, 8), :]
        if shift != 0:
            value = pltpu.roll(value, shift % LANES, 1)
            outside = None
            if cy == 1:
                if c > 0:
                    other = pltpu.roll(post[q, c - 1, pl.ds(row - cx, 8), :], shift, 1)
                    value = jnp.where(lane < shift, other, value)
                else:
                    outside = lane < nz
            if cy == -1:
                if c < count - 1:
                    other = pltpu.roll(post[q, c + 1, pl.ds(row - cx, 8), :], shift % LANES, 1)
                    value = jnp.where(lane >= LANES + shift, other, value)
                else:
                    outside = lane >= LANES - nz
            if cz != 0:
                edge = (lane & (nz - 1)) == (0 if cz == 1 else nz - 1)
                outside = edge if outside is None else outside | edge
            if outside is not None:
                value = jnp.where(outside, post[OPPOSITE[q], c, pl.ds(row, 8), :], value)
        out.append(value)
    return out


def zone_pulled(post, level, row):
    lane = lanes()
    pitch = ZONE_PITCH[level]
    out = []
    for q in range(19):
        cx, cy, cz = VELOCITY[q]
        shift = cz * pitch + cy
        value = post[q, pl.ds(row - cx, 8), :]
        if shift != 0:
            value = pltpu.roll(value, shift % LANES, 1)
            if cz == 1:
                value = jnp.where(lane < pitch, post[OPPOSITE[q], pl.ds(row, 8), :], value)
        out.append(value)
    return out


def zone_masks(level, reach):
    lane = lanes()
    pitch, first = ZONE_PITCH[level], 6 if level == 1 else 4
    top = DEPTH[level] // 4 - 1
    inside = None
    rim = None
    for z in range(top + reach + 1):
        start = z * pitch - first
        row = (lane >= start + Y_LOW - reach) & (lane <= start + Y_HIGH + reach)
        inside = row if inside is None else inside | row
        if z < top:
            row = (lane == start + Y_LOW) | (lane == start + Y_HIGH)
        elif z == top:
            row = (lane >= start + Y_LOW) & (lane <= start + Y_HIGH)
        else:
            continue
        rim = row if rim is None else rim | row
    return inside, rim


def loop(count, body, unroll=None):
    def step(i, carry):
        body(i)
        return carry

    if unroll is None:
        unroll = max(u for u in range(1, 7) if count % u == 0)
    lax.fori_loop(0, count, step, 0, unroll=unroll)


def row_loop(start, count, body):
    loop(count, lambda i: body(pl.multiple_of(start + 8 * i, 8)))


def moved(value, matrix):
    high = value.astype(BF16)
    low = (value - high.astype(F32)).astype(BF16)
    return jnp.dot(jnp.concatenate([high, low], axis=1), matrix, preferred_element_type=F32)


def load_level(level, own, solid, low, high, buf):
    factor, count, row0 = FACTOR[level], CHUNKS[level], ROW0[level]
    n = OWN[level]

    def one(q, source):
        for j in range(8):
            buf[q, j % count, pl.ds(row0 + j // count, 8, stride=factor), :] = source(j)
        if low is not None:
            for c in range(count):
                rows = pl.ds(c, 2 * factor, stride=count) if count > 1 else pl.ds(0, 2 * factor)
                buf[q, c, pl.ds(row0 - 2 * factor, 2 * factor), :] = low[q, rows, :]
                buf[q, c, pl.ds(row0 + n, 2 * factor), :] = high[q, rows, :]

    loop(19, lambda q: one(q, lambda j: own[q, :, pl.ds(j * LANES, LANES)]))
    one(19, lambda j: solid[:, pl.ds(j * LANES, LANES)].astype(F32))


def store_level(level, buf, row0, out):
    factor, count = FACTOR[level], CHUNKS[level]

    def one(q):
        for j in range(8):
            out[q, :, pl.ds(j * LANES, LANES)] = buf[
                q, j % count, pl.ds(row0 + j // count, 8, stride=factor), :
            ]

    loop(19, one)


def collide_rows(level, source, solid, wide, dest, start, groups):
    masks = [interface_mask(level, c) for c in range(CHUNKS[level])]

    def body(row):
        for c in range(CHUNKS[level]):
            v = [source[q, c, pl.ds(row, 8), :] for q in range(19)]
            if wide is not None:
                v = [jnp.where(masks[c], wide[q, c, pl.ds(row, 8), :], v[q]) for q in range(19)]
            post = collided(v, solid[19, c, pl.ds(row, 8), :], level)
            for q in range(19):
                dest[q, c, pl.ds(row, 8), :] = post[q]

    row_loop(start, groups, body)


def pull_rows(level, post, dest, start, groups):
    def body(row):
        for c in range(CHUNKS[level]):
            v = pulled(post, level, row, c)
            for q in range(19):
                dest[q, c, pl.ds(row, 8), :] = v[q]

    row_loop(start, groups, body)


def load_zone(level, zone, zero_row, center, left, right):
    n = OWN[level]
    zone[...] = jnp.zeros(zone.shape, F32)
    for q in range(20):
        zone[q, pl.ds(zero_row - 1, n + 2), :] = center[pl.ds(q * 34, n + 2), :]
        zone[q, pl.ds(zero_row - 7, 8), :] += left[q]
        zone[q, pl.ds(zero_row + n - 1, 8), :] += right[q]


def convert_zone(level, zone, start, groups, rim, out):
    scale = parent_scale(level + 1)

    def body(i):
        row = pl.multiple_of(8 * i, 8)
        v = [zone[q, pl.ds(start + row, 8), :] for q in range(19)]
        v = relax(v, 1.0 - scale, scale)
        for q in range(19):
            out[q, pl.ds(row, 8), :] = v[q] if rim is None else jnp.where(rim, v[q], 0.0)

    loop(groups, body)


def widen(converted, matrix, child, skip, count, wide, spread, first):
    rows = converted.shape[1]
    value = moved(converted[...].reshape(19 * rows, LANES), matrix)
    for c in range(CHUNKS[child]):
        part = value[:, c * LANES : (c + 1) * LANES].reshape(19, rows, LANES)
        spread[...] = part
        for q in range(19):
            t = spread[q, pl.ds(skip, count), :]
            wide[q, c, pl.ds(first, count, stride=2), :] = t
            wide[q, c, pl.ds(first + 1, count, stride=2), :] = t


def start_kernel(own, solid, to_right, to_left, center, to_zone_right, to_zone_left):
    me = lax.axis_index("level")

    def halo(q, source):
        for j in range(8):
            to_left[q, pl.ds(j, 2, stride=8), :] = source(pl.ds(0, 2), j)
            to_right[q, pl.ds(j, 2, stride=8), :] = source(pl.ds(SLAB - 2, 2), j)

    loop(19, lambda q: halo(q, lambda rows, j: own[q, rows, pl.ds(j * LANES, LANES)]))
    halo(19, lambda rows, j: solid[rows, pl.ds(j * LANES, LANES)].astype(F32))

    for level in range(3):

        def push(level=level):
            n, row0, count, rows = OWN[level], ROW0[level], CHUNKS[level], ROWS[level]

            def scoped(buf, post, packed):
                post[...] = jnp.zeros(post.shape, F32)
                buf[19] = jnp.zeros(buf.shape[1:], F32)
                load_level(level, own, solid, None, None, buf)
                collide_rows(level, buf, buf, None, post, row0, n // 8)
                pull_rows(level, post, buf, row0 - 8, n // 8 + 2)
                total = None
                for c in range(count):
                    part = buf[:, c, pl.ds(row0 - 8, n + 16), :].reshape(20 * (n + 16), LANES)
                    part = moved(part, pack_chunk(level, c))
                    total = part if total is None else total + part
                packed[...] = total.reshape(20, n + 16, LANES)
                for q in range(20):
                    center[pl.ds(q * 34, n + 2), :] = packed[q, pl.ds(7, n + 2), :]
                    to_zone_right[q] = packed[q, pl.ds(n + 1, 8), :]
                    to_zone_left[q] = packed[q, pl.ds(7, 8), :]

            pl.run_scoped(
                scoped,
                pltpu.VMEM((20, count, rows, LANES), F32),
                pltpu.VMEM((19, count, rows, LANES), F32),
                pltpu.VMEM((20, n + 16, LANES), F32),
            )

        pl.when(me == level)(push)


def pack_flows(post, start, out, first):
    lane = lanes()

    def body(i):
        row = pl.multiple_of(8 * i, 8)
        total = jnp.zeros((8, LANES), F32)
        for k, q in enumerate(Z_OUT):
            v = pltpu.roll(post[q, pl.ds(start + row, 8), :], (16 * k - zone_lane(2, 8, 1)) % LANES, 1)
            total = jnp.where((lane >= 16 * k) & (lane < 16 * k + 16), v, total)
        for group, y, base in ((Y_DOWN, 8, 80), (Y_UP, 23, 85)):
            for k, q in enumerate(group):
                lane0 = base + k
                v = pltpu.roll(post[q, pl.ds(start + row, 8), :], (lane0 - zone_lane(2, y, 0)) % LANES, 1)
                total = jnp.where((lane == lane0) | (lane == lane0 + 25), v, total)
        out[pl.ds(first + row, 8), :] = total

    loop(6, body)


def finest_role(own, solid, low, high, center, left, right, state, message):
    level, row0, n = 3, ROW0[3], OWN[3]

    def scoped(g, pa, pb, wide, zone, zpost, flat, spread, widen3, restrict3):
        widen3[...] = widen_matrix(3)
        restrict3[...] = restrict_chunk(3, 0)
        load_level(level, own, solid, low, high, g)
        load_zone(2, zone, 16, center, left, right)
        covered, rim = zone_masks(2, 0)
        mask = interface_mask(level, 0)

        def substep(v, row, dest):
            v = [jnp.where(mask, wide[q, 0, pl.ds(row, 8), :], v[q]) for q in range(19)]
            post = collided(v, g[19, 0, pl.ds(row, 8), :], level)
            for q in range(19):
                dest[q, 0, pl.ds(row, 8), :] = post[q]

        for cycle in range(4):
            if cycle > 0:

                def zone_collide(row):
                    v = [zone[q, pl.ds(row, 8), :] for q in range(19)]
                    post = collided(v, zone[19, pl.ds(row, 8), :], 2)
                    for q in range(19):
                        zpost[q, pl.ds(row, 8), :] = post[q]

                def zone_pull(row):
                    v = zone_pulled(zpost, 2, row)
                    for q in range(19):
                        zone[q, pl.ds(row, 8), :] = v[q]

                row_loop(8, 6, zone_collide)
                pack_flows(zpost, 8, message, 48 * (cycle - 1))
                row_loop(8, 6, zone_pull)
            convert_zone(2, zone, 8, 6, rim, flat)
            widen(flat, widen3[...], 3, 0, 48, wide, spread, PAD)
            first, groups = (PAD, 12) if cycle < 2 else (PAD + 8, 10)

            def step_one(row):
                substep([g[q, 0, pl.ds(row, 8), :] for q in range(19)], row, pa)

            def step_two(row):
                substep(pulled(pa, level, row, 0), row, pb)

            def step_out(row):
                v = pulled(pb, level, row, 0)
                for q in range(19):
                    g[q, 0, pl.ds(row, 8), :] = v[q]

            row_loop(first, groups, step_one)
            row_loop(first, groups, step_two)
            if cycle < 3:
                row_loop(first, groups, step_out)
                for q in range(19):
                    flat[q] = (
                        g[q, 0, pl.ds(PAD, 48, stride=2), :] + g[q, 0, pl.ds(PAD + 1, 48, stride=2), :]
                    )
                spread[...] = moved(flat[...].reshape(19 * 48, LANES), restrict3[...]).reshape(19, 48, LANES)
                scale = child_scale(3)

                def restrict(i):
                    row = pl.multiple_of(8 * i, 8)
                    v = relax([spread[q, pl.ds(row, 8), :] for q in range(19)], 1.0 - scale, scale)
                    for q in range(19):
                        old = zone[q, pl.ds(8 + row, 8), :]
                        zone[q, pl.ds(8 + row, 8), :] = jnp.where(covered, v[q], old)

                loop(6, restrict)
            else:
                row_loop(row0, n // 8, step_out)
                store_level(level, g, row0, state)
                for q in range(19):
                    flat[q, pl.ds(0, 32), :] = (
                        g[q, 0, pl.ds(row0, 32, stride=2), :] + g[q, 0, pl.ds(row0 + 1, 32, stride=2), :]
                    )
                flat[:, pl.ds(32, 8), :] = jnp.zeros((19, 8, LANES), F32)
                total = None
                for i in range(4):
                    part = jnp.concatenate(
                        [flat[q, pl.ds(8 * i, 8), :] for q in range(19)] + [jnp.zeros((8, LANES), F32)], axis=0
                    )
                    part = moved(part, compact_chunk(i))
                    total = part if total is None else total + part
                scale = child_scale(3)
                v = relax([total[8 * q : 8 * q + 8] for q in range(19)], 1.0 - scale, scale)
                for q in range(19):
                    message[pl.ds(144 + 8 * q, 8), :] = v[q]
                message[pl.ds(296, 8), :] = jnp.zeros((8, LANES), F32)

    rows = ROWS[3]
    pl.run_scoped(
        scoped,
        pltpu.VMEM((20, 1, rows, LANES), F32),
        pltpu.VMEM((19, 1, rows, LANES), F32),
        pltpu.VMEM((19, 1, rows, LANES), F32),
        pltpu.VMEM((19, 1, rows, LANES), F32),
        pltpu.VMEM((20, 64, LANES), F32),
        pltpu.VMEM((19, 64, LANES), F32),
        pltpu.VMEM((19, 48, LANES), F32),
        pltpu.VMEM((19, 48, LANES), F32),
        pltpu.VMEM((2 * LANES, LANES), BF16),
        pltpu.VMEM((2 * LANES, LANES), BF16),
    )


def restrict_pairs(level, g, first, count, skip, flat):
    flat[...] = jnp.zeros(flat.shape, F32)
    for q in range(19):
        for c in range(CHUNKS[level]):
            flat[q, c, pl.ds(skip, count), :] = (
                g[q, c, pl.ds(first, count, stride=2), :] + g[q, c, pl.ds(first + 1, count, stride=2), :]
            )
    rows = flat.shape[2]
    total = None
    for c in range(CHUNKS[level]):
        part = moved(flat[:, c].reshape(flat.shape[0] * rows, LANES), restrict_chunk(level, c))
        total = part if total is None else total + part
    return total.reshape(flat.shape[0], rows, LANES)


def second_role(own, solid, low, high, center, left, right, keep_post, keep_wide, keep_zone):
    level, row0 = 2, ROW0[2]
    first = row0 - 8

    def scoped(g, wide, zone, zpost, conv, spread, flat):
        load_level(level, own, solid, low, high, g)
        load_zone(1, zone, 16, center, left, right)
        covered, rim = zone_masks(1, 0)
        keep_post[19] = g[19]
        convert_zone(1, zone, 8, 4, rim, conv)
        widen(conv, widen_matrix(2), 2, 4, 24, wide, spread, first)
        collide_rows(level, g, g, wide, keep_post, first, 6)
        pull_rows(level, keep_post, g, first, 6)
        collide_rows(level, g, g, wide, keep_post, first, 6)
        pull_rows(level, keep_post, g, first, 6)
        spread[...] = restrict_pairs(level, g, first, 24, 4, flat)
        scale = child_scale(2)

        def restrict(i):
            row = pl.multiple_of(8 * i, 8)
            v = relax([spread[q, pl.ds(row, 8), :] for q in range(19)], 1.0 - scale, scale)
            v = [jnp.where(covered, v[q], zone[q, pl.ds(8 + row, 8), :]) for q in range(19)]
            post = collided(v, zone[19, pl.ds(8 + row, 8), :], 1)
            for q in range(19):
                zpost[q, pl.ds(8 + row, 8), :] = post[q]

        loop(4, restrict)

        def zone_pull(row):
            v = zone_pulled(zpost, 1, row)
            for q in range(19):
                zone[q, pl.ds(row, 8), :] = v[q]

        row_loop(8, 4, zone_pull)
        convert_zone(1, zone, 8, 4, rim, conv)
        widen(conv, widen_matrix(2), 2, 4, 24, keep_wide, spread, first)
        for q in range(19):
            keep_zone[q] = zone[q, pl.ds(16, 16), :]

    pl.run_scoped(
        scoped,
        pltpu.VMEM((20, 2, ROWS[2], LANES), F32),
        pltpu.VMEM((19, 2, ROWS[2], LANES), F32),
        pltpu.VMEM((20, 48, LANES), F32),
        pltpu.VMEM((19, 48, LANES), F32),
        pltpu.VMEM((19, 32, LANES), F32),
        pltpu.VMEM((19, 32, LANES), F32),
        pltpu.VMEM((19, 2, 32, LANES), F32),
    )


def first_role(own, solid, low, high, center, left, right, state, partial):
    level, row0, n = 1, ROW0[1], OWN[1]
    first = row0 - 8

    def scoped(g, post, wide, zone, conv, spread, flat):
        load_level(level, own, solid, low, high, g)
        load_zone(0, zone, 12, center, left, right)
        convert_zone(0, zone, 8, 2, None, conv)
        widen(conv, widen_matrix(1), 1, 0, 16, wide, spread, first)
        collide_rows(level, g, g, wide, post, first, 4)
        pull_rows(level, post, g, first, 4)
        collide_rows(level, g, g, wide, post, first, 4)
        pull_rows(level, post, g, row0, n // 8)
        store_level(level, g, row0, state)
        total = None
        for c in range(CHUNKS[1]):
            part = moved(g[pl.ds(0, 19), c, pl.ds(row0, n), :].reshape(19 * n, LANES), mean_chunk(c))
            total = part if total is None else total + part
        flat[...] = total.reshape(19, n, LANES)
        for q in range(19):
            partial[q] = flat[q, pl.ds(0, 8, stride=2), :] + flat[q, pl.ds(1, 8, stride=2), :]

    pl.run_scoped(
        scoped,
        pltpu.VMEM((20, 4, ROWS[1], LANES), F32),
        pltpu.VMEM((19, 4, ROWS[1], LANES), F32),
        pltpu.VMEM((19, 4, ROWS[1], LANES), F32),
        pltpu.VMEM((20, 32, LANES), F32),
        pltpu.VMEM((19, 16, LANES), F32),
        pltpu.VMEM((19, 16, LANES), F32),
        pltpu.VMEM((19, n, LANES), F32),
    )


def coarse_role(own, solid, low, high, state):
    level, row0 = 0, ROW0[0]

    def scoped(g, post):
        load_level(level, own, solid, low, high, g)
        collide_rows(level, g, g, None, post, row0 - 8, 3)
        pull_rows(level, post, g, row0, 1)
        store_level(level, g, row0, state)

    pl.run_scoped(
        scoped,
        pltpu.VMEM((20, 8, ROWS[0], LANES), F32),
        pltpu.VMEM((19, 8, ROWS[0], LANES), F32),
    )


def main_kernel(
    own, solid, low, high, center, left, right,
    state, message, keep_post, keep_wide, keep_zone, partial,
):
    me = lax.axis_index("level")
    arrived = (own, solid, low, high, center, left, right)

    @pl.when(me == 3)
    def _():
        finest_role(*arrived, state, message)

    @pl.when(me == 2)
    def _():
        second_role(*arrived, keep_post, keep_wide, keep_zone)

    @pl.when(me == 1)
    def _():
        first_role(*arrived, state, partial)

    @pl.when(me == 0)
    def _():
        coarse_role(own, solid, low, high, state)


def return_kernel(
    message, keep_post, keep_wide, keep_zone, partial,
    state, to_first, to_coarse,
):
    me = lax.axis_index("level")
    level, row0 = 2, ROW0[2]
    first = row0 - 8

    @pl.when(me == 2)
    def _():
        def scoped(g, post, override, back, flat, means, zone):
            flows = message[pl.ds(0, 144), :]
            for k, q in enumerate(FLOW_DIRECTIONS):
                total = moved(flows, flow_chunk(q))
                for c in range(2):
                    override[k, c] = total[:, c * LANES : (c + 1) * LANES]

            def overridden(c, row, cycle, v):
                lane = lanes() + c * LANES
                y, z = lane >> 3, lane & 7
                v = list(v)
                for k, q in enumerate(FLOW_DIRECTIONS):
                    mask = flow_mask(q, y, z)
                    v[q] = jnp.where(mask, override[k, c, pl.ds(48 * cycle + row - first, 8), :], v[q])
                return v

            masks = [interface_mask(level, c) for c in range(2)]

            def begin(row):
                for c in range(2):
                    v = overridden(c, row, 0, [keep_post[q, c, pl.ds(row, 8), :] for q in range(19)])
                    for q in range(19):
                        post[q, c, pl.ds(row, 8), :] = v[q]

            row_loop(first, 6, begin)
            for cycle in (1, 2):
                pull_rows(level, post, g, first, 6)

                def body(row, cycle=cycle):
                    for c in range(2):
                        v = [
                            jnp.where(masks[c], keep_wide[q, c, pl.ds(row, 8), :], g[q, c, pl.ds(row, 8), :])
                            for q in range(19)
                        ]
                        v = collided(v, keep_post[19, c, pl.ds(row, 8), :], level)
                        v = overridden(c, row, cycle, v)
                        for q in range(19):
                            post[q, c, pl.ds(row, 8), :] = v[q]

                row_loop(first, 6, body)
            pull_rows(level, post, g, row0, 4)
            means_back = message[pl.ds(144, 160), :]
            for i in range(4):
                total = moved(means_back, spread_chunk(i))
                for c in range(2):
                    back[i, c] = total[:, c * LANES : (c + 1) * LANES].reshape(20, 8, LANES)
            for c in range(2):
                lane = lanes() + c * LANES
                y, z = lane >> 3, lane & 7
                covered = (y >= Y_LOW) & (y <= Y_HIGH) & (z <= 1)
                for i in range(4):
                    for q in range(19):
                        rows = pl.ds(row0 + 8 * i, 8)
                        g[q, c, rows, :] = jnp.where(covered, back[i, c, q], g[q, c, rows, :])
            store_level(level, g, row0, state)
            means[...] = restrict_pairs(level, g, row0, 16, 0, flat)
            scale = child_scale(2)
            covered, _ = zone_masks(1, 0)
            near, _ = zone_masks(1, 1)
            for i in range(2):
                rows = pl.ds(8 * i, 8)
                v = relax([means[q, rows, :] for q in range(19)], 1.0 - scale, scale)
                for q in range(19):
                    value = jnp.where(covered, v[q], keep_zone[q, rows, :])
                    to_first[q, rows, :] = jnp.where(near, value, 0.0)
            zone[...] = moved(to_first[...].reshape(19 * 16, LANES), mean_zone_matrix()).reshape(19, 16, LANES)
            for q in range(19):
                to_coarse[q] = zone[q, pl.ds(0, 8, stride=2), :] + zone[q, pl.ds(1, 8, stride=2), :]

        pl.run_scoped(
            scoped,
            pltpu.VMEM((19, 2, ROWS[2], LANES), F32),
            pltpu.VMEM((19, 2, ROWS[2], LANES), F32),
            pltpu.VMEM((len(FLOW_DIRECTIONS), 2, 144, LANES), F32),
            pltpu.VMEM((4, 2, 20, 8, LANES), F32),
            pltpu.VMEM((19, 2, 16, LANES), F32),
            pltpu.VMEM((19, 16, LANES), F32),
            pltpu.VMEM((19, 16, LANES), F32),
        )

    @pl.when(me == 1)
    def _():
        to_first[:, pl.ds(0, 8), :] = partial[...]


def finish_kernel(old_state, second_state, from_near, from_far, state):
    me = lax.axis_index("level")

    @pl.when(me == 3)
    def _():
        state[...] = old_state[...]

    @pl.when(me == 2)
    def _():
        state[...] = second_state[...]

    @pl.when(me == 1)
    def _():
        def scoped(wide):
            total = moved(from_near[...].reshape(19 * 16, LANES), spread_zone_matrix())
            for c in range(4):
                wide[:, c] = total[:, c * LANES : (c + 1) * LANES].reshape(19, 16, LANES)

            def one(q):
                for j in range(8):
                    c = j % 4
                    lane = lanes() + c * LANES
                    y, z = lane >> 4, lane & 15
                    near = (y >= Y_LOW - 1) & (y <= Y_HIGH + 1) & (z <= 4)
                    columns = pl.ds(j * LANES, LANES)
                    value = wide[q, c, pl.ds(j // 4, 8, stride=2), :]
                    state[q, :, columns] = jnp.where(near, value, old_state[q, :, columns])

            loop(19, one)

        pl.run_scoped(scoped, pltpu.VMEM((19, 4, 16, LANES), F32))

    @pl.when(me == 0)
    def _():
        def scoped(value):
            scale = child_scale(1)
            v = relax(
                [from_near[q, pl.ds(0, 8), :] + from_far[q] for q in range(19)], 1.0 - scale, scale
            )
            for q in range(19):
                value[q] = v[q]
            value[19] = jnp.zeros((8, LANES), F32)
            total = moved(value[...].reshape(160, LANES), spread_covered_matrix())
            for q in range(19):
                for j in range(8):
                    columns = pl.ds(j * LANES, LANES)
                    if not 2 <= j < 6:
                        state[q, :, columns] = old_state[q, :, columns]
                    else:
                        covered = (lanes() & 31) < 8
                        part = total[8 * q : 8 * q + 8, (j - 2) * LANES : (j - 1) * LANES]
                        state[q, :, columns] = jnp.where(covered, part, old_state[q, :, columns])

        pl.run_scoped(scoped, pltpu.VMEM((20, 8, LANES), F32))


def call(kernel, shapes, args):
    return pl.pallas_call(
        kernel,
        out_shape=[jax.ShapeDtypeStruct(s, F32) for s in shapes],
        in_specs=[pl.BlockSpec(memory_space=pltpu.VMEM)] * len(args),
        out_specs=[pl.BlockSpec(memory_space=pltpu.VMEM)] * len(shapes),
        compiler_params=pltpu.CompilerParams(vmem_limit_bytes=24 * 1024 * 1024),
    )(*args)


def shards(populations, solid):
    own, flags = populations[0], solid[0]
    if own.shape != (19, SLAB, NY * NZ):
        raise ValueError("unexpected slab")
    blocks = lax.axis_size("blocks")
    forward = [(i, (i + 1) % blocks) for i in range(blocks)]
    backward = [(i, (i - 1) % blocks) for i in range(blocks)]
    down = [(i, i + 1) for i in range(LEVELS - 1)]

    def diagonal(step):
        return [
            (level * blocks + b, (level + 1) * blocks + (b + step) % blocks)
            for level in range(LEVELS - 1)
            for b in range(blocks)
        ]

    both = ("level", "blocks")
    to_right, to_left, center, zone_right, zone_left = call(
        start_kernel,
        [(20, 16, LANES), (20, 16, LANES), (680, LANES), (20, 8, LANES), (20, 8, LANES)],
        [own, flags],
    )
    center = lax.ppermute(center, "level", down)
    left = lax.ppermute(zone_right, both, diagonal(1))
    right = lax.ppermute(zone_left, both, diagonal(-1))
    low = lax.ppermute(to_right, "blocks", forward)
    high = lax.ppermute(to_left, "blocks", backward)

    state, message, keep_post, keep_wide, keep_zone, partial = call(
        main_kernel,
        [
            (19, SLAB, NY * NZ),
            (304, LANES),
            (20, 2, ROWS[2], LANES),
            (19, 2, ROWS[2], LANES),
            (19, 16, LANES),
            (19, 8, LANES),
        ],
        [own, flags, low, high, center, left, right],
    )
    message = lax.ppermute(message, "level", [(3, 2)])
    second_state, to_first, to_coarse = call(
        return_kernel,
        [(19, SLAB, NY * NZ), (19, 16, LANES), (19, 8, LANES)],
        [message, keep_post, keep_wide, keep_zone, partial],
    )
    near = lax.ppermute(to_first, "level", [(2, 1), (1, 0)])
    far = lax.ppermute(to_coarse, "level", [(2, 0)])
    (state,) = call(
        finish_kernel,
        [(19, SLAB, NY * NZ)],
        [state, second_state, near, far],
    )
    return state[None]


def solution(mesh):
    in_specs = (P("level", None, "blocks", None), P("level", "blocks", None))
    out_specs = P("level", None, "blocks", None)
    return jax.shard_map(shards, mesh=mesh, in_specs=in_specs, out_specs=out_specs, check_vma=False)
```

```python
import jax
import jax.numpy as jnp
from jax import lax
from jax.experimental import pallas as pl
from jax.experimental.pallas import tpu as pltpu
from jax.sharding import PartitionSpec as P

NY = 32
NZ = 32
LEVELS = 4
SLAB = 8
LANES = 128
VELOCITY = (
    (0, 0, 0),
    (1, 0, 0),
    (-1, 0, 0),
    (0, 1, 0),
    (0, -1, 0),
    (0, 0, 1),
    (0, 0, -1),
    (1, 1, 0),
    (-1, -1, 0),
    (1, -1, 0),
    (-1, 1, 0),
    (1, 0, 1),
    (-1, 0, -1),
    (1, 0, -1),
    (-1, 0, 1),
    (0, 1, 1),
    (0, -1, -1),
    (0, 1, -1),
    (0, -1, 1),
)
OPPOSITE = (0, 2, 1, 4, 3, 6, 5, 8, 7, 10, 9, 12, 11, 14, 13, 16, 15, 18, 17)
TAU_BASE = 1.0
F32 = jnp.float32
BF16 = jnp.bfloat16

PAD = 8
MARGIN = (8, 8, 8, 16)
FACTOR = (1, 2, 4, 8)
CHUNKS = (8, 4, 2, 1)
DEPTH = (32, 16, 8, 4)
OWN = tuple(SLAB * f for f in FACTOR)
ROW0 = tuple(PAD + m for m in MARGIN)
ROWS = tuple(OWN[l] + 2 * ROW0[l] for l in range(LEVELS))

Y_LOW = NY // 4
Y_HIGH = 3 * NY // 4 - 1


def zone_lane(level, y, z):
    if level == 0:
        return (y - 8) * 8 + z
    if level == 1:
        return z * 20 + y - 6
    return z * 25 + y - 4


ZONE_CELLS = (
    [(y, z) for y in range(8, 24) for z in range(8)],
    [(y, z) for y in range(6, 26) for z in range(6)],
    [(y, z) for y in range(5, 27) for z in range(5)],
)
ZONE_PITCH = (None, 20, 25)


def level_lane(level, y, z):
    return y * DEPTH[level] + z


def made(columns, weight, holds):
    row = lax.broadcasted_iota(jnp.int32, (LANES, columns), 0)
    column = lax.broadcasted_iota(jnp.int32, (LANES, columns), 1)
    matrix = jnp.where(holds(row, column), weight, 0.0).astype(BF16)
    return jnp.concatenate([matrix, matrix], axis=0)


def cell_of(level, lane):
    return lane >> (DEPTH[level].bit_length() - 1), lane & (DEPTH[level] - 1)


def pack_chunk(level, c):
    ys, zs = zip(*ZONE_CELLS[level])

    def holds(row, column):
        y, z = cell_of(level, row + c * LANES)
        inside = (y >= min(ys)) & (y <= max(ys)) & (z <= max(zs))
        return inside & (column == zone_lane(level, y, z))

    return made(LANES, 1.0, holds)


def widen_matrix(child):
    def holds(row, column):
        y, z = cell_of(child, column)
        edge = (y == 0) | (y == NY - 1) | (z == DEPTH[child] - 1)
        return edge & (row == zone_lane(child - 1, 8 + (y >> 1), z >> 1))

    return made(CHUNKS[child] * LANES, 1.0, holds)


def restrict_chunk(child, c):
    def holds(row, column):
        y, z = cell_of(child, row + c * LANES)
        return column == zone_lane(child - 1, 8 + (y >> 1), z >> 1)

    return made(LANES, 0.125, holds)


def compact_chunk(i):
    def holds(row, column):
        y, z = cell_of(3, row)
        return column == 32 * i + (y >> 1) * 2 + (z >> 1)

    return made(LANES, 0.125, holds)


def spread_chunk(i):
    def holds(row, column):
        y, z = cell_of(2, column)
        return (y >= Y_LOW) & (y <= Y_HIGH) & (z <= 1) & (row == 32 * i + (y - Y_LOW) * 2 + z)

    return made(2 * LANES, 1.0, holds)


def near_first(y, z):
    return (y >= Y_LOW - 1) & (y <= Y_HIGH + 1) & (z <= 4)


def mean_chunk(c):
    def holds(row, column):
        y, z = cell_of(1, row + c * LANES)
        return jnp.logical_not(near_first(y, z)) & (column == zone_lane(0, 8 + (y >> 1), z >> 1))

    return made(LANES, 0.125, holds)


def zone_cell(level, lane):
    pitch, first = ZONE_PITCH[level], 6 if level == 1 else 4
    z = sum((lane >= pitch * k).astype(jnp.int32) for k in range(1, 7))
    return lane - pitch * z + first, z


def covered_first(y, z):
    return (y >= Y_LOW) & (y <= Y_HIGH) & (z <= 3)


def mean_lane(y, z):
    return y - 11 + 10 * z


def mean_ring_matrix():
    def holds(row, column):
        y, z = zone_cell(1, row)
        ring = near_first(y, z) & jnp.logical_not(covered_first(y, z))
        return ring & (column == mean_lane(8 + (y >> 1), z >> 1))

    return made(LANES, 0.125, holds)


def late_chunk(half, c):
    def holds(row, column):
        y, z = cell_of(2, row + c * LANES)
        return column == 64 * half + (z >> 1) * 16 + (y >> 1)

    return made(LANES, 0.125, holds)


def late_back_chunk(half):
    def holds(row, column):
        y, z = cell_of(1, column + LANES)
        return covered_first(y, z) & (row == 64 * half + z * 16 + y - Y_LOW)

    return made(2 * LANES, 1.0, holds)


def deep_late(cell):
    return (cell >= 4) & (cell < 12)


def late_mean_matrix(half, deep):
    def holds(row, column):
        cell = row - 64 * half
        inside = (cell >= 0) & (cell < 64)
        inside = inside & (deep_late(cell) if deep else jnp.logical_not(deep_late(cell)))
        return inside & (column == mean_lane(12 + ((cell & 15) >> 1), cell >> 5))

    return made(LANES, 0.125, holds)


def deep_matrix(odd):
    def holds(row, column):
        i, y = row >> 5, (row & 31) >> 1
        return ((i & 1) == odd) & (column == 64 * (i >> 1) + 4 + (y >> 1))

    return made(LANES, 0.125, holds)


def mean_back_matrix():
    def holds(row, column):
        z = (row >= 10).astype(jnp.int32) + (row >= 20).astype(jnp.int32)
        return (row < 30) & (column == zone_lane(0, row - 10 * z + 11, z))

    return made(LANES, 1.0, holds)


def packed_planes(source, out, width):
    lane = lanes()
    per = LANES // width
    for plane in range(-(-19 // per)):
        total = jnp.zeros((8, LANES), F32)
        for k in range(per):
            q = per * plane + k
            if q < 19:
                part = source[q] if k == 0 else pltpu.roll(source[q], width * k, 1)
                total = jnp.where((lane >= width * k) & (lane < width * (k + 1)), part, total)
        out[pl.ds(8 * plane, 8), :] = total


def late_means(late, deep, value, scratch):
    for half in range(2):
        scratch[...] = moved(late[...], late_mean_matrix(half, deep)).reshape(20, 8, LANES)
        for q in range(19):
            value[q, pl.ds(4 * half, 4), :] = (
                scratch[q, pl.ds(0, 4, stride=2), :] + scratch[q, pl.ds(1, 4, stride=2), :]
            )


def spread_zone_matrix():
    def holds(row, column):
        y, z = cell_of(1, column)
        return near_first(y, z) & (row == zone_lane(1, y, z))

    return made(4 * LANES, 1.0, holds)


def spread_covered_matrix():
    def holds(row, column):
        y, z = cell_of(0, column + 2 * LANES)
        return (z < 8) & (row == zone_lane(0, y, z))

    return made(4 * LANES, 1.0, holds)


Z_OUT = (5, 11, 14, 15, 18)
Y_DOWN = (4, 8, 9, 16, 18)
Y_UP = (3, 7, 10, 15, 17)
FLOW_DIRECTIONS = tuple(sorted(set(Z_OUT + Y_DOWN + Y_UP)))


def flow_mask(q, y, z):
    mask = None
    if q in Z_OUT:
        mask = (z == 1) & (y >= Y_LOW) & (y <= Y_HIGH)
    for group, edge in ((Y_DOWN, Y_LOW), (Y_UP, Y_HIGH)):
        if q in group:
            cells = (y == edge) & (z <= 1)
            mask = cells if mask is None else mask | cells
    return mask


def flow_chunk(q):
    def holds(row, column):
        y, z = cell_of(2, column)
        source = None
        if q in Y_DOWN:
            source = 80 + Y_DOWN.index(q) + 25 * z
        if q in Y_UP:
            source = 85 + Y_UP.index(q) + 25 * z
        if q in Z_OUT:
            over = 16 * Z_OUT.index(q) + y - Y_LOW
            source = over if source is None else jnp.where(z == 1, over, source)
        return flow_mask(q, y, z) & (row == source)

    return made(2 * LANES, 1.0, holds)


def relaxation(level_id):
    return 2.0**level_id * (TAU_BASE - 0.5) + 0.5


def parent_scale(child):
    return relaxation(child) / (2.0 * relaxation(child - 1))


def child_scale(child):
    return 2.0 * relaxation(child - 1) / relaxation(child)


def relax(v, a, b):
    s = [None] + [v[2 * k - 1] + v[2 * k] for k in range(1, 10)]
    d = [None] + [v[2 * k - 1] - v[2 * k] for k in range(1, 10)]
    rho = (
        (1.0 / 3.0) * v[0]
        + (1.0 / 18.0) * (s[1] + s[2] + s[3])
        + (1.0 / 36.0) * ((s[4] + s[5]) + (s[6] + s[7]) + (s[8] + s[9]))
    )
    mx = (1.0 / 18.0) * d[1] + (1.0 / 36.0) * ((d[4] + d[5]) + (d[6] + d[7]))
    my = (1.0 / 18.0) * d[2] + (1.0 / 36.0) * ((d[4] - d[5]) + (d[8] + d[9]))
    mz = (1.0 / 18.0) * d[3] + (1.0 / 36.0) * ((d[6] - d[7]) + (d[8] - d[9]))
    inv = 1.0 / rho
    ux, uy, uz = mx * inv, my * inv, mz * inv
    ra = a * rho
    base = ra - (1.5 * ra) * (ux * ux + uy * uy + uz * uz)
    r45 = 4.5 * ra
    ra3 = 3.0 * ra

    def kept(q):
        return v[q] if b == 1.0 else b * v[q]

    out = [base if b == 0.0 else base + kept(0)]
    cus = (ux, uy, uz, ux + uy, ux - uy, ux + uz, ux - uz, uy + uz, uy - uz)
    for k in range(1, 10):
        cu = cus[k - 1]
        even = base + r45 * (cu * cu)
        odd = ra3 * cu
        plus, minus = even + odd, even - odd
        if b != 0.0:
            plus, minus = plus + kept(2 * k - 1), minus + kept(2 * k)
        out += [plus, minus]
    return out


def collided(v, solid, level):
    inv_tau = 1.0 / relaxation(level)
    relaxed = relax(v, inv_tau, 1.0 - inv_tau)
    flag = solid != 0.0
    return [jnp.where(flag, v[OPPOSITE[q]], relaxed[q]) for q in range(19)]


def lanes():
    return lax.broadcasted_iota(jnp.int32, (8, LANES), 1)


def interface_mask(level, c):
    lane = lanes()
    nz = DEPTH[level]
    mask = (lane & (nz - 1)) == nz - 1
    if c == 0:
        mask = mask | (lane < nz)
    if c == CHUNKS[level] - 1:
        mask = mask | (lane >= LANES - nz)
    return mask


def pulled(post, level, row, c):
    lane = lanes()
    nz, count = DEPTH[level], CHUNKS[level]
    out = []
    for q in range(19):
        cx, cy, cz = VELOCITY[q]
        shift = cy * nz + cz
        value = post[q, c, pl.ds(row - cx, 8), :]
        if shift != 0:
            value = pltpu.roll(value, shift % LANES, 1)
            outside = None
            if cy == 1:
                if c > 0:
                    other = pltpu.roll(post[q, c - 1, pl.ds(row - cx, 8), :], shift, 1)
                    value = jnp.where(lane < shift, other, value)
                else:
                    outside = lane < nz
            if cy == -1:
                if c < count - 1:
                    other = pltpu.roll(post[q, c + 1, pl.ds(row - cx, 8), :], shift % LANES, 1)
                    value = jnp.where(lane >= LANES + shift, other, value)
                else:
                    outside = lane >= LANES - nz
            if cz != 0:
                edge = (lane & (nz - 1)) == (0 if cz == 1 else nz - 1)
                outside = edge if outside is None else outside | edge
            if outside is not None:
                value = jnp.where(outside, post[OPPOSITE[q], c, pl.ds(row, 8), :], value)
        out.append(value)
    return out


def zone_pulled(post, level, row):
    lane = lanes()
    pitch = ZONE_PITCH[level]
    out = []
    for q in range(19):
        cx, cy, cz = VELOCITY[q]
        shift = cz * pitch + cy
        value = post[q, pl.ds(row - cx, 8), :]
        if shift != 0:
            value = pltpu.roll(value, shift % LANES, 1)
            if cz == 1:
                value = jnp.where(lane < pitch, post[OPPOSITE[q], pl.ds(row, 8), :], value)
        out.append(value)
    return out


def zone_masks(level, reach):
    lane = lanes()
    pitch, first = ZONE_PITCH[level], 6 if level == 1 else 4
    top = DEPTH[level] // 4 - 1
    inside = None
    rim = None
    for z in range(top + reach + 1):
        start = z * pitch - first
        row = (lane >= start + Y_LOW - reach) & (lane <= start + Y_HIGH + reach)
        inside = row if inside is None else inside | row
        if z < top:
            row = (lane == start + Y_LOW) | (lane == start + Y_HIGH)
        elif z == top:
            row = (lane >= start + Y_LOW) & (lane <= start + Y_HIGH)
        else:
            continue
        rim = row if rim is None else rim | row
    return inside, rim


def loop(count, body, unroll=None):
    def step(i, carry):
        body(i)
        return carry

    if unroll is None:
        unroll = max(u for u in range(1, 7) if count % u == 0)
    lax.fori_loop(0, count, step, 0, unroll=unroll)


def row_loop(start, count, body):
    loop(count, lambda i: body(pl.multiple_of(start + 8 * i, 8)))


def moved(value, matrix):
    high = value.astype(BF16)
    low = (value - high.astype(F32)).astype(BF16)
    return jnp.dot(jnp.concatenate([high, low], axis=1), matrix, preferred_element_type=F32)


def load_level(level, own, solid, low, high, buf):
    factor, count, row0 = FACTOR[level], CHUNKS[level], ROW0[level]
    n = OWN[level]

    def one(q, source):
        for j in range(8):
            buf[q, j % count, pl.ds(row0 + j // count, 8, stride=factor), :] = source(j)
        if low is not None:
            for c in range(count):
                rows = pl.ds(c, 2 * factor, stride=count) if count > 1 else pl.ds(0, 2 * factor)
                buf[q, c, pl.ds(row0 - 2 * factor, 2 * factor), :] = low[q, rows, :]
                buf[q, c, pl.ds(row0 + n, 2 * factor), :] = high[q, rows, :]

    loop(19, lambda q: one(q, lambda j: own[q, :, pl.ds(j * LANES, LANES)]))
    one(19, lambda j: solid[:, pl.ds(j * LANES, LANES)].astype(F32))


def store_level(level, buf, row0, out):
    factor, count = FACTOR[level], CHUNKS[level]

    def one(q):
        for j in range(8):
            out[q, :, pl.ds(j * LANES, LANES)] = buf[
                q, j % count, pl.ds(row0 + j // count, 8, stride=factor), :
            ]

    loop(19, one)


def collide_rows(level, source, solid, wide, dest, start, groups):
    masks = [interface_mask(level, c) for c in range(CHUNKS[level])]

    def body(row):
        for c in range(CHUNKS[level]):
            v = [source[q, c, pl.ds(row, 8), :] for q in range(19)]
            if wide is not None:
                v = [jnp.where(masks[c], wide[q, c, pl.ds(row, 8), :], v[q]) for q in range(19)]
            post = collided(v, solid[19, c, pl.ds(row, 8), :], level)
            for q in range(19):
                dest[q, c, pl.ds(row, 8), :] = post[q]

    row_loop(start, groups, body)


def pull_rows(level, post, dest, start, groups):
    def body(row):
        for c in range(CHUNKS[level]):
            v = pulled(post, level, row, c)
            for q in range(19):
                dest[q, c, pl.ds(row, 8), :] = v[q]

    row_loop(start, groups, body)


def load_zone(level, zone, zero_row, center, left, right):
    n = OWN[level]
    zone[...] = jnp.zeros(zone.shape, F32)
    for q in range(20):
        zone[q, pl.ds(zero_row - 1, n + 2), :] = center[pl.ds(q * 34, n + 2), :]
        zone[q, pl.ds(zero_row - 7, 8), :] += left[q]
        zone[q, pl.ds(zero_row + n - 1, 8), :] += right[q]


def convert_zone(level, zone, start, groups, rim, out):
    scale = parent_scale(level + 1)

    def body(i):
        row = pl.multiple_of(8 * i, 8)
        v = [zone[q, pl.ds(start + row, 8), :] for q in range(19)]
        v = relax(v, 1.0 - scale, scale)
        for q in range(19):
            out[q, pl.ds(row, 8), :] = v[q] if rim is None else jnp.where(rim, v[q], 0.0)

    loop(groups, body)


def widen(converted, matrix, child, skip, count, wide, spread, first):
    rows = converted.shape[1]
    value = moved(converted[...].reshape(19 * rows, LANES), matrix)
    for c in range(CHUNKS[child]):
        part = value[:, c * LANES : (c + 1) * LANES].reshape(19, rows, LANES)
        spread[pl.ds(0, 19)] = part
        for q in range(19):
            t = spread[q, pl.ds(skip, count), :]
            wide[q, c, pl.ds(first, count, stride=2), :] = t
            wide[q, c, pl.ds(first + 1, count, stride=2), :] = t


def start_kernel(own, solid, to_right, to_left, center, to_zone_right, to_zone_left):
    me = lax.axis_index("level")

    def halo(q, source):
        for j in range(8):
            to_left[q, pl.ds(j, 2, stride=8), :] = source(pl.ds(0, 2), j)
            to_right[q, pl.ds(j, 2, stride=8), :] = source(pl.ds(SLAB - 2, 2), j)

    loop(19, lambda q: halo(q, lambda rows, j: own[q, rows, pl.ds(j * LANES, LANES)]))
    halo(19, lambda rows, j: solid[rows, pl.ds(j * LANES, LANES)].astype(F32))

    for level in range(3):

        def push(level=level):
            n, row0, count, rows = OWN[level], ROW0[level], CHUNKS[level], ROWS[level]

            def scoped(buf, post, packed):
                post[...] = jnp.zeros(post.shape, F32)
                buf[19] = jnp.zeros(buf.shape[1:], F32)
                load_level(level, own, solid, None, None, buf)
                collide_rows(level, buf, buf, None, post, row0, n // 8)
                pull_rows(level, post, buf, row0 - 8, n // 8 + 2)
                total = None
                for c in range(count):
                    part = buf[:, c, pl.ds(row0 - 8, n + 16), :].reshape(20 * (n + 16), LANES)
                    part = moved(part, pack_chunk(level, c))
                    total = part if total is None else total + part
                packed[...] = total.reshape(20, n + 16, LANES)
                for q in range(20):
                    center[pl.ds(q * 34, n + 2), :] = packed[q, pl.ds(7, n + 2), :]
                    to_zone_right[q] = packed[q, pl.ds(n + 1, 8), :]
                    to_zone_left[q] = packed[q, pl.ds(7, 8), :]

            pl.run_scoped(
                scoped,
                pltpu.VMEM((20, count, rows, LANES), F32),
                pltpu.VMEM((19, count, rows, LANES), F32),
                pltpu.VMEM((20, n + 16, LANES), F32),
            )

        pl.when(me == level)(push)


def pack_flows(post, start, out, first):
    lane = lanes()

    def body(i):
        row = pl.multiple_of(8 * i, 8)
        total = jnp.zeros((8, LANES), F32)
        for k, q in enumerate(Z_OUT):
            v = pltpu.roll(post[q, pl.ds(start + row, 8), :], (16 * k - zone_lane(2, 8, 1)) % LANES, 1)
            total = jnp.where((lane >= 16 * k) & (lane < 16 * k + 16), v, total)
        for group, y, base in ((Y_DOWN, 8, 80), (Y_UP, 23, 85)):
            for k, q in enumerate(group):
                lane0 = base + k
                v = pltpu.roll(post[q, pl.ds(start + row, 8), :], (lane0 - zone_lane(2, y, 0)) % LANES, 1)
                total = jnp.where((lane == lane0) | (lane == lane0 + 25), v, total)
        out[pl.ds(first + row, 8), :] = total

    loop(6, body)


def finest_cycle(g, pa, pb, wide, first, groups):
    mask = interface_mask(3, 0)

    def substep(v, row, dest):
        v = [jnp.where(mask, wide[q, 0, pl.ds(row, 8), :], v[q]) for q in range(19)]
        post = collided(v, g[19, 0, pl.ds(row, 8), :], 3)
        for q in range(19):
            dest[q, 0, pl.ds(row, 8), :] = post[q]

    row_loop(first, groups, lambda row: substep([g[q, 0, pl.ds(row, 8), :] for q in range(19)], row, pa))
    row_loop(first, groups, lambda row: substep(pulled(pa, 3, row, 0), row, pb))


def finest_role(own, solid, low, high, center, left, right, g, zpost, flows):
    def scoped(pa, pb, wide, zone, flat, spread, widen3, restrict3):
        widen3[...] = widen_matrix(3)
        restrict3[...] = restrict_chunk(3, 0)
        load_level(3, own, solid, low, high, g)
        load_zone(2, zone, 16, center, left, right)
        covered, rim = zone_masks(2, 0)
        scale = child_scale(3)

        def restrict(i):
            row = pl.multiple_of(8 * i, 8)
            v = relax([spread[q, pl.ds(row, 8), :] for q in range(19)], 1.0 - scale, scale)
            v = [jnp.where(covered, v[q], zone[q, pl.ds(8 + row, 8), :]) for q in range(19)]
            post = collided(v, zone[19, pl.ds(8 + row, 8), :], 2)
            for q in range(19):
                zpost[q, pl.ds(8 + row, 8), :] = post[q]

        def zone_pull(row):
            v = zone_pulled(zpost, 2, row)
            for q in range(19):
                zone[q, pl.ds(row, 8), :] = v[q]

        def interface():
            convert_zone(2, zone, 8, 6, rim, flat)
            widen(flat, widen3[...], 3, 0, 48, wide, spread, PAD)

        interface()
        for cycle in range(3):
            first, groups = (PAD, 12) if cycle < 2 else (PAD + 8, 10)

            def step_out(row):
                v = pulled(pb, 3, row, 0)
                for q in range(19):
                    g[q, 0, pl.ds(row, 8), :] = v[q]

            finest_cycle(g, pa, pb, wide, first, groups)
            row_loop(first, groups, step_out)
            for q in range(19):
                flat[q] = g[q, 0, pl.ds(PAD, 48, stride=2), :] + g[q, 0, pl.ds(PAD + 1, 48, stride=2), :]
            spread[...] = moved(flat[...].reshape(19 * 48, LANES), restrict3[...]).reshape(19, 48, LANES)
            loop(6, restrict)
            pack_flows(zpost, 8, flows, 48 * cycle)
            if cycle < 2:
                row_loop(8, 6, zone_pull)
                interface()

    rows = ROWS[3]
    pl.run_scoped(
        scoped,
        pltpu.VMEM((19, 1, rows, LANES), F32),
        pltpu.VMEM((19, 1, rows, LANES), F32),
        pltpu.VMEM((19, 1, rows, LANES), F32),
        pltpu.VMEM((20, 64, LANES), F32),
        pltpu.VMEM((19, 48, LANES), F32),
        pltpu.VMEM((19, 48, LANES), F32),
        pltpu.VMEM((2 * LANES, LANES), BF16),
        pltpu.VMEM((2 * LANES, LANES), BF16),
    )


def last_cycle_kernel(g, zpost, state, means, far_first, far_coarse):
    row0, n = ROW0[3], OWN[3]

    @pl.when(lax.axis_index("level") == 3)
    def _():
        def scoped(pa, pb, wide, zone, flat, spread, out, pairs, value, scratch):
            _, rim = zone_masks(2, 0)

            def zone_pull(row):
                v = zone_pulled(zpost, 2, row)
                for q in range(19):
                    zone[q, pl.ds(row, 8), :] = v[q]

            row_loop(8, 6, zone_pull)
            convert_zone(2, zone, 8, 6, rim, flat)
            widen(flat, widen_matrix(3), 3, 0, 48, wide, spread, PAD)
            finest_cycle(g, pa, pb, wide, PAD + 8, 10)

            def step_out(row):
                v = pulled(pb, 3, row, 0)
                for q in range(19):
                    out[q, 0, pl.ds(row - row0, 8), :] = v[q]

            row_loop(row0, n // 8, step_out)
            for q in range(19):
                flat[q, pl.ds(0, 32), :] = (
                    out[q, 0, pl.ds(0, 32, stride=2), :] + out[q, 0, pl.ds(1, 32, stride=2), :]
                )
            total = None
            for i in range(4):
                part = jnp.concatenate(
                    [flat[q, pl.ds(8 * i, 8), :] for q in range(19)] + [jnp.zeros((8, LANES), F32)], axis=0
                )
                part = moved(part, compact_chunk(i))
                total = part if total is None else total + part
            scale = child_scale(3)
            v = relax([total[8 * q : 8 * q + 8] for q in range(19)], 1.0 - scale, scale)
            for q in range(19):
                means[pl.ds(8 * q, 8), :] = v[q]
            means[pl.ds(152, 8), :] = jnp.zeros((8, LANES), F32)
            pairs[...] = jnp.zeros(pairs.shape, F32)
            for q in range(19):
                pairs[pl.ds(4 * q, 4), :] = (
                    means[pl.ds(8 * q, 4, stride=2), :] + means[pl.ds(8 * q + 1, 4, stride=2), :]
                )
            for odd in range(2):
                scratch[pl.ds(0, 80), :] = moved(pairs[...], deep_matrix(odd))
                for q in range(19):
                    value[pl.ds(8 * q + 4 * odd, 4), :] = scratch[pl.ds(4 * q, 4), :]
            scale = child_scale(2)
            v = relax([value[pl.ds(8 * q, 8), :] for q in range(19)], 1.0 - scale, scale)
            deep = deep_late(lanes() & 63)
            for q in range(19):
                value[pl.ds(8 * q, 8), :] = jnp.where(deep, v[q], 0.0)
            value[pl.ds(152, 8), :] = jnp.zeros((8, LANES), F32)
            lane = lanes()
            for plane in range(3):
                total = jnp.zeros((8, LANES), F32)
                for k in range(8):
                    q = 8 * plane + k
                    if q < 19:
                        part = pltpu.roll(value[pl.ds(8 * q, 8), :], (8 * k - 4) % LANES, 1)
                        total = jnp.where(((lane & 63) >> 3) == k, part, total)
                far_first[pl.ds(8 * plane, 8), :] = total
            late_means(value, True, flat.at[:, pl.ds(0, 8)], spread.at[pl.ds(0, 20), pl.ds(0, 8)])
            packed_planes([flat[q, pl.ds(0, 8), :] for q in range(19)], far_coarse, 32)
            store_level(3, out, 0, state)

        rows = ROWS[3]
        pl.run_scoped(
            scoped,
            pltpu.VMEM((19, 1, rows, LANES), F32),
            pltpu.VMEM((19, 1, rows, LANES), F32),
            pltpu.VMEM((19, 1, rows, LANES), F32),
            pltpu.VMEM((19, 64, LANES), F32),
            pltpu.VMEM((19, 48, LANES), F32),
            pltpu.VMEM((20, 48, LANES), F32),
            pltpu.VMEM((19, 1, n, LANES), F32),
            pltpu.VMEM((80, LANES), F32),
            pltpu.VMEM((160, LANES), F32),
            pltpu.VMEM((80, LANES), F32),
        )


def restrict_pairs(level, g, first, count, skip, flat):
    flat[...] = jnp.zeros(flat.shape, F32)
    for q in range(19):
        for c in range(CHUNKS[level]):
            flat[q, c, pl.ds(skip, count), :] = (
                g[q, c, pl.ds(first, count, stride=2), :] + g[q, c, pl.ds(first + 1, count, stride=2), :]
            )
    rows = flat.shape[2]
    total = None
    for c in range(CHUNKS[level]):
        part = moved(flat[:, c].reshape(flat.shape[0] * rows, LANES), restrict_chunk(level, c))
        total = part if total is None else total + part
    return total.reshape(flat.shape[0], rows, LANES)


def second_role(own, solid, low, high, center, left, right, keep_post, keep_wide, early, ring):
    level, row0 = 2, ROW0[2]
    first = row0 - 8

    def scoped(g, wide, zone, zpost, conv, spread, flat):
        load_level(level, own, solid, low, high, g)
        load_zone(1, zone, 16, center, left, right)
        covered, rim = zone_masks(1, 0)
        keep_post[19] = g[19]
        convert_zone(1, zone, 8, 4, rim, conv)
        widen(conv, widen_matrix(2), 2, 4, 24, wide, spread, first)
        collide_rows(level, g, g, wide, keep_post, first, 6)
        pull_rows(level, keep_post, g, first, 6)
        collide_rows(level, g, g, wide, keep_post, first, 6)
        pull_rows(level, keep_post, g, first, 6)
        spread[...] = restrict_pairs(level, g, first, 24, 4, flat)
        scale = child_scale(2)

        def restrict(i):
            row = pl.multiple_of(8 * i, 8)
            v = relax([spread[q, pl.ds(row, 8), :] for q in range(19)], 1.0 - scale, scale)
            v = [jnp.where(covered, v[q], zone[q, pl.ds(8 + row, 8), :]) for q in range(19)]
            post = collided(v, zone[19, pl.ds(8 + row, 8), :], 1)
            for q in range(19):
                zpost[q, pl.ds(8 + row, 8), :] = post[q]

        loop(4, restrict)

        def zone_pull(row):
            v = zone_pulled(zpost, 1, row)
            for q in range(19):
                zone[q, pl.ds(row, 8), :] = v[q]

        row_loop(8, 4, zone_pull)
        convert_zone(1, zone, 8, 4, rim, conv)
        widen(conv, widen_matrix(2), 2, 4, 24, keep_wide, spread, first)
        near, _ = zone_masks(1, 1)
        for q in range(19):
            for i in range(2):
                rows = pl.ds(8 * i, 8)
                early[q, rows, :] = jnp.where(near, zone[q, pl.ds(16 + 8 * i, 8), :], 0.0)
        mean = moved(early[...].reshape(19 * 16, LANES), mean_ring_matrix())
        spread[:, pl.ds(0, 16), :] = mean.reshape(19, 16, LANES)
        for q in range(19):
            ring[q] = spread[q, pl.ds(0, 8, stride=2), :] + spread[q, pl.ds(1, 8, stride=2), :]

    pl.run_scoped(
        scoped,
        pltpu.VMEM((20, 2, ROWS[2], LANES), F32),
        pltpu.VMEM((19, 2, ROWS[2], LANES), F32),
        pltpu.VMEM((20, 48, LANES), F32),
        pltpu.VMEM((19, 48, LANES), F32),
        pltpu.VMEM((19, 32, LANES), F32),
        pltpu.VMEM((19, 32, LANES), F32),
        pltpu.VMEM((19, 2, 32, LANES), F32),
    )


def first_role(own, solid, low, high, center, left, right, state, early):
    level, row0, n = 1, ROW0[1], OWN[1]
    first = row0 - 8

    def scoped(g, post, wide, zone, conv, spread, flat):
        load_level(level, own, solid, low, high, g)
        load_zone(0, zone, 12, center, left, right)
        convert_zone(0, zone, 8, 2, None, conv)
        widen(conv, widen_matrix(1), 1, 0, 16, wide, spread, first)
        collide_rows(level, g, g, wide, post, first, 4)
        pull_rows(level, post, g, first, 4)
        collide_rows(level, g, g, wide, post, first, 4)
        pull_rows(level, post, g, row0, n // 8)
        store_level(level, g, row0, state)
        total = None
        for c in range(CHUNKS[1]):
            part = moved(g[pl.ds(0, 19), c, pl.ds(row0, n), :].reshape(19 * n, LANES), mean_chunk(c))
            total = part if total is None else total + part
        flat[...] = total.reshape(19, n, LANES)
        for q in range(19):
            early[q, pl.ds(0, 8), :] = flat[q, pl.ds(0, 8, stride=2), :] + flat[q, pl.ds(1, 8, stride=2), :]

    pl.run_scoped(
        scoped,
        pltpu.VMEM((20, 4, ROWS[1], LANES), F32),
        pltpu.VMEM((19, 4, ROWS[1], LANES), F32),
        pltpu.VMEM((19, 4, ROWS[1], LANES), F32),
        pltpu.VMEM((20, 32, LANES), F32),
        pltpu.VMEM((19, 16, LANES), F32),
        pltpu.VMEM((19, 16, LANES), F32),
        pltpu.VMEM((19, n, LANES), F32),
    )


def coarse_role(own, solid, low, high, state):
    level, row0 = 0, ROW0[0]

    def scoped(g, post):
        load_level(level, own, solid, low, high, g)
        collide_rows(level, g, g, None, post, row0 - 8, 3)
        pull_rows(level, post, g, row0, 1)
        store_level(level, g, row0, state)

    pl.run_scoped(
        scoped,
        pltpu.VMEM((20, 8, ROWS[0], LANES), F32),
        pltpu.VMEM((19, 8, ROWS[0], LANES), F32),
    )


def main_kernel(
    own, solid, low, high, center, left, right,
    state, fine, fine_post, flows, keep_post, keep_wide, early, ring,
):
    me = lax.axis_index("level")
    arrived = (own, solid, low, high, center, left, right)

    @pl.when(me == 3)
    def _():
        finest_role(*arrived, fine, fine_post, flows)

    @pl.when(me == 2)
    def _():
        second_role(*arrived, keep_post, keep_wide, early, ring)

    @pl.when(me == 1)
    def _():
        first_role(*arrived, state, early)

    @pl.when(me == 0)
    def _():
        coarse_role(own, solid, low, high, state)


def flow_kernel(flows, keep_post, keep_wide, ring, result, late, late_mean):
    level, row0 = 2, ROW0[2]
    first = row0 - 8

    @pl.when(lax.axis_index("level") == 2)
    def _():
        def scoped(g, post, override, flat, value, scratch):
            for k, q in enumerate(FLOW_DIRECTIONS):
                total = moved(flows[...], flow_chunk(q))
                for c in range(2):
                    override[k, c] = total[:, c * LANES : (c + 1) * LANES]

            def overridden(c, row, cycle, v):
                y, z = cell_of(2, lanes() + c * LANES)
                v = list(v)
                for k, q in enumerate(FLOW_DIRECTIONS):
                    value = override[k, c, pl.ds(48 * cycle + row - first, 8), :]
                    v[q] = jnp.where(flow_mask(q, y, z), value, v[q])
                return v

            masks = [interface_mask(level, c) for c in range(2)]

            def begin(row):
                for c in range(2):
                    v = overridden(c, row, 0, [keep_post[q, c, pl.ds(row, 8), :] for q in range(19)])
                    for q in range(19):
                        post[q, c, pl.ds(row, 8), :] = v[q]

            row_loop(first, 6, begin)
            for cycle in (1, 2):
                pull_rows(level, post, g, first, 6)

                def body(row, cycle=cycle):
                    for c in range(2):
                        v = [
                            jnp.where(masks[c], keep_wide[q, c, pl.ds(row, 8), :], g[q, c, pl.ds(row, 8), :])
                            for q in range(19)
                        ]
                        v = collided(v, keep_post[19, c, pl.ds(row, 8), :], level)
                        v = overridden(c, row, cycle, v)
                        for q in range(19):
                            post[q, c, pl.ds(row, 8), :] = v[q]

                row_loop(first, 6, body)

            def last(row):
                for c in range(2):
                    v = pulled(post, level, row, c)
                    for q in range(19):
                        result[q, c, pl.ds(row - row0, 8), :] = v[q]

            row_loop(row0, 4, last)
            for q in range(19):
                for c in range(2):
                    flat[c, q] = result[q, c, pl.ds(0, 16, stride=2), :] + result[q, c, pl.ds(1, 16, stride=2), :]
            flat[:, 19] = jnp.zeros((2, 16, LANES), F32)
            total = None
            for half in range(2):
                for c in range(2):
                    part = moved(flat[c, :, pl.ds(8 * half, 8), :].reshape(160, LANES), late_chunk(half, c))
                    total = part if total is None else total + part
            scale = child_scale(2)
            v = relax([total[8 * q : 8 * q + 8] for q in range(19)], 1.0 - scale, scale)
            for q in range(19):
                late[pl.ds(8 * q, 8), :] = v[q]
            late[pl.ds(152, 8), :] = jnp.zeros((8, LANES), F32)
            late_means(late, False, value, scratch)
            packed_planes([value[q] + ring[q] for q in range(19)], late_mean, 32)

        pl.run_scoped(
            scoped,
            pltpu.VMEM((19, 2, ROWS[2], LANES), F32),
            pltpu.VMEM((19, 2, ROWS[2], LANES), F32),
            pltpu.VMEM((len(FLOW_DIRECTIONS), 2, 144, LANES), F32),
            pltpu.VMEM((2, 20, 16, LANES), F32),
            pltpu.VMEM((19, 8, LANES), F32),
            pltpu.VMEM((20, 8, LANES), F32),
        )


def finish_kernel(old_state, result, third_state, early, near, far, far_coarse, state):
    me = lax.axis_index("level")

    @pl.when(me == 3)
    def _():
        state[...] = third_state[...]

    @pl.when(me == 2)
    def _():
        def scoped(g, back):
            for i in range(4):
                total = moved(near[...], spread_chunk(i))
                for c in range(2):
                    back[i, c] = total[:, c * LANES : (c + 1) * LANES].reshape(20, 8, LANES)
            for c in range(2):
                y, z = cell_of(2, lanes() + c * LANES)
                covered = (y >= Y_LOW) & (y <= Y_HIGH) & (z <= 1)

                def insert(q, c=c, covered=covered):
                    for i in range(4):
                        rows = pl.ds(8 * i, 8)
                        g[q, c, rows, :] = jnp.where(covered, back[i, c, q], result[q, c, rows, :])

                loop(19, insert, 1)
            store_level(2, g, 0, state)

        pl.run_scoped(
            scoped, pltpu.VMEM((19, 2, OWN[2], LANES), F32), pltpu.VMEM((4, 2, 20, 8, LANES), F32)
        )

    @pl.when(me == 1)
    def _():
        def scoped(wide, inner, value):
            lane = lanes()
            deep = deep_late(lane & 63)
            for q in range(19):
                part = pltpu.roll(far[pl.ds(8 * (q // 8), 8), :], (4 - 8 * (q % 8)) % LANES, 1)
                value[pl.ds(8 * q, 8), :] = jnp.where(deep, part, near[pl.ds(8 * q, 8), :])
            value[pl.ds(152, 8), :] = jnp.zeros((8, LANES), F32)
            total = moved(early[...].reshape(19 * 16, LANES), spread_zone_matrix())
            for c in range(4):
                wide[:, c] = total[:, c * LANES : (c + 1) * LANES].reshape(19, 16, LANES)
            for half in range(2):
                total = moved(value[...], late_back_chunk(half))
                for c in range(2):
                    part = total[:, c * LANES : (c + 1) * LANES].reshape(20, 8, LANES)
                    inner[c, :, pl.ds(8 * half, 8), :] = part

            def one(q):
                for j in range(8):
                    c = j % 4
                    y, z = cell_of(1, lanes() + c * LANES)
                    columns = pl.ds(j * LANES, LANES)
                    rows = pl.ds(j // 4, 8, stride=2)
                    value = jnp.where(near_first(y, z), wide[q, c, rows, :], old_state[q, :, columns])
                    if c in (1, 2):
                        value = jnp.where(covered_first(y, z), inner[c - 1, q, rows, :], value)
                    state[q, :, columns] = value

            loop(19, one)

        pl.run_scoped(
            scoped,
            pltpu.VMEM((19, 4, 16, LANES), F32),
            pltpu.VMEM((2, 20, 16, LANES), F32),
            pltpu.VMEM((160, LANES), F32),
        )

    @pl.when(me == 0)
    def _():
        def scoped(value):
            lane = lanes()
            for q in range(19):
                rows = pl.ds(8 * (q // 4), 8)
                part = far[rows, :] + far_coarse[rows, :]
                if q % 4:
                    part = pltpu.roll(part, LANES - 32 * (q % 4), 1)
                value[q] = jnp.where(lane < 32, part, 0.0)
            value[19] = jnp.zeros((8, LANES), F32)
            total = moved(value[...].reshape(160, LANES), mean_back_matrix())
            scale = child_scale(1)
            v = relax(
                [early[q, pl.ds(0, 8), :] + total[8 * q : 8 * q + 8] for q in range(19)],
                1.0 - scale,
                scale,
            )
            for q in range(19):
                value[q] = v[q]
            total = moved(value[...].reshape(160, LANES), spread_covered_matrix())
            for q in range(19):
                for j in range(8):
                    columns = pl.ds(j * LANES, LANES)
                    if not 2 <= j < 6:
                        state[q, :, columns] = old_state[q, :, columns]
                    else:
                        covered = (lane & 31) < 8
                        part = total[8 * q : 8 * q + 8, (j - 2) * LANES : (j - 1) * LANES]
                        state[q, :, columns] = jnp.where(covered, part, old_state[q, :, columns])

        pl.run_scoped(scoped, pltpu.VMEM((20, 8, LANES), F32))


def call(kernel, shapes, args, micros):
    return pl.pallas_call(
        kernel,
        out_shape=[jax.ShapeDtypeStruct(s, F32) for s in shapes],
        in_specs=[pl.BlockSpec(memory_space=pltpu.VMEM)] * len(args),
        out_specs=[pl.BlockSpec(memory_space=pltpu.VMEM)] * len(shapes),
        cost_estimate=pl.CostEstimate(
            flops=int(micros * 1e9), bytes_accessed=int(micros * 3.6e6), transcendentals=0
        ),
        compiler_params=pltpu.CompilerParams(vmem_limit_bytes=24 * 1024 * 1024),
    )(*args)


def shards(populations, solid):
    own, flags = populations[0], solid[0]
    if own.shape != (19, SLAB, NY * NZ):
        raise ValueError("unexpected slab")
    blocks = lax.axis_size("blocks")
    forward = [(i, (i + 1) % blocks) for i in range(blocks)]
    backward = [(i, (i - 1) % blocks) for i in range(blocks)]
    down = [(i, i + 1) for i in range(LEVELS - 1)]

    def diagonal(step):
        return [
            (level * blocks + b, (level + 1) * blocks + (b + step) % blocks)
            for level in range(LEVELS - 1)
            for b in range(blocks)
        ]

    both = ("level", "blocks")
    to_right, to_left, center, zone_right, zone_left = call(
        start_kernel,
        [(20, 16, LANES), (20, 16, LANES), (680, LANES), (20, 8, LANES), (20, 8, LANES)],
        [own, flags],
        1.5,
    )
    center = lax.ppermute(center, "level", down)
    left = lax.ppermute(zone_right, both, diagonal(1))
    right = lax.ppermute(zone_left, both, diagonal(-1))
    low = lax.ppermute(to_right, "blocks", forward)
    high = lax.ppermute(to_left, "blocks", backward)

    full = (19, SLAB, NY * NZ)
    state, fine, fine_post, flows, keep_post, keep_wide, early, ring = call(
        main_kernel,
        [
            full,
            (20, 1, ROWS[3], LANES),
            (19, 64, LANES),
            (144, LANES),
            (20, 2, ROWS[2], LANES),
            (19, 2, ROWS[2], LANES),
            (19, 16, LANES),
            (19, 8, LANES),
        ],
        [own, flags, low, high, center, left, right],
        8.0,
    )
    flows = lax.ppermute(flows, "level", [(3, 2)])
    early = lax.ppermute(early, "level", [(2, 1), (1, 0)])
    third_state, means, far_first, far_coarse = call(
        last_cycle_kernel, [full, (160, LANES), (40, LANES), (40, LANES)], [fine, fine_post], 4.0
    )
    far_coarse = lax.ppermute(far_coarse, "level", [(3, 0)])
    result, late, late_mean = call(
        flow_kernel,
        [(19, 2, OWN[2], LANES), (160, LANES), (40, LANES)],
        [flows, keep_post, keep_wide, ring],
        2.5,
    )
    me = lax.axis_index("level")
    far = lax.ppermute(jnp.where(me == 3, far_first, late_mean), "level", [(3, 1), (2, 0)])
    near = lax.ppermute(jnp.where(me == 3, means, late), "level", [(3, 2), (2, 1)])
    (state,) = call(
        finish_kernel, [full], [state, result, third_state, early, near, far, far_coarse], 1.0
    )
    return state[None]


def solution(mesh):
    in_specs = (P("level", None, "blocks", None), P("level", "blocks", None))
    out_specs = P("level", None, "blocks", None)
    return jax.shard_map(shards, mesh=mesh, in_specs=in_specs, out_specs=out_specs, check_vma=False)
```

```python
import jax
import jax.numpy as jnp
from jax import lax
from jax.experimental import pallas as pl
from jax.experimental.pallas import tpu as pltpu
from jax.sharding import PartitionSpec as P

NY = 32
NZ = 32
LEVELS = 4
SLAB = 8
LANES = 128
VELOCITY = (
    (0, 0, 0),
    (1, 0, 0),
    (-1, 0, 0),
    (0, 1, 0),
    (0, -1, 0),
    (0, 0, 1),
    (0, 0, -1),
    (1, 1, 0),
    (-1, -1, 0),
    (1, -1, 0),
    (-1, 1, 0),
    (1, 0, 1),
    (-1, 0, -1),
    (1, 0, -1),
    (-1, 0, 1),
    (0, 1, 1),
    (0, -1, -1),
    (0, 1, -1),
    (0, -1, 1),
)
OPPOSITE = (0, 2, 1, 4, 3, 6, 5, 8, 7, 10, 9, 12, 11, 14, 13, 16, 15, 18, 17)
TAU_BASE = 1.0
F32 = jnp.float32
BF16 = jnp.bfloat16

PAD = 8
MARGIN = (8, 8, 8, 16)
FACTOR = (1, 2, 4, 8)
CHUNKS = (8, 4, 2, 1)
DEPTH = (32, 16, 8, 4)
OWN = tuple(SLAB * f for f in FACTOR)
ROW0 = tuple(PAD + m for m in MARGIN)
ROWS = tuple(OWN[l] + 2 * ROW0[l] for l in range(LEVELS))

Y_LOW = NY // 4
Y_HIGH = 3 * NY // 4 - 1


def zone_lane(level, y, z):
    if level == 0:
        return (y - 8) * 8 + z
    if level == 1:
        return z * 20 + y - 6
    return z * 25 + y - 4


ZONE_PITCH = (None, 20, 25)


def level_lane(level, y, z):
    return y * DEPTH[level] + z


def made(columns, weight, holds):
    row = lax.broadcasted_iota(jnp.int32, (LANES, columns), 0)
    column = lax.broadcasted_iota(jnp.int32, (LANES, columns), 1)
    matrix = jnp.where(holds(row, column), weight, 0.0).astype(BF16)
    return jnp.concatenate([matrix, matrix], axis=0)


def cell_of(level, lane):
    return lane >> (DEPTH[level].bit_length() - 1), lane & (DEPTH[level] - 1)


def message_cell(level, y, z):
    if level == 0:
        side = (z < 7) & ((y == 8) | (y == 23))
        top = (z == 7) & (y >= 8) & (y <= 23)
        return jnp.where(z == 7, y - 8, 16 + 2 * z + (y == 23).astype(jnp.int32)), side | top
    if level == 1:
        outer = ((y >= 6) & (y <= 8)) | ((y >= 23) & (y <= 25))
        side = (z < 3) & outer
        top = (z >= 3) & (z <= 5) & (y >= 6) & (y <= 25)
        return jnp.where(z >= 3, (z - 3) * 20 + y - 6, 60 + z * 6 + jnp.where(y < 9, y - 6, y - 20)), side | top
    outer = ((y >= 5) & (y <= 8)) | ((y >= 23) & (y <= 26))
    side = (z == 0) & outer
    top = (z >= 1) & (z <= 4) & (y >= 5) & (y <= 26)
    return jnp.where(z >= 1, (z - 1) * 22 + y - 5, 88 + jnp.where(y < 9, y - 5, y - 19)), side | top


def pack_chunk(level, c):
    def holds(row, column):
        y, z = cell_of(level, row + c * LANES)
        lane, sent = message_cell(level, y, z)
        return sent & (column == lane)

    return made(LANES, 1.0, holds)


def flag_chunk(level, c):
    def holds(row, column):
        y, z = cell_of(level, row + c * LANES)
        if level == 0:
            inside = (y >= 8) & (y <= 23) & (z <= 7)
        elif level == 1:
            inside = (y >= 6) & (y <= 25) & (z <= 5)
        else:
            inside = (y >= 5) & (y <= 26) & (z <= 4)
        return inside & (column == zone_lane(level, y, z))

    return made(LANES, 1.0, holds)


def fold_chunk(level, c):
    def holds(row, column):
        y, z = cell_of(level, row + c * LANES)
        lane, sent = message_cell(level, y, z)
        return sent & ((column & (LANES - 1)) == 96 + (lane & 31)) & ((column >> 7) == (lane >> 5))

    return made(3 * LANES, 1.0, holds)


def unpack_matrix(level, k):
    def holds(row, column):
        y, z = zone_cell(level, column & (LANES - 1))
        lane, sent = message_cell(level, y, z)
        folded = (row == 96 + (lane & 31)) & ((lane >> 5) == k)
        own = row == lane
        return sent & (((column < LANES) & own) | ((column >= LANES) & folded))

    return made(2 * LANES, 1.0, holds)


def widen_matrix(child):
    def holds(row, column):
        y, z = cell_of(child, column)
        edge = (y == 0) | (y == NY - 1) | (z == DEPTH[child] - 1)
        return edge & (row == zone_lane(child - 1, 8 + (y >> 1), z >> 1))

    return made(CHUNKS[child] * LANES, 1.0, holds)


def restrict_chunk(child, c):
    def holds(row, column):
        y, z = cell_of(child, row + c * LANES)
        return column == zone_lane(child - 1, 8 + (y >> 1), z >> 1)

    return made(LANES, 0.125, holds)


def compact_chunk(i):
    def holds(row, column):
        y, z = cell_of(3, row)
        return column == 32 * i + (y >> 1) * 2 + (z >> 1)

    return made(LANES, 0.125, holds)


def spread_chunk(i):
    def holds(row, column):
        y, z = cell_of(2, column)
        return (y >= Y_LOW) & (y <= Y_HIGH) & (z <= 1) & (row == 32 * i + (y - Y_LOW) * 2 + z)

    return made(2 * LANES, 1.0, holds)


def near_first(y, z):
    return (y >= Y_LOW - 1) & (y <= Y_HIGH + 1) & (z <= 4)


def mean_chunk(c):
    def holds(row, column):
        y, z = cell_of(1, row + c * LANES)
        return jnp.logical_not(near_first(y, z)) & (column == zone_lane(0, 8 + (y >> 1), z >> 1))

    return made(LANES, 0.125, holds)


def zone_cell(level, lane):
    if level == 0:
        return 8 + (lane >> 3), lane & 7
    pitch, first = ZONE_PITCH[level], 6 if level == 1 else 4
    z = sum((lane >= pitch * k).astype(jnp.int32) for k in range(1, 7))
    return lane - pitch * z + first, z


def covered_first(y, z):
    return (y >= Y_LOW) & (y <= Y_HIGH) & (z <= 3)


def mean_lane(y, z):
    return y - 11 + 10 * z


def mean_ring_matrix():
    def holds(row, column):
        y, z = zone_cell(1, row)
        ring = near_first(y, z) & jnp.logical_not(covered_first(y, z))
        return ring & (column == mean_lane(8 + (y >> 1), z >> 1))

    return made(LANES, 0.125, holds)


def late_chunk(half, c):
    def holds(row, column):
        y, z = cell_of(2, row + c * LANES)
        return column == 64 * half + (z >> 1) * 16 + (y >> 1)

    return made(LANES, 0.125, holds)


def late_back_chunk(half):
    def holds(row, column):
        y, z = cell_of(1, column + LANES)
        return covered_first(y, z) & (row == 64 * half + z * 16 + y - Y_LOW)

    return made(2 * LANES, 1.0, holds)


def deep_late(cell):
    return (cell >= 4) & (cell < 12)


def late_mean_matrix(half, deep):
    def holds(row, column):
        cell = row - 64 * half
        inside = (cell >= 0) & (cell < 64)
        inside = inside & (deep_late(cell) if deep else jnp.logical_not(deep_late(cell)))
        return inside & (column == mean_lane(12 + ((cell & 15) >> 1), cell >> 5))

    return made(LANES, 0.125, holds)


def deep_matrix(odd):
    def holds(row, column):
        i, y = row >> 5, (row & 31) >> 1
        return ((i & 1) == odd) & (column == 64 * (i >> 1) + 4 + (y >> 1))

    return made(LANES, 0.125, holds)


def mean_back_matrix():
    def holds(row, column):
        z = (row >= 10).astype(jnp.int32) + (row >= 20).astype(jnp.int32)
        return (row < 30) & (column == zone_lane(0, row - 10 * z + 11, z))

    return made(LANES, 1.0, holds)


def packed_planes(source, out, width):
    lane = lanes()
    per = LANES // width
    for plane in range(-(-19 // per)):
        total = jnp.zeros((8, LANES), F32)
        for k in range(per):
            q = per * plane + k
            if q < 19:
                part = source[q] if k == 0 else pltpu.roll(source[q], width * k, 1)
                total = jnp.where((lane >= width * k) & (lane < width * (k + 1)), part, total)
        out[pl.ds(8 * plane, 8), :] = total


def late_means(late, deep, value, scratch):
    for half in range(2):
        scratch[...] = moved(late[...], late_mean_matrix(half, deep)).reshape(20, 8, LANES)
        for q in range(19):
            value[q, pl.ds(4 * half, 4), :] = (
                scratch[q, pl.ds(0, 4, stride=2), :] + scratch[q, pl.ds(1, 4, stride=2), :]
            )


def spread_zone_matrix():
    def holds(row, column):
        y, z = cell_of(1, column)
        return near_first(y, z) & (row == zone_lane(1, y, z))

    return made(4 * LANES, 1.0, holds)


def spread_covered_matrix():
    def holds(row, column):
        y, z = cell_of(0, column + 2 * LANES)
        return (z < 8) & (row == zone_lane(0, y, z))

    return made(4 * LANES, 1.0, holds)


Z_OUT = (5, 11, 14, 15, 18)
Y_DOWN = (4, 8, 9, 16, 18)
Y_UP = (3, 7, 10, 15, 17)
FLOW_DIRECTIONS = tuple(sorted(set(Z_OUT + Y_DOWN + Y_UP)))


def flow_mask(q, y, z):
    mask = None
    if q in Z_OUT:
        mask = (z == 1) & (y >= Y_LOW) & (y <= Y_HIGH)
    for group, edge in ((Y_DOWN, Y_LOW), (Y_UP, Y_HIGH)):
        if q in group:
            cells = (y == edge) & (z <= 1)
            mask = cells if mask is None else mask | cells
    return mask


def flow_chunk(q):
    def holds(row, column):
        y, z = cell_of(2, column)
        source = None
        if q in Y_DOWN:
            source = 80 + Y_DOWN.index(q) + 25 * z
        if q in Y_UP:
            source = 85 + Y_UP.index(q) + 25 * z
        if q in Z_OUT:
            over = 16 * Z_OUT.index(q) + y - Y_LOW
            source = over if source is None else jnp.where(z == 1, over, source)
        return flow_mask(q, y, z) & (row == source)

    return made(2 * LANES, 1.0, holds)


def relaxation(level_id):
    return 2.0**level_id * (TAU_BASE - 0.5) + 0.5


def parent_scale(child):
    return relaxation(child) / (2.0 * relaxation(child - 1))


def child_scale(child):
    return 2.0 * relaxation(child - 1) / relaxation(child)


def relax(v, a, b):
    s = [None] + [v[2 * k - 1] + v[2 * k] for k in range(1, 10)]
    d = [None] + [v[2 * k - 1] - v[2 * k] for k in range(1, 10)]
    rho = (
        (1.0 / 3.0) * v[0]
        + (1.0 / 18.0) * (s[1] + s[2] + s[3])
        + (1.0 / 36.0) * ((s[4] + s[5]) + (s[6] + s[7]) + (s[8] + s[9]))
    )
    mx = (1.0 / 18.0) * d[1] + (1.0 / 36.0) * ((d[4] + d[5]) + (d[6] + d[7]))
    my = (1.0 / 18.0) * d[2] + (1.0 / 36.0) * ((d[4] - d[5]) + (d[8] + d[9]))
    mz = (1.0 / 18.0) * d[3] + (1.0 / 36.0) * ((d[6] - d[7]) + (d[8] - d[9]))
    inv = 1.0 / rho
    ux, uy, uz = mx * inv, my * inv, mz * inv
    ra = a * rho
    base = ra - (1.5 * ra) * (ux * ux + uy * uy + uz * uz)
    r45 = 4.5 * ra
    ra3 = 3.0 * ra

    def kept(q):
        return v[q] if b == 1.0 else b * v[q]

    out = [base if b == 0.0 else base + kept(0)]
    cus = (ux, uy, uz, ux + uy, ux - uy, ux + uz, ux - uz, uy + uz, uy - uz)
    for k in range(1, 10):
        cu = cus[k - 1]
        even = base + r45 * (cu * cu)
        odd = ra3 * cu
        plus, minus = even + odd, even - odd
        if b != 0.0:
            plus, minus = plus + kept(2 * k - 1), minus + kept(2 * k)
        out += [plus, minus]
    return out


def collided(v, solid, level):
    inv_tau = 1.0 / relaxation(level)
    relaxed = relax(v, inv_tau, 1.0 - inv_tau)
    flag = solid != 0.0
    return [jnp.where(flag, v[OPPOSITE[q]], relaxed[q]) for q in range(19)]


def lanes():
    return lax.broadcasted_iota(jnp.int32, (8, LANES), 1)


def interface_mask(level, c):
    lane = lanes()
    nz = DEPTH[level]
    mask = (lane & (nz - 1)) == nz - 1
    if c == 0:
        mask = mask | (lane < nz)
    if c == CHUNKS[level] - 1:
        mask = mask | (lane >= LANES - nz)
    return mask


def pulled(post, level, row, c):
    lane = lanes()
    nz, count = DEPTH[level], CHUNKS[level]
    out = []
    for q in range(19):
        cx, cy, cz = VELOCITY[q]
        shift = cy * nz + cz
        value = post[q, c, pl.ds(row - cx, 8), :]
        if shift != 0:
            value = pltpu.roll(value, shift % LANES, 1)
            outside = None
            if cy == 1:
                if c > 0:
                    other = pltpu.roll(post[q, c - 1, pl.ds(row - cx, 8), :], shift, 1)
                    value = jnp.where(lane < shift, other, value)
                else:
                    outside = lane < nz
            if cy == -1:
                if c < count - 1:
                    other = pltpu.roll(post[q, c + 1, pl.ds(row - cx, 8), :], shift % LANES, 1)
                    value = jnp.where(lane >= LANES + shift, other, value)
                else:
                    outside = lane >= LANES - nz
            if cz != 0:
                edge = (lane & (nz - 1)) == (0 if cz == 1 else nz - 1)
                outside = edge if outside is None else outside | edge
            if outside is not None:
                value = jnp.where(outside, post[OPPOSITE[q], c, pl.ds(row, 8), :], value)
        out.append(value)
    return out


def zone_pulled(post, level, row):
    lane = lanes()
    pitch = ZONE_PITCH[level]
    out = []
    for q in range(19):
        cx, cy, cz = VELOCITY[q]
        shift = cz * pitch + cy
        value = post[q, pl.ds(row - cx, 8), :]
        if shift != 0:
            value = pltpu.roll(value, shift % LANES, 1)
            if cz == 1:
                value = jnp.where(lane < pitch, post[OPPOSITE[q], pl.ds(row, 8), :], value)
        out.append(value)
    return out


def zone_masks(level, reach):
    lane = lanes()
    pitch, first = ZONE_PITCH[level], 6 if level == 1 else 4
    top = DEPTH[level] // 4 - 1
    inside = None
    rim = None
    for z in range(top + reach + 1):
        start = z * pitch - first
        row = (lane >= start + Y_LOW - reach) & (lane <= start + Y_HIGH + reach)
        inside = row if inside is None else inside | row
        if z < top:
            row = (lane == start + Y_LOW) | (lane == start + Y_HIGH)
        elif z == top:
            row = (lane >= start + Y_LOW) & (lane <= start + Y_HIGH)
        else:
            continue
        rim = row if rim is None else rim | row
    return inside, rim


def loop(count, body, unroll=None):
    def step(i, carry):
        body(i)
        return carry

    if unroll is None:
        unroll = max(u for u in range(1, 7) if count % u == 0)
    lax.fori_loop(0, count, step, 0, unroll=unroll)


def row_loop(start, count, body):
    loop(count, lambda i: body(pl.multiple_of(start + 8 * i, 8)))


def moved(value, matrix):
    high = value.astype(BF16)
    low = (value - high.astype(F32)).astype(BF16)
    return jnp.dot(jnp.concatenate([high, low], axis=1), matrix, preferred_element_type=F32)


def load_level(level, own, low, high, buf):
    factor, count, row0 = FACTOR[level], CHUNKS[level], ROW0[level]
    n = OWN[level]

    def one(q, source):
        for j in range(8):
            buf[q, j % count, pl.ds(row0 + j // count, 8, stride=factor), :] = source(j)
        if low is not None:
            for c in range(count):
                rows = pl.ds(c, 2 * factor, stride=count) if count > 1 else pl.ds(0, 2 * factor)
                buf[q, c, pl.ds(row0 - 2 * factor, 2 * factor), :] = low[q, rows, :]
                buf[q, c, pl.ds(row0 + n, 2 * factor), :] = high[q, rows, :]

    loop(20, lambda q: one(q, lambda j: own[q, :, pl.ds(j * LANES, LANES)]))


def store_level(level, buf, row0, out):
    factor, count = FACTOR[level], CHUNKS[level]

    def one(q):
        for j in range(8):
            out[q, :, pl.ds(j * LANES, LANES)] = buf[
                q, j % count, pl.ds(row0 + j // count, 8, stride=factor), :
            ]

    loop(19, one)


def collide_rows(level, source, solid, wide, dest, start, groups):
    masks = [interface_mask(level, c) for c in range(CHUNKS[level])]

    def body(row):
        for c in range(CHUNKS[level]):
            v = [source[q, c, pl.ds(row, 8), :] for q in range(19)]
            if wide is not None:
                v = [jnp.where(masks[c], wide[q, c, pl.ds(row, 8), :], v[q]) for q in range(19)]
            post = collided(v, solid[19, c, pl.ds(row, 8), :], level)
            for q in range(19):
                dest[q, c, pl.ds(row, 8), :] = post[q]

    row_loop(start, groups, body)


def pull_rows(level, post, dest, start, groups):
    def body(row):
        for c in range(CHUNKS[level]):
            v = pulled(post, level, row, c)
            for q in range(19):
                dest[q, c, pl.ds(row, 8), :] = v[q]

    row_loop(start, groups, body)


PLANES = 15
CENTER_ROWS = (PLANES + 1) * (OWN[2] + 2)


def load_zone(level, zone, zero_row, center, left, right, start, rows):
    n = OWN[level]

    def scoped(planes):
        planes[...] = jnp.zeros(planes.shape, F32)
        for p in range(PLANES + 1):
            planes[p, pl.ds(zero_row - 1, n + 2), :] = center[pl.ds(p * (OWN[2] + 2), n + 2), :]
            planes[p, pl.ds(zero_row - 7, 8), :] += left[p]
            planes[p, pl.ds(zero_row + n - 1, 8), :] += right[p]
        folded = None
        for k in range(3):
            part = jnp.concatenate([planes[3 * j + k, pl.ds(start, rows), :] for j in range(5)], axis=0)
            total = moved(part, unpack_matrix(level, k))
            for j in range(5):
                zone[3 * j + k, pl.ds(start, rows), :] = total[rows * j : rows * (j + 1), :LANES]
            folded = total[:, LANES:] if folded is None else folded + total[:, LANES:]
        for j in range(4):
            zone[PLANES + j, pl.ds(start, rows), :] = folded[rows * j : rows * (j + 1)]
        zone[19, pl.ds(start, rows), :] = planes[PLANES, pl.ds(start, rows), :]

    pl.run_scoped(scoped, pltpu.VMEM((PLANES + 1, *zone.shape[1:]), F32))


def convert_zone(level, zone, start, groups, rim, out):
    scale = parent_scale(level + 1)

    def body(i):
        row = pl.multiple_of(8 * i, 8)
        v = [zone[q, pl.ds(start + row, 8), :] for q in range(19)]
        v = relax(v, 1.0 - scale, scale)
        for q in range(19):
            out[q, pl.ds(row, 8), :] = v[q] if rim is None else jnp.where(rim, v[q], 0.0)

    loop(groups, body)


def widen(converted, matrix, child, skip, count, wide, spread, first):
    rows = converted.shape[1]
    value = moved(converted[...].reshape(19 * rows, LANES), matrix)
    for c in range(CHUNKS[child]):
        part = value[:, c * LANES : (c + 1) * LANES].reshape(19, rows, LANES)
        if count < rows:
            spread[pl.ds(0, 19)] = part
        for q in range(19):
            t = part[q] if count == rows else spread[q, pl.ds(skip, count), :]
            wide[q, c, pl.ds(first, count, stride=2), :] = t
            wide[q, c, pl.ds(first + 1, count, stride=2), :] = t


def start_kernel(own, to_right, to_left, center, to_zone_right, to_zone_left):
    me = lax.axis_index("level")

    def halo(q, source):
        for j in range(8):
            to_left[q, pl.ds(j, 2, stride=8), :] = source(pl.ds(0, 2), j)
            to_right[q, pl.ds(j, 2, stride=8), :] = source(pl.ds(SLAB - 2, 2), j)

    loop(20, lambda q: halo(q, lambda rows, j: own[q, rows, pl.ds(j * LANES, LANES)]))

    for level in range(3):

        def push(level=level):
            n, row0, count, rows = OWN[level], ROW0[level], CHUNKS[level], ROWS[level]
            span = max(n + 16, 32)

            def scoped(buf, post, packed):
                post[...] = jnp.zeros(post.shape, F32)
                buf[19] = jnp.zeros(buf.shape[1:], F32)
                load_level(level, own, None, None, buf)
                collide_rows(level, buf, buf, None, post, row0, n // 8)
                pull_rows(level, post, buf, row0 - 8, n // 8 + 2)
                def spanned(first, many, c):
                    return buf[pl.ds(first, many), c, pl.ds(row0 - 8, span), :].reshape(many * span, LANES)

                main = folded = flags = None
                for c in range(count):
                    part = moved(spanned(0, PLANES, c), pack_chunk(level, c))
                    main = part if main is None else main + part
                    part = moved(spanned(PLANES, 4, c), fold_chunk(level, c))
                    folded = part if folded is None else folded + part
                    part = moved(spanned(19, 1, c), flag_chunk(level, c))
                    flags = part if flags is None else flags + part
                for p in range(PLANES):
                    j, k = divmod(p, 3)
                    part = main[span * p : span * (p + 1)]
                    if j < 4:
                        part = part + folded[span * j : span * (j + 1), LANES * k : LANES * (k + 1)]
                    packed[p] = part
                packed[PLANES] = flags
                for p in range(PLANES + 1):
                    center[pl.ds(p * (OWN[2] + 2), n + 2), :] = packed[p, pl.ds(7, n + 2), :]
                    to_zone_right[p] = packed[p, pl.ds(n + 1, 8), :]
                    to_zone_left[p] = packed[p, pl.ds(7, 8), :]

            pl.run_scoped(
                scoped,
                pltpu.VMEM((20, count, rows, LANES), F32),
                pltpu.VMEM((19, count, rows, LANES), F32),
                pltpu.VMEM((PLANES + 1, span, LANES), F32),
            )

        pl.when(me == level)(push)


def pack_flows(post, out, row):
    lane = lanes()
    total = jnp.zeros((8, LANES), F32)
    for k, q in enumerate(Z_OUT):
        v = pltpu.roll(post[q], (16 * k - zone_lane(2, 8, 1)) % LANES, 1)
        total = jnp.where((lane >= 16 * k) & (lane < 16 * k + 16), v, total)
    for group, y, base in ((Y_DOWN, 8, 80), (Y_UP, 23, 85)):
        for k, q in enumerate(group):
            lane0 = base + k
            v = pltpu.roll(post[q], (lane0 - zone_lane(2, y, 0)) % LANES, 1)
            total = jnp.where((lane == lane0) | (lane == lane0 + 25), v, total)
    out[pl.ds(pl.multiple_of(row, 8), 8), :] = total


def pull_and_convert(zpost, zone, row, rim, converted):
    scale = parent_scale(3)
    v = zone_pulled(zpost, 2, row)
    if zone is not None:
        for q in range(19):
            zone[q, pl.ds(row, 8), :] = v[q]
    v = relax(v, 1.0 - scale, scale)
    for q in range(19):
        converted[q, pl.ds(pl.multiple_of(row - 8, 8), 8), :] = jnp.where(rim, v[q], 0.0)


def finest_cycle(g, pa, pb, wide, first, groups):
    mask = interface_mask(3, 0)

    def substep(v, row, dest):
        v = [jnp.where(mask, wide[q, 0, pl.ds(row, 8), :], v[q]) for q in range(19)]
        post = collided(v, g[19, 0, pl.ds(row, 8), :], 3)
        for q in range(19):
            dest[q, 0, pl.ds(row, 8), :] = post[q]

    row_loop(first, groups, lambda row: substep([g[q, 0, pl.ds(row, 8), :] for q in range(19)], row, pa))
    row_loop(first, groups, lambda row: substep(pulled(pa, 3, row, 0), row, pb))


def finest_role(own, low, high, center, left, right, g, zpost, flows):
    def scoped(pa, pb, wide, zone, flat, spread, widen3, restrict3):
        widen3[...] = widen_matrix(3)
        restrict3[...] = restrict_chunk(3, 0)
        load_level(3, own, low, high, g)
        load_zone(2, zone, 16, center, left, right, 8, 48)
        covered, rim = zone_masks(2, 0)
        scale = child_scale(3)

        def restrict(i):
            row = pl.multiple_of(8 * i, 8)
            v = relax([spread[q, pl.ds(row, 8), :] for q in range(19)], 1.0 - scale, scale)
            v = [jnp.where(covered, v[q], zone[q, pl.ds(8 + row, 8), :]) for q in range(19)]
            post = collided(v, zone[19, pl.ds(8 + row, 8), :], 2)
            for q in range(19):
                zpost[q, pl.ds(8 + row, 8), :] = post[q]
            return post

        def interface():
            widen(flat, widen3[...], 3, 0, 48, wide, spread, PAD)

        convert_zone(2, zone, 8, 6, rim, flat)
        interface()
        for cycle in range(3):
            first, groups = (PAD, 12) if cycle < 2 else (PAD + 8, 10)

            def step_out(row):
                v = pulled(pb, 3, row, 0)
                for q in range(19):
                    g[q, 0, pl.ds(row, 8), :] = v[q]

            finest_cycle(g, pa, pb, wide, first, groups)
            row_loop(first, groups, step_out)
            for q in range(19):
                flat[q] = g[q, 0, pl.ds(PAD, 48, stride=2), :] + g[q, 0, pl.ds(PAD + 1, 48, stride=2), :]
            spread[...] = moved(flat[...].reshape(19 * 48, LANES), restrict3[...]).reshape(19, 48, LANES)
            loop(6, lambda i: pack_flows(restrict(i), flows, 48 * cycle + 8 * i))
            if cycle < 2:
                row_loop(8, 6, lambda row: pull_and_convert(zpost, zone, row, rim, flat))
                interface()

    rows = ROWS[3]
    pl.run_scoped(
        scoped,
        pltpu.VMEM((19, 1, rows, LANES), F32),
        pltpu.VMEM((19, 1, rows, LANES), F32),
        pltpu.VMEM((19, 1, rows, LANES), F32),
        pltpu.VMEM((20, 64, LANES), F32),
        pltpu.VMEM((19, 48, LANES), F32),
        pltpu.VMEM((19, 48, LANES), F32),
        pltpu.VMEM((2 * LANES, LANES), BF16),
        pltpu.VMEM((2 * LANES, LANES), BF16),
    )


def last_cycle_kernel(g, zpost, state, means, far_first, far_coarse):
    row0, n = ROW0[3], OWN[3]

    @pl.when(lax.axis_index("level") == 3)
    def _():
        def scoped(pa, pb, wide, flat, spread, out, pairs, value, scratch):
            _, rim = zone_masks(2, 0)

            row_loop(8, 6, lambda row: pull_and_convert(zpost, None, row, rim, flat))
            widen(flat, widen_matrix(3), 3, 0, 48, wide, spread, PAD)
            finest_cycle(g, pa, pb, wide, PAD + 8, 10)

            def step_out(row):
                v = pulled(pb, 3, row, 0)
                for q in range(19):
                    out[q, 0, pl.ds(row - row0, 8), :] = v[q]

            row_loop(row0, n // 8, step_out)
            for q in range(19):
                flat[q, pl.ds(0, 32), :] = (
                    out[q, 0, pl.ds(0, 32, stride=2), :] + out[q, 0, pl.ds(1, 32, stride=2), :]
                )
            total = None
            for i in range(4):
                part = jnp.concatenate(
                    [flat[q, pl.ds(8 * i, 8), :] for q in range(19)] + [jnp.zeros((8, LANES), F32)], axis=0
                )
                part = moved(part, compact_chunk(i))
                total = part if total is None else total + part
            scale = child_scale(3)
            v = relax([total[8 * q : 8 * q + 8] for q in range(19)], 1.0 - scale, scale)
            for q in range(19):
                means[pl.ds(8 * q, 8), :] = v[q]
            means[pl.ds(152, 8), :] = jnp.zeros((8, LANES), F32)
            pairs[...] = jnp.zeros(pairs.shape, F32)
            for q in range(19):
                pairs[pl.ds(4 * q, 4), :] = (
                    means[pl.ds(8 * q, 4, stride=2), :] + means[pl.ds(8 * q + 1, 4, stride=2), :]
                )
            for odd in range(2):
                scratch[pl.ds(0, 80), :] = moved(pairs[...], deep_matrix(odd))
                for q in range(19):
                    value[pl.ds(8 * q + 4 * odd, 4), :] = scratch[pl.ds(4 * q, 4), :]
            scale = child_scale(2)
            v = relax([value[pl.ds(8 * q, 8), :] for q in range(19)], 1.0 - scale, scale)
            deep = deep_late(lanes() & 63)
            for q in range(19):
                value[pl.ds(8 * q, 8), :] = jnp.where(deep, v[q], 0.0)
            value[pl.ds(152, 8), :] = jnp.zeros((8, LANES), F32)
            lane = lanes()
            for plane in range(3):
                total = jnp.zeros((8, LANES), F32)
                for k in range(8):
                    q = 8 * plane + k
                    if q < 19:
                        part = pltpu.roll(value[pl.ds(8 * q, 8), :], (8 * k - 4) % LANES, 1)
                        total = jnp.where(((lane & 63) >> 3) == k, part, total)
                far_first[pl.ds(8 * plane, 8), :] = total
            late_means(value, True, flat.at[:, pl.ds(0, 8)], spread.at[pl.ds(0, 20), pl.ds(0, 8)])
            packed_planes([flat[q, pl.ds(0, 8), :] for q in range(19)], far_coarse, 32)
            store_level(3, out, 0, state)

        rows = ROWS[3]
        pl.run_scoped(
            scoped,
            pltpu.VMEM((19, 1, rows, LANES), F32),
            pltpu.VMEM((19, 1, rows, LANES), F32),
            pltpu.VMEM((19, 1, rows, LANES), F32),
            pltpu.VMEM((19, 48, LANES), F32),
            pltpu.VMEM((20, 48, LANES), F32),
            pltpu.VMEM((19, 1, n, LANES), F32),
            pltpu.VMEM((80, LANES), F32),
            pltpu.VMEM((160, LANES), F32),
            pltpu.VMEM((80, LANES), F32),
        )


def restrict_pairs(level, g, first, count, skip, flat):
    flat[...] = jnp.zeros(flat.shape, F32)
    for q in range(19):
        for c in range(CHUNKS[level]):
            flat[q, c, pl.ds(skip, count), :] = (
                g[q, c, pl.ds(first, count, stride=2), :] + g[q, c, pl.ds(first + 1, count, stride=2), :]
            )
    rows = flat.shape[2]
    total = None
    for c in range(CHUNKS[level]):
        part = moved(flat[:, c].reshape(flat.shape[0] * rows, LANES), restrict_chunk(level, c))
        total = part if total is None else total + part
    return total.reshape(flat.shape[0], rows, LANES)


def second_role(own, low, high, center, left, right, keep_post, keep_wide, early, ring):
    level, row0 = 2, ROW0[2]
    first = row0 - 8

    def scoped(g, wide, zone, zpost, conv, spread, flat):
        load_level(level, own, low, high, g)
        load_zone(1, zone, 16, center, left, right, 8, 32)
        covered, rim = zone_masks(1, 0)
        keep_post[19] = g[19]
        convert_zone(1, zone, 8, 4, rim, conv)
        widen(conv, widen_matrix(2), 2, 4, 24, wide, spread, first)
        collide_rows(level, g, g, wide, keep_post, first, 6)
        pull_rows(level, keep_post, g, first, 6)
        collide_rows(level, g, g, wide, keep_post, first, 6)
        pull_rows(level, keep_post, g, first, 6)
        spread[...] = restrict_pairs(level, g, first, 24, 4, flat)
        scale = child_scale(2)

        def restrict(i):
            row = pl.multiple_of(8 * i, 8)
            v = relax([spread[q, pl.ds(row, 8), :] for q in range(19)], 1.0 - scale, scale)
            v = [jnp.where(covered, v[q], zone[q, pl.ds(8 + row, 8), :]) for q in range(19)]
            post = collided(v, zone[19, pl.ds(8 + row, 8), :], 1)
            for q in range(19):
                zpost[q, pl.ds(8 + row, 8), :] = post[q]

        loop(4, restrict)

        def zone_pull(row):
            v = zone_pulled(zpost, 1, row)
            for q in range(19):
                zone[q, pl.ds(row, 8), :] = v[q]

        row_loop(8, 4, zone_pull)
        convert_zone(1, zone, 8, 4, rim, conv)
        widen(conv, widen_matrix(2), 2, 4, 24, keep_wide, spread, first)
        near, _ = zone_masks(1, 1)
        for q in range(19):
            for i in range(2):
                rows = pl.ds(8 * i, 8)
                early[q, rows, :] = jnp.where(near, zone[q, pl.ds(16 + 8 * i, 8), :], 0.0)
        mean = moved(early[...].reshape(19 * 16, LANES), mean_ring_matrix())
        spread[:, pl.ds(0, 16), :] = mean.reshape(19, 16, LANES)
        for q in range(19):
            ring[q] = spread[q, pl.ds(0, 8, stride=2), :] + spread[q, pl.ds(1, 8, stride=2), :]

    pl.run_scoped(
        scoped,
        pltpu.VMEM((20, 2, ROWS[2], LANES), F32),
        pltpu.VMEM((19, 2, ROWS[2], LANES), F32),
        pltpu.VMEM((20, 48, LANES), F32),
        pltpu.VMEM((19, 48, LANES), F32),
        pltpu.VMEM((19, 32, LANES), F32),
        pltpu.VMEM((19, 32, LANES), F32),
        pltpu.VMEM((19, 2, 32, LANES), F32),
    )


def first_role(own, low, high, center, left, right, state, early):
    level, row0, n = 1, ROW0[1], OWN[1]
    first = row0 - 8

    def scoped(g, post, wide, zone, conv, spread, flat):
        load_level(level, own, low, high, g)
        load_zone(0, zone, 12, center, left, right, 8, 16)
        y, z = zone_cell(0, lanes())
        convert_zone(0, zone, 8, 2, (z == 7) | (y == Y_LOW) | (y == Y_HIGH), conv)
        widen(conv, widen_matrix(1), 1, 0, 16, wide, spread, first)
        collide_rows(level, g, g, wide, post, first, 4)
        pull_rows(level, post, g, first, 4)
        collide_rows(level, g, g, wide, post, first, 4)
        pull_rows(level, post, g, row0, n // 8)
        store_level(level, g, row0, state)
        total = None
        for c in range(CHUNKS[1]):
            part = moved(g[pl.ds(0, 19), c, pl.ds(row0, n), :].reshape(19 * n, LANES), mean_chunk(c))
            total = part if total is None else total + part
        flat[...] = total.reshape(19, n, LANES)
        for q in range(19):
            early[q, pl.ds(0, 8), :] = flat[q, pl.ds(0, 8, stride=2), :] + flat[q, pl.ds(1, 8, stride=2), :]

    pl.run_scoped(
        scoped,
        pltpu.VMEM((20, 4, ROWS[1], LANES), F32),
        pltpu.VMEM((19, 4, ROWS[1], LANES), F32),
        pltpu.VMEM((19, 4, ROWS[1], LANES), F32),
        pltpu.VMEM((20, 32, LANES), F32),
        pltpu.VMEM((19, 16, LANES), F32),
        pltpu.VMEM((19, 16, LANES), F32),
        pltpu.VMEM((19, n, LANES), F32),
    )


def coarse_role(own, low, high, state):
    level, row0 = 0, ROW0[0]

    def scoped(g, post):
        load_level(level, own, low, high, g)
        collide_rows(level, g, g, None, post, row0 - 8, 3)
        pull_rows(level, post, g, row0, 1)
        store_level(level, g, row0, state)

    pl.run_scoped(
        scoped,
        pltpu.VMEM((20, 8, ROWS[0], LANES), F32),
        pltpu.VMEM((19, 8, ROWS[0], LANES), F32),
    )


def main_kernel(
    own, low, high, center, left, right,
    state, fine, fine_post, flows, keep_post, keep_wide, early, ring,
):
    me = lax.axis_index("level")
    arrived = (own, low, high, center, left, right)

    @pl.when(me == 3)
    def _():
        finest_role(*arrived, fine, fine_post, flows)

    @pl.when(me == 2)
    def _():
        second_role(*arrived, keep_post, keep_wide, early, ring)

    @pl.when(me == 1)
    def _():
        first_role(*arrived, state, early)

    @pl.when(me == 0)
    def _():
        coarse_role(own, low, high, state)


def flow_kernel(flows, keep_post, keep_wide, ring, result, late, late_mean):
    level, row0 = 2, ROW0[2]
    first = row0 - 8

    @pl.when(lax.axis_index("level") == 2)
    def _():
        def scoped(g, post, override, flat, value, scratch):
            for k, q in enumerate(FLOW_DIRECTIONS):
                total = moved(flows[...], flow_chunk(q))
                for c in range(2):
                    override[k, c] = total[:, c * LANES : (c + 1) * LANES]

            def overridden(c, row, cycle, v):
                y, z = cell_of(2, lanes() + c * LANES)
                v = list(v)
                for k, q in enumerate(FLOW_DIRECTIONS):
                    value = override[k, c, pl.ds(48 * cycle + row - first, 8), :]
                    v[q] = jnp.where(flow_mask(q, y, z), value, v[q])
                return v

            masks = [interface_mask(level, c) for c in range(2)]

            def begin(row):
                for c in range(2):
                    v = overridden(c, row, 0, [keep_post[q, c, pl.ds(row, 8), :] for q in range(19)])
                    for q in range(19):
                        post[q, c, pl.ds(row, 8), :] = v[q]

            row_loop(first, 6, begin)
            for cycle in (1, 2):
                pull_rows(level, post, g, first, 6)

                def body(row, cycle=cycle):
                    for c in range(2):
                        v = [
                            jnp.where(masks[c], keep_wide[q, c, pl.ds(row, 8), :], g[q, c, pl.ds(row, 8), :])
                            for q in range(19)
                        ]
                        v = collided(v, keep_post[19, c, pl.ds(row, 8), :], level)
                        v = overridden(c, row, cycle, v)
                        for q in range(19):
                            post[q, c, pl.ds(row, 8), :] = v[q]

                row_loop(first, 6, body)

            def last(row):
                for c in range(2):
                    v = pulled(post, level, row, c)
                    for q in range(19):
                        result[q, c, pl.ds(row - row0, 8), :] = v[q]

            row_loop(row0, 4, last)
            for q in range(19):
                for c in range(2):
                    flat[c, q] = result[q, c, pl.ds(0, 16, stride=2), :] + result[q, c, pl.ds(1, 16, stride=2), :]
            flat[:, 19] = jnp.zeros((2, 16, LANES), F32)
            total = None
            for half in range(2):
                for c in range(2):
                    part = moved(flat[c, :, pl.ds(8 * half, 8), :].reshape(160, LANES), late_chunk(half, c))
                    total = part if total is None else total + part
            scale = child_scale(2)
            v = relax([total[8 * q : 8 * q + 8] for q in range(19)], 1.0 - scale, scale)
            for q in range(19):
                late[pl.ds(8 * q, 8), :] = v[q]
            late[pl.ds(152, 8), :] = jnp.zeros((8, LANES), F32)
            late_means(late, False, value, scratch)
            packed_planes([value[q] + ring[q] for q in range(19)], late_mean, 32)

        pl.run_scoped(
            scoped,
            pltpu.VMEM((19, 2, ROWS[2], LANES), F32),
            pltpu.VMEM((19, 2, ROWS[2], LANES), F32),
            pltpu.VMEM((len(FLOW_DIRECTIONS), 2, 144, LANES), F32),
            pltpu.VMEM((2, 20, 16, LANES), F32),
            pltpu.VMEM((19, 8, LANES), F32),
            pltpu.VMEM((20, 8, LANES), F32),
        )


def finish_kernel(old_state, result, third_state, means, early, late, far, far_coarse, state):
    me = lax.axis_index("level")

    @pl.when(me == 3)
    def _():
        state[...] = third_state[...]

    @pl.when(me == 2)
    def _():
        def scoped(g, back):
            for i in range(4):
                total = moved(means[...], spread_chunk(i))
                for c in range(2):
                    back[i, c] = total[:, c * LANES : (c + 1) * LANES].reshape(20, 8, LANES)
            for c in range(2):
                y, z = cell_of(2, lanes() + c * LANES)
                covered = (y >= Y_LOW) & (y <= Y_HIGH) & (z <= 1)

                def insert(q, c=c, covered=covered):
                    for i in range(4):
                        rows = pl.ds(8 * i, 8)
                        g[q, c, rows, :] = jnp.where(covered, back[i, c, q], result[q, c, rows, :])

                loop(19, insert, 1)
            store_level(2, g, 0, state)

        pl.run_scoped(
            scoped, pltpu.VMEM((19, 2, OWN[2], LANES), F32), pltpu.VMEM((4, 2, 20, 8, LANES), F32)
        )

    @pl.when(me == 1)
    def _():
        def scoped(wide, inner, value):
            lane = lanes()
            deep = deep_late(lane & 63)
            for q in range(19):
                part = pltpu.roll(far[pl.ds(8 * (q // 8), 8), :], (4 - 8 * (q % 8)) % LANES, 1)
                value[pl.ds(8 * q, 8), :] = jnp.where(deep, part, late[pl.ds(8 * q, 8), :])
            value[pl.ds(152, 8), :] = jnp.zeros((8, LANES), F32)
            total = moved(early[...].reshape(19 * 16, LANES), spread_zone_matrix())
            for c in range(4):
                wide[:, c] = total[:, c * LANES : (c + 1) * LANES].reshape(19, 16, LANES)
            for half in range(2):
                total = moved(value[...], late_back_chunk(half))
                for c in range(2):
                    part = total[:, c * LANES : (c + 1) * LANES].reshape(20, 8, LANES)
                    inner[c, :, pl.ds(8 * half, 8), :] = part

            def one(q):
                for j in range(8):
                    c = j % 4
                    y, z = cell_of(1, lanes() + c * LANES)
                    columns = pl.ds(j * LANES, LANES)
                    rows = pl.ds(j // 4, 8, stride=2)
                    value = jnp.where(near_first(y, z), wide[q, c, rows, :], old_state[q, :, columns])
                    if c in (1, 2):
                        value = jnp.where(covered_first(y, z), inner[c - 1, q, rows, :], value)
                    state[q, :, columns] = value

            loop(19, one)

        pl.run_scoped(
            scoped,
            pltpu.VMEM((19, 4, 16, LANES), F32),
            pltpu.VMEM((2, 20, 16, LANES), F32),
            pltpu.VMEM((160, LANES), F32),
        )

    @pl.when(me == 0)
    def _():
        def scoped(value):
            lane = lanes()
            for q in range(19):
                rows = pl.ds(8 * (q // 4), 8)
                part = far[rows, :] + far_coarse[rows, :]
                if q % 4:
                    part = pltpu.roll(part, LANES - 32 * (q % 4), 1)
                value[q] = jnp.where(lane < 32, part, 0.0)
            value[19] = jnp.zeros((8, LANES), F32)
            total = moved(value[...].reshape(160, LANES), mean_back_matrix())
            scale = child_scale(1)
            v = relax(
                [early[q, pl.ds(0, 8), :] + total[8 * q : 8 * q + 8] for q in range(19)],
                1.0 - scale,
                scale,
            )
            for q in range(19):
                value[q] = v[q]
            total = moved(value[...].reshape(160, LANES), spread_covered_matrix())
            for q in range(19):
                for j in range(8):
                    columns = pl.ds(j * LANES, LANES)
                    if not 2 <= j < 6:
                        state[q, :, columns] = old_state[q, :, columns]
                    else:
                        covered = (lane & 31) < 8
                        part = total[8 * q : 8 * q + 8, (j - 2) * LANES : (j - 1) * LANES]
                        state[q, :, columns] = jnp.where(covered, part, old_state[q, :, columns])

        pl.run_scoped(scoped, pltpu.VMEM((20, 8, LANES), F32))


def call(kernel, shapes, args, micros):
    return pl.pallas_call(
        kernel,
        out_shape=[jax.ShapeDtypeStruct(s, F32) for s in shapes],
        in_specs=[pl.BlockSpec(memory_space=pltpu.VMEM)] * len(args),
        out_specs=[pl.BlockSpec(memory_space=pltpu.VMEM)] * len(shapes),
        cost_estimate=pl.CostEstimate(
            flops=int(micros * 1e9), bytes_accessed=int(micros * 3.6e6), transcendentals=0
        ),
        compiler_params=pltpu.CompilerParams(vmem_limit_bytes=24 * 1024 * 1024),
    )(*args)


def shards(populations, solid):
    if populations.shape[1:] != (19, SLAB, NY * NZ):
        raise ValueError("unexpected slab")
    own = jnp.concatenate([populations[0], solid.astype(F32)], axis=0)
    blocks = lax.axis_size("blocks")
    forward = [(i, (i + 1) % blocks) for i in range(blocks)]
    backward = [(i, (i - 1) % blocks) for i in range(blocks)]
    down = [(i, i + 1) for i in range(LEVELS - 1)]

    def diagonal(step):
        return [
            (level * blocks + b, (level + 1) * blocks + (b + step) % blocks)
            for level in range(LEVELS - 1)
            for b in range(blocks)
        ]

    both = ("level", "blocks")
    to_right, to_left, center, zone_right, zone_left = call(
        start_kernel,
        [(20, 16, LANES), (20, 16, LANES), (CENTER_ROWS, LANES), (PLANES + 1, 8, LANES), (PLANES + 1, 8, LANES)],
        [own],
        1.5,
    )
    center = lax.ppermute(center, "level", down)
    left = lax.ppermute(zone_right, both, diagonal(1))
    right = lax.ppermute(zone_left, both, diagonal(-1))
    low = lax.ppermute(to_right, "blocks", forward)
    high = lax.ppermute(to_left, "blocks", backward)

    full = (19, SLAB, NY * NZ)
    state, fine, fine_post, flows, keep_post, keep_wide, early, ring = call(
        main_kernel,
        [
            full,
            (20, 1, ROWS[3], LANES),
            (19, 64, LANES),
            (144, LANES),
            (20, 2, ROWS[2], LANES),
            (19, 2, ROWS[2], LANES),
            (19, 16, LANES),
            (19, 8, LANES),
        ],
        [own, low, high, center, left, right],
        8.0,
    )
    flows = lax.ppermute(flows, "level", [(3, 2)])
    early = lax.ppermute(early, "level", [(2, 1), (1, 0)])
    third_state, means, far_first, far_coarse = call(
        last_cycle_kernel, [full, (160, LANES), (40, LANES), (40, LANES)], [fine, fine_post], 4.0
    )
    far_coarse = lax.ppermute(far_coarse, "level", [(3, 0)])
    means = lax.ppermute(means, "level", [(3, 2)])
    result, late, late_mean = call(
        flow_kernel,
        [(19, 2, OWN[2], LANES), (160, LANES), (40, LANES)],
        [flows, keep_post, keep_wide, ring],
        2.5,
    )
    me = lax.axis_index("level")
    far = lax.ppermute(jnp.where(me == 3, far_first, late_mean), "level", [(3, 1), (2, 0)])
    late = lax.ppermute(late, "level", [(2, 1)])
    (state,) = call(
        finish_kernel, [full], [state, result, third_state, means, early, late, far, far_coarse], 1.0
    )
    return state[None]


def solution(mesh):
    in_specs = (P("level", None, "blocks", None), P("level", "blocks", None))
    out_specs = P("level", None, "blocks", None)
    return jax.shard_map(shards, mesh=mesh, in_specs=in_specs, out_specs=out_specs, check_vma=False)
```

```python
import jax
import jax.numpy as jnp
from jax import lax
from jax.experimental import pallas as pl
from jax.experimental.pallas import tpu as pltpu
from jax.sharding import PartitionSpec as P

NY = 32
NZ = 32
LEVELS = 4
SLAB = 8
LANES = 128
VELOCITY = (
    (0, 0, 0),
    (1, 0, 0),
    (-1, 0, 0),
    (0, 1, 0),
    (0, -1, 0),
    (0, 0, 1),
    (0, 0, -1),
    (1, 1, 0),
    (-1, -1, 0),
    (1, -1, 0),
    (-1, 1, 0),
    (1, 0, 1),
    (-1, 0, -1),
    (1, 0, -1),
    (-1, 0, 1),
    (0, 1, 1),
    (0, -1, -1),
    (0, 1, -1),
    (0, -1, 1),
)
OPPOSITE = (0, 2, 1, 4, 3, 6, 5, 8, 7, 10, 9, 12, 11, 14, 13, 16, 15, 18, 17)
TAU_BASE = 1.0
F32 = jnp.float32
BF16 = jnp.bfloat16

PAD = 8
MARGIN = (8, 8, 8, 16)
FACTOR = (1, 2, 4, 8)
CHUNKS = (8, 4, 2, 1)
DEPTH = (32, 16, 8, 4)
OWN = tuple(SLAB * f for f in FACTOR)
ROW0 = tuple(PAD + m for m in MARGIN)
ROWS = tuple(OWN[l] + 2 * ROW0[l] for l in range(LEVELS))

Y_LOW = NY // 4
Y_HIGH = 3 * NY // 4 - 1


def zone_lane(level, y, z):
    if level == 0:
        return (y - 8) * 8 + z
    if level == 1:
        return z * 20 + y - 6
    return z * 25 + y - 4


ZONE_PITCH = (None, 20, 25)


def level_lane(level, y, z):
    return y * DEPTH[level] + z


def made(columns, weight, holds):
    row = lax.broadcasted_iota(jnp.int32, (LANES, columns), 0)
    column = lax.broadcasted_iota(jnp.int32, (LANES, columns), 1)
    matrix = jnp.where(holds(row, column), weight, 0.0).astype(BF16)
    return jnp.concatenate([matrix, matrix], axis=0)


def cell_of(level, lane):
    return lane >> (DEPTH[level].bit_length() - 1), lane & (DEPTH[level] - 1)


def message_cell(level, y, z):
    if level == 0:
        side = (z < 7) & ((y == 8) | (y == 23))
        top = (z == 7) & (y >= 8) & (y <= 23)
        return jnp.where(z == 7, y - 8, 16 + 2 * z + (y == 23).astype(jnp.int32)), side | top
    if level == 1:
        outer = ((y >= 6) & (y <= 8)) | ((y >= 23) & (y <= 25))
        side = (z < 3) & outer
        top = (z >= 3) & (z <= 5) & (y >= 6) & (y <= 25)
        return jnp.where(z >= 3, (z - 3) * 20 + y - 6, 60 + z * 6 + jnp.where(y < 9, y - 6, y - 20)), side | top
    outer = ((y >= 5) & (y <= 8)) | ((y >= 23) & (y <= 26))
    side = (z == 0) & outer
    top = (z >= 1) & (z <= 4) & (y >= 5) & (y <= 26)
    return jnp.where(z >= 1, (z - 1) * 22 + y - 5, 88 + jnp.where(y < 9, y - 5, y - 19)), side | top


def pack_chunk(level, c):
    def holds(row, column):
        y, z = cell_of(level, row + c * LANES)
        lane, sent = message_cell(level, y, z)
        return sent & (column == lane)

    return made(LANES, 1.0, holds)


def flag_chunk(level, c):
    def holds(row, column):
        y, z = cell_of(level, row + c * LANES)
        if level == 0:
            inside = (y >= 8) & (y <= 23) & (z <= 7)
        elif level == 1:
            inside = (y >= 6) & (y <= 25) & (z <= 5)
        else:
            inside = (y >= 5) & (y <= 26) & (z <= 4)
        return inside & (column == zone_lane(level, y, z))

    return made(LANES, 1.0, holds)


def fold_chunk(level, c):
    def holds(row, column):
        y, z = cell_of(level, row + c * LANES)
        lane, sent = message_cell(level, y, z)
        return sent & ((column & (LANES - 1)) == 96 + (lane & 31)) & ((column >> 7) == (lane >> 5))

    return made(3 * LANES, 1.0, holds)


def unpack_matrix(level, k):
    def holds(row, column):
        y, z = zone_cell(level, column & (LANES - 1))
        lane, sent = message_cell(level, y, z)
        folded = (row == 96 + (lane & 31)) & ((lane >> 5) == k)
        own = row == lane
        return sent & (((column < LANES) & own) | ((column >= LANES) & folded))

    return made(2 * LANES, 1.0, holds)


def widen_matrix(child):
    def holds(row, column):
        y, z = cell_of(child, column)
        edge = (y == 0) | (y == NY - 1) | (z == DEPTH[child] - 1)
        return edge & (row == zone_lane(child - 1, 8 + (y >> 1), z >> 1))

    return made(CHUNKS[child] * LANES, 1.0, holds)


def restrict_chunk(child, c):
    def holds(row, column):
        y, z = cell_of(child, row + c * LANES)
        return column == zone_lane(child - 1, 8 + (y >> 1), z >> 1)

    return made(LANES, 0.125, holds)


def compact_chunk(i):
    def holds(row, column):
        y, z = cell_of(3, row)
        return column == 32 * i + (y >> 1) * 2 + (z >> 1)

    return made(LANES, 0.125, holds)


def spread_chunk(i):
    def holds(row, column):
        y, z = cell_of(2, column)
        return (y >= Y_LOW) & (y <= Y_HIGH) & (z <= 1) & (row == 32 * i + (y - Y_LOW) * 2 + z)

    return made(2 * LANES, 1.0, holds)


def near_first(y, z):
    return (y >= Y_LOW - 1) & (y <= Y_HIGH + 1) & (z <= 4)


def mean_chunk(c):
    def holds(row, column):
        y, z = cell_of(1, row + c * LANES)
        return jnp.logical_not(near_first(y, z)) & (column == zone_lane(0, 8 + (y >> 1), z >> 1))

    return made(LANES, 0.125, holds)


def zone_cell(level, lane):
    if level == 0:
        return 8 + (lane >> 3), lane & 7
    pitch, first = ZONE_PITCH[level], 6 if level == 1 else 4
    z = sum((lane >= pitch * k).astype(jnp.int32) for k in range(1, 7))
    return lane - pitch * z + first, z


def covered_first(y, z):
    return (y >= Y_LOW) & (y <= Y_HIGH) & (z <= 3)


def mean_lane(y, z):
    return y - 11 + 10 * z


def mean_ring_matrix():
    def holds(row, column):
        y, z = zone_cell(1, row)
        ring = near_first(y, z) & jnp.logical_not(covered_first(y, z))
        return ring & (column == mean_lane(8 + (y >> 1), z >> 1))

    return made(LANES, 0.125, holds)


def late_chunk(half, c):
    def holds(row, column):
        y, z = cell_of(2, row + c * LANES)
        return column == 64 * half + (z >> 1) * 16 + (y >> 1)

    return made(LANES, 0.125, holds)


def late_back_chunk(half):
    def holds(row, column):
        y, z = cell_of(1, column + LANES)
        return covered_first(y, z) & (row == 64 * half + z * 16 + y - Y_LOW)

    return made(2 * LANES, 1.0, holds)


def deep_late(cell):
    return (cell >= 4) & (cell < 12)


def late_mean_matrix(half, deep):
    def holds(row, column):
        cell = row - 64 * half
        inside = (cell >= 0) & (cell < 64)
        inside = inside & (deep_late(cell) if deep else jnp.logical_not(deep_late(cell)))
        return inside & (column == mean_lane(12 + ((cell & 15) >> 1), cell >> 5))

    return made(LANES, 0.125, holds)


def deep_matrix(odd):
    def holds(row, column):
        i, y = row >> 5, (row & 31) >> 1
        return ((i & 1) == odd) & (column == 64 * (i >> 1) + 4 + (y >> 1))

    return made(LANES, 0.125, holds)


def mean_back_matrix():
    def holds(row, column):
        z = (row >= 10).astype(jnp.int32) + (row >= 20).astype(jnp.int32)
        return (row < 30) & (column == zone_lane(0, row - 10 * z + 11, z))

    return made(LANES, 1.0, holds)


def packed_planes(source, out, width):
    lane = lanes()
    per = LANES // width
    for plane in range(-(-19 // per)):
        total = jnp.zeros((8, LANES), F32)
        for k in range(per):
            q = per * plane + k
            if q < 19:
                part = source[q] if k == 0 else pltpu.roll(source[q], width * k, 1)
                total = jnp.where((lane >= width * k) & (lane < width * (k + 1)), part, total)
        out[pl.ds(8 * plane, 8), :] = total


def late_means(late, deep, value, scratch):
    for half in range(2):
        scratch[...] = moved(late[...], late_mean_matrix(half, deep)).reshape(20, 8, LANES)
        for q in range(19):
            value[q, pl.ds(4 * half, 4), :] = (
                scratch[q, pl.ds(0, 4, stride=2), :] + scratch[q, pl.ds(1, 4, stride=2), :]
            )


def spread_zone_matrix():
    def holds(row, column):
        y, z = cell_of(1, column)
        return near_first(y, z) & (row == zone_lane(1, y, z))

    return made(4 * LANES, 1.0, holds)


def spread_covered_matrix():
    def holds(row, column):
        y, z = cell_of(0, column + 2 * LANES)
        return (z < 8) & (row == zone_lane(0, y, z))

    return made(4 * LANES, 1.0, holds)


Z_OUT = (5, 11, 14, 15, 18)
Y_DOWN = (4, 8, 9, 16, 18)
Y_UP = (3, 7, 10, 15, 17)
FLOW_DIRECTIONS = tuple(sorted(set(Z_OUT + Y_DOWN + Y_UP)))


def flow_mask(q, y, z):
    mask = None
    if q in Z_OUT:
        mask = (z == 1) & (y >= Y_LOW) & (y <= Y_HIGH)
    for group, edge in ((Y_DOWN, Y_LOW), (Y_UP, Y_HIGH)):
        if q in group:
            cells = (y == edge) & (z <= 1)
            mask = cells if mask is None else mask | cells
    return mask


FLOW_CHUNKS = tuple(
    (q, c) for q in FLOW_DIRECTIONS for c in range(2) if q in Z_OUT or q in (Y_DOWN, Y_UP)[c]
)


def flow_chunk(q, c):
    def holds(row, column):
        y, z = cell_of(2, column + c * LANES)
        source = None
        if q in Y_DOWN:
            source = 80 + Y_DOWN.index(q) + 25 * z
        if q in Y_UP:
            source = 85 + Y_UP.index(q) + 25 * z
        if q in Z_OUT:
            over = 16 * Z_OUT.index(q) + y - Y_LOW
            source = over if source is None else jnp.where(z == 1, over, source)
        return flow_mask(q, y, z) & (row == source)

    return made(LANES, 1.0, holds)


def relaxation(level_id):
    return 2.0**level_id * (TAU_BASE - 0.5) + 0.5


def parent_scale(child):
    return relaxation(child) / (2.0 * relaxation(child - 1))


def child_scale(child):
    return 2.0 * relaxation(child - 1) / relaxation(child)


def relax(v, a, b):
    s = [None] + [v[2 * k - 1] + v[2 * k] for k in range(1, 10)]
    d = [None] + [v[2 * k - 1] - v[2 * k] for k in range(1, 10)]
    rho = (
        (1.0 / 3.0) * v[0]
        + (1.0 / 18.0) * (s[1] + s[2] + s[3])
        + (1.0 / 36.0) * ((s[4] + s[5]) + (s[6] + s[7]) + (s[8] + s[9]))
    )
    mx = (1.0 / 18.0) * d[1] + (1.0 / 36.0) * ((d[4] + d[5]) + (d[6] + d[7]))
    my = (1.0 / 18.0) * d[2] + (1.0 / 36.0) * ((d[4] - d[5]) + (d[8] + d[9]))
    mz = (1.0 / 18.0) * d[3] + (1.0 / 36.0) * ((d[6] - d[7]) + (d[8] - d[9]))
    inv = 1.0 / rho
    ux, uy, uz = mx * inv, my * inv, mz * inv
    ra = a * rho
    base = ra - (1.5 * ra) * (ux * ux + uy * uy + uz * uz)
    r45 = 4.5 * ra
    ra3 = 3.0 * ra

    def kept(q):
        return v[q] if b == 1.0 else b * v[q]

    out = [base if b == 0.0 else base + kept(0)]
    cus = (ux, uy, uz, ux + uy, ux - uy, ux + uz, ux - uz, uy + uz, uy - uz)
    for k in range(1, 10):
        cu = cus[k - 1]
        even = base + r45 * (cu * cu)
        odd = ra3 * cu
        plus, minus = even + odd, even - odd
        if b != 0.0:
            plus, minus = plus + kept(2 * k - 1), minus + kept(2 * k)
        out += [plus, minus]
    return out


def collided(v, solid, level):
    inv_tau = 1.0 / relaxation(level)
    relaxed = relax(v, inv_tau, 1.0 - inv_tau)
    flag = solid != 0.0
    return [jnp.where(flag, v[OPPOSITE[q]], relaxed[q]) for q in range(19)]


def lanes():
    return lax.broadcasted_iota(jnp.int32, (8, LANES), 1)


def interface_mask(level, c):
    lane = lanes()
    nz = DEPTH[level]
    mask = (lane & (nz - 1)) == nz - 1
    if c == 0:
        mask = mask | (lane < nz)
    if c == CHUNKS[level] - 1:
        mask = mask | (lane >= LANES - nz)
    return mask


def pulled(post, level, row, chunks, interface_next=False):
    lane = lanes()
    nz, count = DEPTH[level], CHUNKS[level]
    out = [[] for _ in chunks]
    for q in range(19):
        cx, cy, cz = VELOCITY[q]
        shift = cy * nz + cz
        rolled = {}

        def moved_chunk(c):
            if c not in rolled:
                value = post[q, c, pl.ds(row - cx, 8), :]
                rolled[c] = pltpu.roll(value, shift % LANES, 1) if shift != 0 else value
            return rolled[c]

        for place, c in enumerate(chunks):
            value = moved_chunk(c)
            outside = None
            if cy == 1:
                if c > 0:
                    value = jnp.where(lane < shift, moved_chunk(c - 1), value)
                else:
                    outside = lane < nz
            if cy == -1:
                if c < count - 1:
                    value = jnp.where(lane >= LANES + shift, moved_chunk(c + 1), value)
                else:
                    outside = lane >= LANES - nz
            if cz != 0:
                edge = (lane & (nz - 1)) == (0 if cz == 1 else nz - 1)
                outside = edge if outside is None else outside | edge
            if interface_next:
                outside = (lane & (nz - 1)) == 0 if cz == 1 else None
            if outside is not None:
                value = jnp.where(outside, post[OPPOSITE[q], c, pl.ds(row, 8), :], value)
            out[place].append(value)
    return out


def zone_pulled(post, level, row):
    lane = lanes()
    pitch = ZONE_PITCH[level]
    out = []
    for q in range(19):
        cx, cy, cz = VELOCITY[q]
        shift = cz * pitch + cy
        value = post[q, pl.ds(row - cx, 8), :]
        if shift != 0:
            value = pltpu.roll(value, shift % LANES, 1)
            if cz == 1:
                value = jnp.where(lane < pitch, post[OPPOSITE[q], pl.ds(row, 8), :], value)
        out.append(value)
    return out


def zone_masks(level, reach):
    lane = lanes()
    pitch, first = ZONE_PITCH[level], 6 if level == 1 else 4
    top = DEPTH[level] // 4 - 1
    inside = None
    rim = None
    for z in range(top + reach + 1):
        start = z * pitch - first
        row = (lane >= start + Y_LOW - reach) & (lane <= start + Y_HIGH + reach)
        inside = row if inside is None else inside | row
        if z < top:
            row = (lane == start + Y_LOW) | (lane == start + Y_HIGH)
        elif z == top:
            row = (lane >= start + Y_LOW) & (lane <= start + Y_HIGH)
        else:
            continue
        rim = row if rim is None else rim | row
    return inside, rim


def loop(count, body, unroll=None):
    def step(i, carry):
        body(i)
        return carry

    if unroll is None:
        unroll = max(u for u in range(1, 7) if count % u == 0)
    lax.fori_loop(0, count, step, 0, unroll=unroll)


def row_loop(start, count, body):
    loop(count, lambda i: body(pl.multiple_of(start + 8 * i, 8)))


def moved(value, matrix):
    high = value.astype(BF16)
    low = (value - high.astype(F32)).astype(BF16)
    return jnp.dot(jnp.concatenate([high, low], axis=1), matrix, preferred_element_type=F32)


def load_level(level, own, low, high, buf):
    factor, count, row0 = FACTOR[level], CHUNKS[level], ROW0[level]
    n = OWN[level]

    def one(q, source):
        for j in range(8):
            buf[q, j % count, pl.ds(row0 + j // count, 8, stride=factor), :] = source(j)
        if low is not None:
            for c in range(count):
                rows = pl.ds(c, 2 * factor, stride=count) if count > 1 else pl.ds(0, 2 * factor)
                buf[q, c, pl.ds(row0 - 2 * factor, 2 * factor), :] = low[q, rows, :]
                buf[q, c, pl.ds(row0 + n, 2 * factor), :] = high[q, rows, :]

    loop(20, lambda q: one(q, lambda j: own[q, :, pl.ds(j * LANES, LANES)]))


def store_level(level, buf, row0, out):
    factor, count = FACTOR[level], CHUNKS[level]

    def one(q):
        for j in range(8):
            out[q, :, pl.ds(j * LANES, LANES)] = buf[
                q, j % count, pl.ds(row0 + j // count, 8, stride=factor), :
            ]

    loop(19, one)


def collide_rows(level, source, solid, wide, dest, start, groups):
    masks = [interface_mask(level, c) for c in range(CHUNKS[level])]

    def body(row):
        for c in range(CHUNKS[level]):
            v = [source[q, c, pl.ds(row, 8), :] for q in range(19)]
            if wide is not None:
                v = [jnp.where(masks[c], wide[q, c, pl.ds(row, 8), :], v[q]) for q in range(19)]
            post = collided(v, solid[19, c, pl.ds(row, 8), :], level)
            for q in range(19):
                dest[q, c, pl.ds(row, 8), :] = post[q]

    row_loop(start, groups, body)


def pull_rows(level, post, dest, start, groups):
    def body(row):
        step = min(2, CHUNKS[level])
        for first in range(0, CHUNKS[level], step):
            chunks = range(first, first + step)
            for c, v in zip(chunks, pulled(post, level, row, chunks)):
                for q in range(19):
                    dest[q, c, pl.ds(row, 8), :] = v[q]

    row_loop(start, groups, body)


PLANES = 15
CENTER_ROWS = (PLANES + 1) * (OWN[2] + 2)


def load_zone(level, zone, zero_row, center, left, right, start, rows):
    n = OWN[level]

    def scoped(planes):
        planes[...] = jnp.zeros(planes.shape, F32)
        for p in range(PLANES + 1):
            planes[p, pl.ds(zero_row - 1, n + 2), :] = center[pl.ds(p * (OWN[2] + 2), n + 2), :]
            planes[p, pl.ds(zero_row - 7, 8), :] += left[p]
            planes[p, pl.ds(zero_row + n - 1, 8), :] += right[p]
        folded = None
        for k in range(3):
            part = jnp.concatenate([planes[3 * j + k, pl.ds(start, rows), :] for j in range(5)], axis=0)
            total = moved(part, unpack_matrix(level, k))
            for j in range(5):
                zone[3 * j + k, pl.ds(start, rows), :] = total[rows * j : rows * (j + 1), :LANES]
            folded = total[:, LANES:] if folded is None else folded + total[:, LANES:]
        for j in range(4):
            zone[PLANES + j, pl.ds(start, rows), :] = folded[rows * j : rows * (j + 1)]
        zone[19, pl.ds(start, rows), :] = planes[PLANES, pl.ds(start, rows), :]

    pl.run_scoped(scoped, pltpu.VMEM((PLANES + 1, *zone.shape[1:]), F32))


def convert_zone(level, zone, start, groups, rim, out):
    scale = parent_scale(level + 1)

    def body(i):
        row = pl.multiple_of(8 * i, 8)
        v = [zone[q, pl.ds(start + row, 8), :] for q in range(19)]
        v = relax(v, 1.0 - scale, scale)
        for q in range(19):
            out[q, pl.ds(row, 8), :] = v[q] if rim is None else jnp.where(rim, v[q], 0.0)

    loop(groups, body)


def widen(converted, matrix, child, skip, count, wide, spread, first):
    rows = converted.shape[1]
    value = moved(converted[...].reshape(19 * rows, LANES), matrix)
    for c in range(CHUNKS[child]):
        part = value[:, c * LANES : (c + 1) * LANES].reshape(19, rows, LANES)
        if count < rows:
            spread[pl.ds(0, 19)] = part
        for q in range(19):
            t = part[q] if count == rows else spread[q, pl.ds(skip, count), :]
            wide[q, c, pl.ds(first, count, stride=2), :] = t
            wide[q, c, pl.ds(first + 1, count, stride=2), :] = t


def start_kernel(own, to_right, to_left, center, to_zone_right, to_zone_left):
    me = lax.axis_index("level")

    def halo(q, source):
        for j in range(8):
            to_left[q, pl.ds(j, 2, stride=8), :] = source(pl.ds(0, 2), j)
            to_right[q, pl.ds(j, 2, stride=8), :] = source(pl.ds(SLAB - 2, 2), j)

    loop(20, lambda q: halo(q, lambda rows, j: own[q, rows, pl.ds(j * LANES, LANES)]))

    for level in range(3):

        def push(level=level):
            n, row0, count, rows = OWN[level], ROW0[level], CHUNKS[level], ROWS[level]
            span = max(n + 16, 32)

            def scoped(buf, post, packed):
                post[...] = jnp.zeros(post.shape, F32)
                buf[19] = jnp.zeros(buf.shape[1:], F32)
                load_level(level, own, None, None, buf)
                collide_rows(level, buf, buf, None, post, row0, n // 8)
                pull_rows(level, post, buf, row0 - 8, n // 8 + 2)
                def spanned(first, many, c):
                    return buf[pl.ds(first, many), c, pl.ds(row0 - 8, span), :].reshape(many * span, LANES)

                main = folded = flags = None
                for c in range(count):
                    part = moved(spanned(0, PLANES, c), pack_chunk(level, c))
                    main = part if main is None else main + part
                    part = moved(spanned(PLANES, 4, c), fold_chunk(level, c))
                    folded = part if folded is None else folded + part
                    part = moved(spanned(19, 1, c), flag_chunk(level, c))
                    flags = part if flags is None else flags + part
                for p in range(PLANES):
                    j, k = divmod(p, 3)
                    part = main[span * p : span * (p + 1)]
                    if j < 4:
                        part = part + folded[span * j : span * (j + 1), LANES * k : LANES * (k + 1)]
                    packed[p] = part
                packed[PLANES] = flags
                for p in range(PLANES + 1):
                    center[pl.ds(p * (OWN[2] + 2), n + 2), :] = packed[p, pl.ds(7, n + 2), :]
                    to_zone_right[p] = packed[p, pl.ds(n + 1, 8), :]
                    to_zone_left[p] = packed[p, pl.ds(7, 8), :]

            pl.run_scoped(
                scoped,
                pltpu.VMEM((20, count, rows, LANES), F32),
                pltpu.VMEM((19, count, rows, LANES), F32),
                pltpu.VMEM((PLANES + 1, span, LANES), F32),
            )

        pl.when(me == level)(push)


def pack_flows(post, out, row):
    lane = lanes()
    total = jnp.zeros((8, LANES), F32)
    for k, q in enumerate(Z_OUT):
        v = pltpu.roll(post[q], (16 * k - zone_lane(2, 8, 1)) % LANES, 1)
        total = jnp.where((lane >= 16 * k) & (lane < 16 * k + 16), v, total)
    for group, y, base in ((Y_DOWN, 8, 80), (Y_UP, 23, 85)):
        for k, q in enumerate(group):
            lane0 = base + k
            v = pltpu.roll(post[q], (lane0 - zone_lane(2, y, 0)) % LANES, 1)
            total = jnp.where((lane == lane0) | (lane == lane0 + 25), v, total)
    out[pl.ds(row, 8), :] = total


def interface_values(zpost, zone, rim, matrix, wide):
    scale = parent_scale(3)
    for i in range(3):
        halves = []
        for half in range(2):
            rows = pl.ds(8 + 16 * i + 8 * half, 8)
            if zpost is None:
                v = [zone[q, rows, :] for q in range(19)]
            else:
                v = zone_pulled(zpost, 2, 8 + 16 * i + 8 * half)
                if zone is not None:
                    for q in range(19):
                        zone[q, rows, :] = v[q]
            v = relax(v, 1.0 - scale, scale)
            halves.append([jnp.where(rim, v[q], 0.0) for q in range(19)])
        part = jnp.concatenate([halves[half][q] for q in range(19) for half in range(2)], axis=0)
        total = moved(part, matrix[...])
        for q in range(19):
            t = total[16 * q : 16 * q + 16]
            wide[q, 0, pl.ds(PAD + 32 * i, 16, stride=2), :] = t
            wide[q, 0, pl.ds(PAD + 32 * i + 1, 16, stride=2), :] = t


def restrict_and_collide(g, zone, covered, matrix, zpost, flows, first):
    scale = child_scale(3)
    for i in range(3):
        even, odd = pl.ds(PAD + 32 * i, 16, stride=2), pl.ds(PAD + 32 * i + 1, 16, stride=2)
        part = jnp.concatenate([g[q, 0, even, :] + g[q, 0, odd, :] for q in range(19)], axis=0)
        total = moved(part, matrix[...])
        for half in range(2):
            rows = pl.ds(8 + 16 * i + 8 * half, 8)
            v = relax([total[16 * q + 8 * half : 16 * q + 8 * half + 8] for q in range(19)], 1.0 - scale, scale)
            v = [jnp.where(covered, v[q], zone[q, rows, :]) for q in range(19)]
            post = collided(v, zone[19, rows, :], 2)
            for q in range(19):
                zpost[q, rows, :] = post[q]
            pack_flows(post, flows, first + 16 * i + 8 * half)


def finest_cycle(g, pa, pb, wide, first, groups):
    mask = interface_mask(3, 0)

    def substep(v, row, dest):
        v = [jnp.where(mask, wide[q, 0, pl.ds(row, 8), :], v[q]) for q in range(19)]
        post = collided(v, g[19, 0, pl.ds(row, 8), :], 3)
        for q in range(19):
            dest[q, 0, pl.ds(row, 8), :] = post[q]

    row_loop(first, groups, lambda row: substep([g[q, 0, pl.ds(row, 8), :] for q in range(19)], row, pa))
    row_loop(first, groups, lambda row: substep(pulled(pa, 3, row, [0], True)[0], row, pb))


def finest_role(own, low, high, center, left, right, g, zpost, flows):
    def scoped(pa, pb, wide, zone, widen3, restrict3):
        widen3[...] = widen_matrix(3)
        restrict3[...] = restrict_chunk(3, 0)
        load_level(3, own, low, high, g)
        load_zone(2, zone, 16, center, left, right, 8, 48)
        covered, rim = zone_masks(2, 0)
        interface_values(None, zone, rim, widen3, wide)
        for cycle in range(3):
            first, groups = (PAD, 12) if cycle < 2 else (PAD + 8, 10)

            def step_out(row):
                v = pulled(pb, 3, row, [0])[0]
                for q in range(19):
                    g[q, 0, pl.ds(row, 8), :] = v[q]

            finest_cycle(g, pa, pb, wide, first, groups)
            row_loop(first, groups, step_out)
            restrict_and_collide(g, zone, covered, restrict3, zpost, flows, 48 * cycle)
            if cycle < 2:
                interface_values(zpost, zone, rim, widen3, wide)

    rows = ROWS[3]
    pl.run_scoped(
        scoped,
        pltpu.VMEM((19, 1, rows, LANES), F32),
        pltpu.VMEM((19, 1, rows, LANES), F32),
        pltpu.VMEM((19, 1, rows, LANES), F32),
        pltpu.VMEM((20, 64, LANES), F32),
        pltpu.VMEM((2 * LANES, LANES), BF16),
        pltpu.VMEM((2 * LANES, LANES), BF16),
    )


def last_cycle_kernel(g, zpost, state, means, far_first, far_coarse, matrices):
    row0, n = ROW0[3], OWN[3]

    @pl.when(lax.axis_index("level") == 2)
    def _():
        for k, (q, c) in enumerate(FLOW_CHUNKS):
            matrices[:, pl.ds(k * LANES, LANES)] = flow_chunk(q, c)

    @pl.when(lax.axis_index("level") == 3)
    def _():
        def scoped(pa, pb, wide, flat, spread, out, pairs, value, scratch, widen3):
            _, rim = zone_masks(2, 0)

            widen3[...] = widen_matrix(3)
            interface_values(zpost, None, rim, widen3, wide)
            finest_cycle(g, pa, pb, wide, PAD + 8, 10)

            def step_out(row):
                v = pulled(pb, 3, row, [0])[0]
                for q in range(19):
                    out[q, 0, pl.ds(row - row0, 8), :] = v[q]

            row_loop(row0, n // 8, step_out)
            for q in range(19):
                flat[q, pl.ds(0, 32), :] = (
                    out[q, 0, pl.ds(0, 32, stride=2), :] + out[q, 0, pl.ds(1, 32, stride=2), :]
                )
            total = None
            for i in range(4):
                part = jnp.concatenate(
                    [flat[q, pl.ds(8 * i, 8), :] for q in range(19)] + [jnp.zeros((8, LANES), F32)], axis=0
                )
                part = moved(part, compact_chunk(i))
                total = part if total is None else total + part
            scale = child_scale(3)
            v = relax([total[8 * q : 8 * q + 8] for q in range(19)], 1.0 - scale, scale)
            for q in range(19):
                means[pl.ds(8 * q, 8), :] = v[q]
            means[pl.ds(152, 8), :] = jnp.zeros((8, LANES), F32)
            pairs[...] = jnp.zeros(pairs.shape, F32)
            for q in range(19):
                pairs[pl.ds(4 * q, 4), :] = (
                    means[pl.ds(8 * q, 4, stride=2), :] + means[pl.ds(8 * q + 1, 4, stride=2), :]
                )
            for odd in range(2):
                scratch[pl.ds(0, 80), :] = moved(pairs[...], deep_matrix(odd))
                for q in range(19):
                    value[pl.ds(8 * q + 4 * odd, 4), :] = scratch[pl.ds(4 * q, 4), :]
            scale = child_scale(2)
            v = relax([value[pl.ds(8 * q, 8), :] for q in range(19)], 1.0 - scale, scale)
            deep = deep_late(lanes() & 63)
            for q in range(19):
                value[pl.ds(8 * q, 8), :] = jnp.where(deep, v[q], 0.0)
            value[pl.ds(152, 8), :] = jnp.zeros((8, LANES), F32)
            lane = lanes()
            for plane in range(3):
                total = jnp.zeros((8, LANES), F32)
                for k in range(8):
                    q = 8 * plane + k
                    if q < 19:
                        part = pltpu.roll(value[pl.ds(8 * q, 8), :], (8 * k - 4) % LANES, 1)
                        total = jnp.where(((lane & 63) >> 3) == k, part, total)
                far_first[pl.ds(8 * plane, 8), :] = total
            late_means(value, True, flat.at[:, pl.ds(0, 8)], spread.at[pl.ds(0, 20), pl.ds(0, 8)])
            packed_planes([flat[q, pl.ds(0, 8), :] for q in range(19)], far_coarse, 32)
            store_level(3, out, 0, state)

        rows = ROWS[3]
        pl.run_scoped(
            scoped,
            pltpu.VMEM((19, 1, rows, LANES), F32),
            pltpu.VMEM((19, 1, rows, LANES), F32),
            pltpu.VMEM((19, 1, rows, LANES), F32),
            pltpu.VMEM((19, 48, LANES), F32),
            pltpu.VMEM((20, 48, LANES), F32),
            pltpu.VMEM((19, 1, n, LANES), F32),
            pltpu.VMEM((80, LANES), F32),
            pltpu.VMEM((160, LANES), F32),
            pltpu.VMEM((80, LANES), F32),
            pltpu.VMEM((2 * LANES, LANES), BF16),
        )


def restrict_pairs(level, g, first, count, skip, flat):
    flat[...] = jnp.zeros(flat.shape, F32)
    for q in range(19):
        for c in range(CHUNKS[level]):
            flat[q, c, pl.ds(skip, count), :] = (
                g[q, c, pl.ds(first, count, stride=2), :] + g[q, c, pl.ds(first + 1, count, stride=2), :]
            )
    rows = flat.shape[2]
    total = None
    for c in range(CHUNKS[level]):
        part = moved(flat[:, c].reshape(flat.shape[0] * rows, LANES), restrict_chunk(level, c))
        total = part if total is None else total + part
    return total.reshape(flat.shape[0], rows, LANES)


def second_role(own, low, high, center, left, right, keep_post, keep_wide, early, ring):
    level, row0 = 2, ROW0[2]
    first = row0 - 8

    def scoped(g, wide, zone, zpost, conv, spread, flat):
        load_level(level, own, low, high, g)
        load_zone(1, zone, 16, center, left, right, 8, 32)
        covered, rim = zone_masks(1, 0)
        keep_post[19] = g[19]
        convert_zone(1, zone, 8, 4, rim, conv)
        widen(conv, widen_matrix(2), 2, 4, 24, wide, spread, first)
        collide_rows(level, g, g, wide, keep_post, first, 6)
        pull_rows(level, keep_post, g, first, 6)
        collide_rows(level, g, g, wide, keep_post, first, 6)
        pull_rows(level, keep_post, g, first, 6)
        spread[...] = restrict_pairs(level, g, first, 24, 4, flat)
        scale = child_scale(2)

        def restrict(i):
            row = pl.multiple_of(8 * i, 8)
            v = relax([spread[q, pl.ds(row, 8), :] for q in range(19)], 1.0 - scale, scale)
            v = [jnp.where(covered, v[q], zone[q, pl.ds(8 + row, 8), :]) for q in range(19)]
            post = collided(v, zone[19, pl.ds(8 + row, 8), :], 1)
            for q in range(19):
                zpost[q, pl.ds(8 + row, 8), :] = post[q]

        loop(4, restrict)

        def zone_pull(row):
            v = zone_pulled(zpost, 1, row)
            for q in range(19):
                zone[q, pl.ds(row, 8), :] = v[q]

        row_loop(8, 4, zone_pull)
        convert_zone(1, zone, 8, 4, rim, conv)
        widen(conv, widen_matrix(2), 2, 4, 24, keep_wide, spread, first)
        near, _ = zone_masks(1, 1)
        for q in range(19):
            for i in range(2):
                rows = pl.ds(8 * i, 8)
                early[q, rows, :] = jnp.where(near, zone[q, pl.ds(16 + 8 * i, 8), :], 0.0)
        mean = moved(early[...].reshape(19 * 16, LANES), mean_ring_matrix())
        spread[:, pl.ds(0, 16), :] = mean.reshape(19, 16, LANES)
        for q in range(19):
            ring[q] = spread[q, pl.ds(0, 8, stride=2), :] + spread[q, pl.ds(1, 8, stride=2), :]

    pl.run_scoped(
        scoped,
        pltpu.VMEM((20, 2, ROWS[2], LANES), F32),
        pltpu.VMEM((19, 2, ROWS[2], LANES), F32),
        pltpu.VMEM((20, 48, LANES), F32),
        pltpu.VMEM((19, 48, LANES), F32),
        pltpu.VMEM((19, 32, LANES), F32),
        pltpu.VMEM((19, 32, LANES), F32),
        pltpu.VMEM((19, 2, 32, LANES), F32),
    )


def first_role(own, low, high, center, left, right, state, early):
    level, row0, n = 1, ROW0[1], OWN[1]
    first = row0 - 8

    def scoped(g, post, wide, zone, conv, spread, flat):
        load_level(level, own, low, high, g)
        load_zone(0, zone, 12, center, left, right, 8, 16)
        y, z = zone_cell(0, lanes())
        convert_zone(0, zone, 8, 2, (z == 7) | (y == Y_LOW) | (y == Y_HIGH), conv)
        widen(conv, widen_matrix(1), 1, 0, 16, wide, spread, first)
        collide_rows(level, g, g, wide, post, first, 4)
        pull_rows(level, post, g, first, 4)
        collide_rows(level, g, g, wide, post, first, 4)
        pull_rows(level, post, g, row0, n // 8)
        store_level(level, g, row0, state)
        total = None
        for c in range(CHUNKS[1]):
            part = moved(g[pl.ds(0, 19), c, pl.ds(row0, n), :].reshape(19 * n, LANES), mean_chunk(c))
            total = part if total is None else total + part
        flat[...] = total.reshape(19, n, LANES)
        for q in range(19):
            early[q, pl.ds(0, 8), :] = flat[q, pl.ds(0, 8, stride=2), :] + flat[q, pl.ds(1, 8, stride=2), :]

    pl.run_scoped(
        scoped,
        pltpu.VMEM((20, 4, ROWS[1], LANES), F32),
        pltpu.VMEM((19, 4, ROWS[1], LANES), F32),
        pltpu.VMEM((19, 4, ROWS[1], LANES), F32),
        pltpu.VMEM((20, 32, LANES), F32),
        pltpu.VMEM((19, 16, LANES), F32),
        pltpu.VMEM((19, 16, LANES), F32),
        pltpu.VMEM((19, n, LANES), F32),
    )


def coarse_role(own, low, high, state):
    level, row0 = 0, ROW0[0]

    def scoped(g, post):
        load_level(level, own, low, high, g)
        collide_rows(level, g, g, None, post, row0 - 8, 3)
        pull_rows(level, post, g, row0, 1)
        store_level(level, g, row0, state)

    pl.run_scoped(
        scoped,
        pltpu.VMEM((20, 8, ROWS[0], LANES), F32),
        pltpu.VMEM((19, 8, ROWS[0], LANES), F32),
    )


def main_kernel(
    own, low, high, center, left, right,
    state, fine, fine_post, flows, keep_post, keep_wide, early, ring,
):
    me = lax.axis_index("level")
    arrived = (own, low, high, center, left, right)

    @pl.when(me == 3)
    def _():
        finest_role(*arrived, fine, fine_post, flows)

    @pl.when(me == 2)
    def _():
        second_role(*arrived, keep_post, keep_wide, early, ring)

    @pl.when(me == 1)
    def _():
        first_role(*arrived, state, early)

    @pl.when(me == 0)
    def _():
        coarse_role(own, low, high, state)


def flow_kernel(flows, keep_post, keep_wide, ring, matrices, result, late, late_mean):
    level, row0 = 2, ROW0[2]
    first = row0 - 8

    @pl.when(lax.axis_index("level") == 2)
    def _():
        def scoped(g, post, override, flat, value, scratch):
            total = moved(flows[...], matrices[...])
            for k in range(len(FLOW_CHUNKS)):
                override[k] = total[:, k * LANES : (k + 1) * LANES]
            outward = []
            for q, c in FLOW_CHUNKS:
                y, z = cell_of(2, lanes() + c * LANES)
                outward.append(flow_mask(q, y, z))

            def overridden(c, row, cycle, v):
                v = list(v)
                for k, (q, chunk) in enumerate(FLOW_CHUNKS):
                    if chunk == c:
                        value = override[k, pl.ds(48 * cycle + row - first, 8), :]
                        v[q] = jnp.where(outward[k], value, v[q])
                return v

            masks = [interface_mask(level, c) for c in range(2)]

            def begin(row):
                for c in range(2):
                    v = overridden(c, row, 0, [keep_post[q, c, pl.ds(row, 8), :] for q in range(19)])
                    for q in range(19):
                        post[q, c, pl.ds(row, 8), :] = v[q]

            row_loop(first, 6, begin)
            for cycle in (1, 2):
                pull_rows(level, post, g, first, 6)

                def body(row, cycle=cycle):
                    for c in range(2):
                        v = [
                            jnp.where(masks[c], keep_wide[q, c, pl.ds(row, 8), :], g[q, c, pl.ds(row, 8), :])
                            for q in range(19)
                        ]
                        v = collided(v, keep_post[19, c, pl.ds(row, 8), :], level)
                        v = overridden(c, row, cycle, v)
                        for q in range(19):
                            post[q, c, pl.ds(row, 8), :] = v[q]

                row_loop(first, 6, body)

            def last(row):
                for c, v in enumerate(pulled(post, level, row, range(2))):
                    for q in range(19):
                        result[q, c, pl.ds(row - row0, 8), :] = v[q]

            row_loop(row0, 4, last)
            for q in range(19):
                for c in range(2):
                    flat[c, q] = result[q, c, pl.ds(0, 16, stride=2), :] + result[q, c, pl.ds(1, 16, stride=2), :]
            flat[:, 19] = jnp.zeros((2, 16, LANES), F32)
            total = None
            for half in range(2):
                for c in range(2):
                    part = moved(flat[c, :, pl.ds(8 * half, 8), :].reshape(160, LANES), late_chunk(half, c))
                    total = part if total is None else total + part
            scale = child_scale(2)
            v = relax([total[8 * q : 8 * q + 8] for q in range(19)], 1.0 - scale, scale)
            for q in range(19):
                late[pl.ds(8 * q, 8), :] = v[q]
            late[pl.ds(152, 8), :] = jnp.zeros((8, LANES), F32)
            late_means(late, False, value, scratch)
            packed_planes([value[q] + ring[q] for q in range(19)], late_mean, 32)

        pl.run_scoped(
            scoped,
            pltpu.VMEM((19, 2, ROWS[2], LANES), F32),
            pltpu.VMEM((19, 2, ROWS[2], LANES), F32),
            pltpu.VMEM((len(FLOW_CHUNKS), 144, LANES), F32),
            pltpu.VMEM((2, 20, 16, LANES), F32),
            pltpu.VMEM((19, 8, LANES), F32),
            pltpu.VMEM((20, 8, LANES), F32),
        )


def prepare_kernel(early, far, far_coarse, means, covered, near):
    me = lax.axis_index("level")

    @pl.when(me == 2)
    def _():
        for i in range(4):
            total = moved(means[...], spread_chunk(i))
            for c in range(2):
                covered[2 * i + c] = total[:, c * LANES : (c + 1) * LANES]

    @pl.when(me == 1)
    def _():
        total = moved(early[...].reshape(19 * 16, LANES), spread_zone_matrix())
        for c in range(4):
            near[c] = total[:, c * LANES : (c + 1) * LANES]

    @pl.when(me == 0)
    def _():
        def scoped(value):
            lane = lanes()
            for q in range(19):
                rows = pl.ds(8 * (q // 4), 8)
                part = far[rows, :] + far_coarse[rows, :]
                if q % 4:
                    part = pltpu.roll(part, LANES - 32 * (q % 4), 1)
                value[q] = jnp.where(lane < 32, part, 0.0)
            value[19] = jnp.zeros((8, LANES), F32)
            total = moved(value[...].reshape(160, LANES), mean_back_matrix())
            scale = child_scale(1)
            v = relax(
                [early[q, pl.ds(0, 8), :] + total[8 * q : 8 * q + 8] for q in range(19)],
                1.0 - scale,
                scale,
            )
            for q in range(19):
                value[q] = v[q]
            total = moved(value[...].reshape(160, LANES), spread_covered_matrix())
            for c in range(4):
                covered[c] = total[:, c * LANES : (c + 1) * LANES]

        pl.run_scoped(scoped, pltpu.VMEM((20, 8, LANES), F32))


def finish_kernel(old_state, result, third_state, late, far, covered_values, near, state):
    me = lax.axis_index("level")

    @pl.when(me == 3)
    def _():
        state[...] = third_state[...]

    @pl.when(me == 2)
    def _():
        def scoped(g):
            for c in range(2):
                y, z = cell_of(2, lanes() + c * LANES)
                covered = (y >= Y_LOW) & (y <= Y_HIGH) & (z <= 1)

                def insert(q, c=c, covered=covered):
                    for i in range(4):
                        rows = pl.ds(8 * i, 8)
                        value = covered_values[2 * i + c, pl.ds(pl.multiple_of(8 * q, 8), 8), :]
                        g[q, c, rows, :] = jnp.where(covered, value, result[q, c, rows, :])

                loop(19, insert, 19)
            store_level(2, g, 0, state)

        pl.run_scoped(scoped, pltpu.VMEM((19, 2, OWN[2], LANES), F32))

    @pl.when(me == 1)
    def _():
        def scoped(inner, value):
            lane = lanes()
            deep = deep_late(lane & 63)
            for q in range(19):
                part = pltpu.roll(far[pl.ds(8 * (q // 8), 8), :], (4 - 8 * (q % 8)) % LANES, 1)
                value[pl.ds(8 * q, 8), :] = jnp.where(deep, part, late[pl.ds(8 * q, 8), :])
            value[pl.ds(152, 8), :] = jnp.zeros((8, LANES), F32)
            for half in range(2):
                total = moved(value[...], late_back_chunk(half))
                for c in range(2):
                    part = total[:, c * LANES : (c + 1) * LANES].reshape(20, 8, LANES)
                    inner[c, :, pl.ds(8 * half, 8), :] = part

            def one(q):
                for j in range(8):
                    c = j % 4
                    y, z = cell_of(1, lanes() + c * LANES)
                    columns = pl.ds(j * LANES, LANES)
                    rows = pl.ds(j // 4, 8, stride=2)
                    ring = near[c, pl.ds(16 * q + j // 4, 8, stride=2), :]
                    value = jnp.where(near_first(y, z), ring, old_state[q, :, columns])
                    if c in (1, 2):
                        value = jnp.where(covered_first(y, z), inner[c - 1, q, rows, :], value)
                    state[q, :, columns] = value

            loop(19, one)

        pl.run_scoped(
            scoped,
            pltpu.VMEM((2, 20, 16, LANES), F32),
            pltpu.VMEM((160, LANES), F32),
        )

    @pl.when(me == 0)
    def _():
        covered = (lanes() & 31) < 8

        def one(q):
            rows = pl.ds(pl.multiple_of(8 * q, 8), 8)
            for j in range(8):
                columns = pl.ds(j * LANES, LANES)
                value = old_state[q, :, columns]
                if 2 <= j < 6:
                    value = jnp.where(covered, covered_values[j - 2, rows, :], value)
                state[q, :, columns] = value

        loop(19, one, 19)


def call(kernel, shapes, args, micros):
    return pl.pallas_call(
        kernel,
        out_shape=[
            jax.ShapeDtypeStruct(s[:-1], BF16) if s[-1] is BF16 else jax.ShapeDtypeStruct(s, F32) for s in shapes
        ],
        in_specs=[pl.BlockSpec(memory_space=pltpu.VMEM)] * len(args),
        out_specs=[pl.BlockSpec(memory_space=pltpu.VMEM)] * len(shapes),
        cost_estimate=pl.CostEstimate(
            flops=int(micros * 1e9), bytes_accessed=int(micros * 3.6e6), transcendentals=0
        ),
        compiler_params=pltpu.CompilerParams(vmem_limit_bytes=24 * 1024 * 1024),
    )(*args)


def shards(populations, solid):
    if populations.shape[1:] != (19, SLAB, NY * NZ):
        raise ValueError("unexpected slab")
    own = jnp.concatenate([populations[0], solid.astype(F32)], axis=0)
    blocks = lax.axis_size("blocks")
    forward = [(i, (i + 1) % blocks) for i in range(blocks)]
    backward = [(i, (i - 1) % blocks) for i in range(blocks)]
    down = [(i, i + 1) for i in range(LEVELS - 1)]

    def diagonal(step):
        return [
            (level * blocks + b, (level + 1) * blocks + (b + step) % blocks)
            for level in range(LEVELS - 1)
            for b in range(blocks)
        ]

    both = ("level", "blocks")
    to_right, to_left, center, zone_right, zone_left = call(
        start_kernel,
        [(20, 16, LANES), (20, 16, LANES), (CENTER_ROWS, LANES), (PLANES + 1, 8, LANES), (PLANES + 1, 8, LANES)],
        [own],
        1.5,
    )
    center = lax.ppermute(center, "level", down)
    left = lax.ppermute(zone_right, both, diagonal(1))
    right = lax.ppermute(zone_left, both, diagonal(-1))
    low = lax.ppermute(to_right, "blocks", forward)
    high = lax.ppermute(to_left, "blocks", backward)

    full = (19, SLAB, NY * NZ)
    state, fine, fine_post, flows, keep_post, keep_wide, early, ring = call(
        main_kernel,
        [
            full,
            (20, 1, ROWS[3], LANES),
            (19, 64, LANES),
            (144, LANES),
            (20, 2, ROWS[2], LANES),
            (19, 2, ROWS[2], LANES),
            (19, 16, LANES),
            (19, 8, LANES),
        ],
        [own, low, high, center, left, right],
        8.0,
    )
    flows = lax.ppermute(flows, "level", [(3, 2)])
    early = lax.ppermute(early, "level", [(2, 1), (1, 0)])
    third_state, means, far_first, far_coarse, matrices = call(
        last_cycle_kernel,
        [full, (160, LANES), (40, LANES), (40, LANES), (2 * LANES, len(FLOW_CHUNKS) * LANES, BF16)],
        [fine, fine_post],
        4.0,
    )
    far_coarse = lax.ppermute(far_coarse, "level", [(3, 0)])
    means = lax.ppermute(means, "level", [(3, 2)])
    result, late, late_mean = call(
        flow_kernel,
        [(19, 2, OWN[2], LANES), (160, LANES), (40, LANES)],
        [flows, keep_post, keep_wide, ring, matrices],
        2.5,
    )
    me = lax.axis_index("level")
    far = lax.ppermute(jnp.where(me == 3, far_first, late_mean), "level", [(3, 1), (2, 0)])
    late = lax.ppermute(late, "level", [(2, 1)])
    covered, near = call(
        prepare_kernel, [(8, 160, LANES), (4, 304, LANES)], [early, far, far_coarse, means], 4.0
    )
    (state,) = call(
        finish_kernel, [full], [state, result, third_state, late, far, covered, near], 1.0
    )
    return state[None]


def solution(mesh):
    in_specs = (P("level", None, "blocks", None), P("level", "blocks", None))
    out_specs = P("level", None, "blocks", None)
    return jax.shard_map(shards, mesh=mesh, in_specs=in_specs, out_specs=out_specs, check_vma=False)
```

```python
import jax
import jax.numpy as jnp
from jax import lax
from jax.experimental import pallas as pl
from jax.experimental.pallas import tpu as pltpu
from jax.sharding import PartitionSpec as P

NY = 32
NZ = 32
LEVELS = 4
SLAB = 8
LANES = 128
VELOCITY = (
    (0, 0, 0),
    (1, 0, 0),
    (-1, 0, 0),
    (0, 1, 0),
    (0, -1, 0),
    (0, 0, 1),
    (0, 0, -1),
    (1, 1, 0),
    (-1, -1, 0),
    (1, -1, 0),
    (-1, 1, 0),
    (1, 0, 1),
    (-1, 0, -1),
    (1, 0, -1),
    (-1, 0, 1),
    (0, 1, 1),
    (0, -1, -1),
    (0, 1, -1),
    (0, -1, 1),
)
OPPOSITE = (0, 2, 1, 4, 3, 6, 5, 8, 7, 10, 9, 12, 11, 14, 13, 16, 15, 18, 17)
TAU_BASE = 1.0
F32 = jnp.float32
BF16 = jnp.bfloat16

PAD = 8
MARGIN = (8, 8, 8, 16)
FACTOR = (1, 2, 4, 8)
CHUNKS = (8, 4, 2, 1)
DEPTH = (32, 16, 8, 4)
OWN = tuple(SLAB * f for f in FACTOR)
ROW0 = tuple(PAD + m for m in MARGIN)
ROWS = tuple(OWN[l] + 2 * ROW0[l] for l in range(LEVELS))

Y_LOW = NY // 4
Y_HIGH = 3 * NY // 4 - 1


def zone_lane(level, y, z):
    if level == 0:
        return (y - 8) * 8 + z
    if level == 1:
        return z * 20 + y - 6
    return z * 25 + y - 4


ZONE_PITCH = (None, 20, 25)


def level_lane(level, y, z):
    return y * DEPTH[level] + z


def made(columns, weight, holds):
    row = lax.broadcasted_iota(jnp.int32, (LANES, columns), 0)
    column = lax.broadcasted_iota(jnp.int32, (LANES, columns), 1)
    matrix = jnp.where(holds(row, column), weight, 0.0).astype(BF16)
    return jnp.concatenate([matrix, matrix], axis=0)


def cell_of(level, lane):
    return lane >> (DEPTH[level].bit_length() - 1), lane & (DEPTH[level] - 1)


def message_cell(level, y, z):
    if level == 0:
        side = (z < 7) & ((y == 8) | (y == 23))
        top = (z == 7) & (y >= 8) & (y <= 23)
        return jnp.where(z == 7, y - 8, 16 + 2 * z + (y == 23).astype(jnp.int32)), side | top
    if level == 1:
        outer = ((y >= 6) & (y <= 8)) | ((y >= 23) & (y <= 25))
        side = (z < 3) & outer
        top = (z >= 3) & (z <= 5) & (y >= 6) & (y <= 25)
        return jnp.where(z >= 3, (z - 3) * 20 + y - 6, 60 + z * 6 + jnp.where(y < 9, y - 6, y - 20)), side | top
    outer = ((y >= 5) & (y <= 8)) | ((y >= 23) & (y <= 26))
    side = (z == 0) & outer
    top = (z >= 1) & (z <= 4) & (y >= 5) & (y <= 26)
    return jnp.where(z >= 1, (z - 1) * 22 + y - 5, 88 + jnp.where(y < 9, y - 5, y - 19)), side | top


def pack_chunk(level, c):
    def holds(row, column):
        y, z = cell_of(level, row + c * LANES)
        lane, sent = message_cell(level, y, z)
        return sent & (column == lane)

    return made(LANES, 1.0, holds)


def flag_chunk(level, c):
    def holds(row, column):
        y, z = cell_of(level, row + c * LANES)
        if level == 0:
            inside = (y >= 8) & (y <= 23) & (z <= 7)
        elif level == 1:
            inside = (y >= 6) & (y <= 25) & (z <= 5)
        else:
            inside = (y >= 5) & (y <= 26) & (z <= 4)
        return inside & (column == zone_lane(level, y, z))

    return made(LANES, 1.0, holds)


def fold_chunk(level, c):
    def holds(row, column):
        y, z = cell_of(level, row + c * LANES)
        lane, sent = message_cell(level, y, z)
        return sent & ((column & (LANES - 1)) == 96 + (lane & 31)) & ((column >> 7) == (lane >> 5))

    return made(3 * LANES, 1.0, holds)


def unpack_matrix(level, k):
    def holds(row, column):
        y, z = zone_cell(level, column & (LANES - 1))
        lane, sent = message_cell(level, y, z)
        folded = (row == 96 + (lane & 31)) & ((lane >> 5) == k)
        own = row == lane
        return sent & (((column < LANES) & own) | ((column >= LANES) & folded))

    return made(2 * LANES, 1.0, holds)


def widen_matrix(child):
    def holds(row, column):
        y, z = cell_of(child, column)
        edge = (y == 0) | (y == NY - 1) | (z == DEPTH[child] - 1)
        return edge & (row == zone_lane(child - 1, 8 + (y >> 1), z >> 1))

    return made(CHUNKS[child] * LANES, 1.0, holds)


def restrict_chunk(child, c):
    def holds(row, column):
        y, z = cell_of(child, row + c * LANES)
        return column == zone_lane(child - 1, 8 + (y >> 1), z >> 1)

    return made(LANES, 0.125, holds)


def compact_chunk(i):
    def holds(row, column):
        y, z = cell_of(3, row)
        return column == 32 * i + (y >> 1) * 2 + (z >> 1)

    return made(LANES, 0.125, holds)


def spread_chunk(i):
    def holds(row, column):
        y, z = cell_of(2, column)
        return (y >= Y_LOW) & (y <= Y_HIGH) & (z <= 1) & (row == 32 * i + (y - Y_LOW) * 2 + z)

    return made(2 * LANES, 1.0, holds)


def near_first(y, z):
    return (y >= Y_LOW - 1) & (y <= Y_HIGH + 1) & (z <= 4)


def mean_chunk(c):
    def holds(row, column):
        y, z = cell_of(1, row + c * LANES)
        return jnp.logical_not(near_first(y, z)) & (column == zone_lane(0, 8 + (y >> 1), z >> 1))

    return made(LANES, 0.125, holds)


def zone_cell(level, lane):
    if level == 0:
        return 8 + (lane >> 3), lane & 7
    pitch, first = ZONE_PITCH[level], 6 if level == 1 else 4
    z = sum((lane >= pitch * k).astype(jnp.int32) for k in range(1, 7))
    return lane - pitch * z + first, z


def covered_first(y, z):
    return (y >= Y_LOW) & (y <= Y_HIGH) & (z <= 3)


def mean_lane(y, z):
    return y - 11 + 10 * z


def mean_ring_matrix():
    def holds(row, column):
        y, z = zone_cell(1, row)
        ring = near_first(y, z) & jnp.logical_not(covered_first(y, z))
        return ring & (column == mean_lane(8 + (y >> 1), z >> 1))

    return made(LANES, 0.125, holds)


def late_chunk(half, c):
    def holds(row, column):
        y, z = cell_of(2, row + c * LANES)
        return column == 64 * half + (z >> 1) * 16 + (y >> 1)

    return made(LANES, 0.125, holds)


def late_back_chunk(half):
    def holds(row, column):
        y, z = cell_of(1, column + LANES)
        return covered_first(y, z) & (row == 64 * half + z * 16 + y - Y_LOW)

    return made(2 * LANES, 1.0, holds)


def deep_late(cell):
    return (cell >= 4) & (cell < 12)


def late_mean_matrix(half, deep):
    def holds(row, column):
        cell = row - 64 * half
        inside = (cell >= 0) & (cell < 64)
        inside = inside & (deep_late(cell) if deep else jnp.logical_not(deep_late(cell)))
        return inside & (column == mean_lane(12 + ((cell & 15) >> 1), cell >> 5))

    return made(LANES, 0.125, holds)


def deep_matrix(odd):
    def holds(row, column):
        i, y = row >> 5, (row & 31) >> 1
        return ((i & 1) == odd) & (column == 64 * (i >> 1) + 4 + (y >> 1))

    return made(LANES, 0.125, holds)


def mean_back_matrix():
    def holds(row, column):
        z = (row >= 10).astype(jnp.int32) + (row >= 20).astype(jnp.int32)
        return (row < 30) & (column == zone_lane(0, row - 10 * z + 11, z))

    return made(LANES, 1.0, holds)


def packed_planes(source, out, width):
    lane = lanes()
    per = LANES // width
    for plane in range(-(-19 // per)):
        total = jnp.zeros((8, LANES), F32)
        for k in range(per):
            q = per * plane + k
            if q < 19:
                part = source[q] if k == 0 else pltpu.roll(source[q], width * k, 1)
                total = jnp.where((lane >= width * k) & (lane < width * (k + 1)), part, total)
        out[pl.ds(8 * plane, 8), :] = total


def late_means(late, weights, value, scratch):
    for half in range(2):
        scratch[...] = moved(late[...], weights[half]).reshape(20, 8, LANES)
        for q in range(19):
            value[q, pl.ds(4 * half, 4), :] = (
                scratch[q, pl.ds(0, 4, stride=2), :] + scratch[q, pl.ds(1, 4, stride=2), :]
            )


def spread_zone_matrix():
    def holds(row, column):
        y, z = cell_of(1, column)
        return near_first(y, z) & (row == zone_lane(1, y, z))

    return made(4 * LANES, 1.0, holds)


def spread_covered_matrix():
    def holds(row, column):
        y, z = cell_of(0, column + 2 * LANES)
        return (z < 8) & (row == zone_lane(0, y, z))

    return made(4 * LANES, 1.0, holds)


Z_OUT = (5, 11, 14, 15, 18)
Y_DOWN = (4, 8, 9, 16, 18)
Y_UP = (3, 7, 10, 15, 17)
FLOW_DIRECTIONS = tuple(sorted(set(Z_OUT + Y_DOWN + Y_UP)))


def flow_mask(q, y, z):
    mask = None
    if q in Z_OUT:
        mask = (z == 1) & (y >= Y_LOW) & (y <= Y_HIGH)
    for group, edge in ((Y_DOWN, Y_LOW), (Y_UP, Y_HIGH)):
        if q in group:
            cells = (y == edge) & (z <= 1)
            mask = cells if mask is None else mask | cells
    return mask


FLOW_CHUNKS = tuple(
    (q, c) for q in FLOW_DIRECTIONS for c in range(2) if q in Z_OUT or q in (Y_DOWN, Y_UP)[c]
)


LATE_AT = len(FLOW_CHUNKS)


def flow_chunk(q, c):
    def holds(row, column):
        y, z = cell_of(2, column + c * LANES)
        source = None
        if q in Y_DOWN:
            source = 80 + Y_DOWN.index(q) + 25 * z
        if q in Y_UP:
            source = 85 + Y_UP.index(q) + 25 * z
        if q in Z_OUT:
            over = 16 * Z_OUT.index(q) + y - Y_LOW
            source = over if source is None else jnp.where(z == 1, over, source)
        return flow_mask(q, y, z) & (row == source)

    return made(LANES, 1.0, holds)


def relaxation(level_id):
    return 2.0**level_id * (TAU_BASE - 0.5) + 0.5


def parent_scale(child):
    return relaxation(child) / (2.0 * relaxation(child - 1))


def child_scale(child):
    return 2.0 * relaxation(child - 1) / relaxation(child)


def relax(v, a, b):
    s = [None] + [v[2 * k - 1] + v[2 * k] for k in range(1, 10)]
    d = [None] + [v[2 * k - 1] - v[2 * k] for k in range(1, 10)]
    rho = (
        (1.0 / 3.0) * v[0]
        + (1.0 / 18.0) * (s[1] + s[2] + s[3])
        + (1.0 / 36.0) * ((s[4] + s[5]) + (s[6] + s[7]) + (s[8] + s[9]))
    )
    mx = (1.0 / 18.0) * d[1] + (1.0 / 36.0) * ((d[4] + d[5]) + (d[6] + d[7]))
    my = (1.0 / 18.0) * d[2] + (1.0 / 36.0) * ((d[4] - d[5]) + (d[8] + d[9]))
    mz = (1.0 / 18.0) * d[3] + (1.0 / 36.0) * ((d[6] - d[7]) + (d[8] - d[9]))
    inv = 1.0 / rho
    ux, uy, uz = mx * inv, my * inv, mz * inv
    ra = a * rho
    base = ra - (1.5 * ra) * (ux * ux + uy * uy + uz * uz)
    r45 = 4.5 * ra
    ra3 = 3.0 * ra

    def kept(q):
        return v[q] if b == 1.0 else b * v[q]

    out = [base if b == 0.0 else base + kept(0)]
    cus = (ux, uy, uz, ux + uy, ux - uy, ux + uz, ux - uz, uy + uz, uy - uz)
    for k in range(1, 10):
        cu = cus[k - 1]
        even = base + r45 * (cu * cu)
        odd = ra3 * cu
        plus, minus = even + odd, even - odd
        if b != 0.0:
            plus, minus = plus + kept(2 * k - 1), minus + kept(2 * k)
        out += [plus, minus]
    return out


def collided(v, solid, level):
    inv_tau = 1.0 / relaxation(level)
    relaxed = relax(v, inv_tau, 1.0 - inv_tau)
    flag = solid != 0.0
    return [jnp.where(flag, v[OPPOSITE[q]], relaxed[q]) for q in range(19)]


def lanes():
    return lax.broadcasted_iota(jnp.int32, (8, LANES), 1)


def interface_mask(level, c):
    lane = lanes()
    nz = DEPTH[level]
    mask = (lane & (nz - 1)) == nz - 1
    if c == 0:
        mask = mask | (lane < nz)
    if c == CHUNKS[level] - 1:
        mask = mask | (lane >= LANES - nz)
    return mask


def pulled(post, level, row, chunks, interface_next=False):
    lane = lanes()
    nz, count = DEPTH[level], CHUNKS[level]
    out = [[] for _ in chunks]
    for q in range(19):
        cx, cy, cz = VELOCITY[q]
        shift = cy * nz + cz
        rolled = {}

        def moved_chunk(c):
            if c not in rolled:
                value = post[q, c, pl.ds(row - cx, 8), :]
                rolled[c] = pltpu.roll(value, shift % LANES, 1) if shift != 0 else value
            return rolled[c]

        for place, c in enumerate(chunks):
            value = moved_chunk(c)
            outside = None
            if cy == 1:
                if c > 0:
                    value = jnp.where(lane < shift, moved_chunk(c - 1), value)
                else:
                    outside = lane < nz
            if cy == -1:
                if c < count - 1:
                    value = jnp.where(lane >= LANES + shift, moved_chunk(c + 1), value)
                else:
                    outside = lane >= LANES - nz
            if cz != 0:
                edge = (lane & (nz - 1)) == (0 if cz == 1 else nz - 1)
                outside = edge if outside is None else outside | edge
            if interface_next:
                outside = (lane & (nz - 1)) == 0 if cz == 1 else None
            if outside is not None:
                value = jnp.where(outside, post[OPPOSITE[q], c, pl.ds(row, 8), :], value)
            out[place].append(value)
    return out


def zone_pulled(post, level, row):
    lane = lanes()
    pitch = ZONE_PITCH[level]
    out = []
    for q in range(19):
        cx, cy, cz = VELOCITY[q]
        shift = cz * pitch + cy
        value = post[q, pl.ds(row - cx, 8), :]
        if shift != 0:
            value = pltpu.roll(value, shift % LANES, 1)
            if cz == 1:
                value = jnp.where(lane < pitch, post[OPPOSITE[q], pl.ds(row, 8), :], value)
        out.append(value)
    return out


def zone_masks(level, reach):
    lane = lanes()
    pitch, first = ZONE_PITCH[level], 6 if level == 1 else 4
    top = DEPTH[level] // 4 - 1
    inside = None
    rim = None
    for z in range(top + reach + 1):
        start = z * pitch - first
        row = (lane >= start + Y_LOW - reach) & (lane <= start + Y_HIGH + reach)
        inside = row if inside is None else inside | row
        if z < top:
            row = (lane == start + Y_LOW) | (lane == start + Y_HIGH)
        elif z == top:
            row = (lane >= start + Y_LOW) & (lane <= start + Y_HIGH)
        else:
            continue
        rim = row if rim is None else rim | row
    return inside, rim


def loop(count, body, unroll=None):
    def step(i, carry):
        body(i)
        return carry

    if unroll is None:
        unroll = max(u for u in range(1, 13) if count % u == 0)
    lax.fori_loop(0, count, step, 0, unroll=unroll)


def row_loop(start, count, body):
    loop(count, lambda i: body(pl.multiple_of(start + 8 * i, 8)))


def moved(value, matrix):
    high = value.astype(BF16)
    low = (value - high.astype(F32)).astype(BF16)
    return jnp.dot(jnp.concatenate([high, low], axis=1), matrix, preferred_element_type=F32)


def load_level(level, own, flags, low, high, buf):
    factor, count, row0 = FACTOR[level], CHUNKS[level], ROW0[level]
    n = OWN[level]

    def one(q, source):
        for j in range(8):
            buf[q, j % count, pl.ds(row0 + j // count, 8, stride=factor), :] = source(j)
        if low is not None:
            for c in range(count):
                rows = pl.ds(c, 2 * factor, stride=count) if count > 1 else pl.ds(0, 2 * factor)
                buf[q, c, pl.ds(row0 - 2 * factor, 2 * factor), :] = low[q, rows, :]
                buf[q, c, pl.ds(row0 + n, 2 * factor), :] = high[q, rows, :]

    loop(19, lambda q: one(q, lambda j: own[q, :, pl.ds(j * LANES, LANES)]))
    one(19, lambda j: flags[:, pl.ds(j * LANES, LANES)])


def store_level(level, buf, row0, out):
    factor, count = FACTOR[level], CHUNKS[level]

    def one(q):
        for j in range(8):
            out[q, :, pl.ds(j * LANES, LANES)] = buf[
                q, j % count, pl.ds(row0 + j // count, 8, stride=factor), :
            ]

    loop(19, one)


def collide_rows(level, source, solid, wide, dest, start, groups):
    masks = [interface_mask(level, c) for c in range(CHUNKS[level])]

    def body(row):
        for c in range(CHUNKS[level]):
            v = [source[q, c, pl.ds(row, 8), :] for q in range(19)]
            if wide is not None:
                v = [jnp.where(masks[c], wide[q, c, pl.ds(row, 8), :], v[q]) for q in range(19)]
            post = collided(v, solid[19, c, pl.ds(row, 8), :], level)
            for q in range(19):
                dest[q, c, pl.ds(row, 8), :] = post[q]

    row_loop(start, groups, body)


def pull_rows(level, post, dest, start, groups):
    def body(row):
        step = min(2, CHUNKS[level])
        for first in range(0, CHUNKS[level], step):
            chunks = range(first, first + step)
            for c, v in zip(chunks, pulled(post, level, row, chunks)):
                for q in range(19):
                    dest[q, c, pl.ds(row, 8), :] = v[q]

    row_loop(start, groups, body)


PLANES = 15
CENTER_ROWS = (PLANES + 1) * (OWN[2] + 2)


def load_zone(level, zone, zero_row, center, left, right, start, rows):
    n = OWN[level]

    def scoped(planes):
        planes[...] = jnp.zeros(planes.shape, F32)
        for p in range(PLANES + 1):
            planes[p, pl.ds(zero_row - 1, n + 2), :] = center[pl.ds(p * (OWN[2] + 2), n + 2), :]
            planes[p, pl.ds(zero_row - 7, 8), :] += left[p]
            planes[p, pl.ds(zero_row + n - 1, 8), :] += right[p]
        folded = None
        for k in range(3):
            part = jnp.concatenate([planes[3 * j + k, pl.ds(start, rows), :] for j in range(5)], axis=0)
            total = moved(part, unpack_matrix(level, k))
            for j in range(5):
                zone[3 * j + k, pl.ds(start, rows), :] = total[rows * j : rows * (j + 1), :LANES]
            folded = total[:, LANES:] if folded is None else folded + total[:, LANES:]
        for j in range(4):
            zone[PLANES + j, pl.ds(start, rows), :] = folded[rows * j : rows * (j + 1)]
        zone[19, pl.ds(start, rows), :] = planes[PLANES, pl.ds(start, rows), :]

    pl.run_scoped(scoped, pltpu.VMEM((PLANES + 1, *zone.shape[1:]), F32))


def convert_zone(level, zone, start, groups, rim, out):
    scale = parent_scale(level + 1)

    def body(i):
        row = pl.multiple_of(8 * i, 8)
        v = [zone[q, pl.ds(start + row, 8), :] for q in range(19)]
        v = relax(v, 1.0 - scale, scale)
        for q in range(19):
            out[q, pl.ds(row, 8), :] = v[q] if rim is None else jnp.where(rim, v[q], 0.0)

    loop(groups, body)


def widen(converted, matrix, child, skip, count, wide, spread, first):
    rows = converted.shape[1]
    value = moved(converted[...].reshape(19 * rows, LANES), matrix)
    for c in range(CHUNKS[child]):
        part = value[:, c * LANES : (c + 1) * LANES].reshape(19, rows, LANES)
        if count < rows:
            spread[pl.ds(0, 19)] = part
        for q in range(19):
            t = part[q] if count == rows else spread[q, pl.ds(skip, count), :]
            wide[q, c, pl.ds(first, count, stride=2), :] = t
            wide[q, c, pl.ds(first + 1, count, stride=2), :] = t


def start_kernel(own, flags, to_right, to_left, center, to_zone_right, to_zone_left):
    me = lax.axis_index("level")

    def halo(q, source):
        for j in range(8):
            to_left[q, pl.ds(j, 2, stride=8), :] = source(pl.ds(0, 2), j)
            to_right[q, pl.ds(j, 2, stride=8), :] = source(pl.ds(SLAB - 2, 2), j)

    loop(19, lambda q: halo(q, lambda rows, j: own[q, rows, pl.ds(j * LANES, LANES)]))
    halo(19, lambda rows, j: flags[rows, pl.ds(j * LANES, LANES)])

    for level in range(3):

        def push(level=level):
            n, row0, count, rows = OWN[level], ROW0[level], CHUNKS[level], ROWS[level]
            span = max(n + 16, 32)

            def scoped(buf, post, packed):
                post[...] = jnp.zeros(post.shape, F32)
                buf[19] = jnp.zeros(buf.shape[1:], F32)
                load_level(level, own, flags, None, None, buf)
                collide_rows(level, buf, buf, None, post, row0, n // 8)
                pull_rows(level, post, buf, row0 - 8, n // 8 + 2)
                def spanned(first, many, c):
                    return buf[pl.ds(first, many), c, pl.ds(row0 - 8, span), :].reshape(many * span, LANES)

                main = folded = solid = None
                for c in range(count):
                    part = moved(spanned(0, PLANES, c), pack_chunk(level, c))
                    main = part if main is None else main + part
                    part = moved(spanned(PLANES, 4, c), fold_chunk(level, c))
                    folded = part if folded is None else folded + part
                    part = moved(spanned(19, 1, c), flag_chunk(level, c))
                    solid = part if solid is None else solid + part
                for p in range(PLANES):
                    j, k = divmod(p, 3)
                    part = main[span * p : span * (p + 1)]
                    if j < 4:
                        part = part + folded[span * j : span * (j + 1), LANES * k : LANES * (k + 1)]
                    packed[p] = part
                packed[PLANES] = solid
                for p in range(PLANES + 1):
                    center[pl.ds(p * (OWN[2] + 2), n + 2), :] = packed[p, pl.ds(7, n + 2), :]
                    to_zone_right[p] = packed[p, pl.ds(n + 1, 8), :]
                    to_zone_left[p] = packed[p, pl.ds(7, 8), :]

            pl.run_scoped(
                scoped,
                pltpu.VMEM((20, count, rows, LANES), F32),
                pltpu.VMEM((19, count, rows, LANES), F32),
                pltpu.VMEM((PLANES + 1, span, LANES), F32),
            )

        pl.when(me == level)(push)


def pack_flows(post, out, row):
    lane = lanes()
    total = jnp.zeros((8, LANES), F32)
    for k, q in enumerate(Z_OUT):
        v = pltpu.roll(post[q], (16 * k - zone_lane(2, 8, 1)) % LANES, 1)
        total = jnp.where((lane >= 16 * k) & (lane < 16 * k + 16), v, total)
    for group, y, base in ((Y_DOWN, 8, 80), (Y_UP, 23, 85)):
        for k, q in enumerate(group):
            lane0 = base + k
            v = pltpu.roll(post[q], (lane0 - zone_lane(2, y, 0)) % LANES, 1)
            total = jnp.where((lane == lane0) | (lane == lane0 + 25), v, total)
    out[pl.ds(row, 8), :] = total


def interface_values(zpost, zone, rim, matrix, wide):
    scale = parent_scale(3)
    for i in range(3):
        halves = []
        for half in range(2):
            rows = pl.ds(8 + 16 * i + 8 * half, 8)
            if zpost is None:
                v = [zone[q, rows, :] for q in range(19)]
            else:
                v = zone_pulled(zpost, 2, 8 + 16 * i + 8 * half)
                if zone is not None:
                    for q in range(19):
                        zone[q, rows, :] = v[q]
            v = relax(v, 1.0 - scale, scale)
            halves.append([jnp.where(rim, v[q], 0.0) for q in range(19)])
        part = jnp.concatenate([halves[half][q] for q in range(19) for half in range(2)], axis=0)
        total = moved(part, matrix[...])
        for q in range(19):
            t = total[16 * q : 16 * q + 16]
            wide[q, 0, pl.ds(PAD + 32 * i, 16, stride=2), :] = t
            wide[q, 0, pl.ds(PAD + 32 * i + 1, 16, stride=2), :] = t


def restrict_and_collide(g, zone, covered, matrix, zpost, flows, first):
    scale = child_scale(3)
    for i in range(3):
        even, odd = pl.ds(PAD + 32 * i, 16, stride=2), pl.ds(PAD + 32 * i + 1, 16, stride=2)
        part = jnp.concatenate([g[q, 0, even, :] + g[q, 0, odd, :] for q in range(19)], axis=0)
        total = moved(part, matrix[...])
        for half in range(2):
            rows = pl.ds(8 + 16 * i + 8 * half, 8)
            v = relax([total[16 * q + 8 * half : 16 * q + 8 * half + 8] for q in range(19)], 1.0 - scale, scale)
            v = [jnp.where(covered, v[q], zone[q, rows, :]) for q in range(19)]
            post = collided(v, zone[19, rows, :], 2)
            for q in range(19):
                zpost[q, rows, :] = post[q]
            pack_flows(post, flows, first + 16 * i + 8 * half)


def finest_cycle(g, pa, pb, wide, first, groups):
    mask = interface_mask(3, 0)

    def substep(v, row, dest):
        v = [jnp.where(mask, wide[q, 0, pl.ds(row, 8), :], v[q]) for q in range(19)]
        post = collided(v, g[19, 0, pl.ds(row, 8), :], 3)
        for q in range(19):
            dest[q, 0, pl.ds(row, 8), :] = post[q]

    row_loop(first, groups, lambda row: substep([g[q, 0, pl.ds(row, 8), :] for q in range(19)], row, pa))
    row_loop(first, groups, lambda row: substep(pulled(pa, 3, row, [0], True)[0], row, pb))


def finest_role(own, flags, low, high, center, left, right, g, zpost, flows):
    def scoped(pa, pb, wide, zone, widen3, restrict3):
        widen3[...] = widen_matrix(3)
        restrict3[...] = restrict_chunk(3, 0)
        load_level(3, own, flags, low, high, g)
        load_zone(2, zone, 16, center, left, right, 8, 48)
        covered, rim = zone_masks(2, 0)
        interface_values(None, zone, rim, widen3, wide)
        for cycle in range(3):
            first, groups = (PAD, 12) if cycle < 2 else (PAD + 8, 10)

            def step_out(row):
                v = pulled(pb, 3, row, [0])[0]
                for q in range(19):
                    g[q, 0, pl.ds(row, 8), :] = v[q]

            finest_cycle(g, pa, pb, wide, first, groups)
            row_loop(first, groups, step_out)
            restrict_and_collide(g, zone, covered, restrict3, zpost, flows, 48 * cycle)
            if cycle < 2:
                interface_values(zpost, zone, rim, widen3, wide)

    rows = ROWS[3]
    pl.run_scoped(
        scoped,
        pltpu.VMEM((19, 1, rows, LANES), F32),
        pltpu.VMEM((19, 1, rows, LANES), F32),
        pltpu.VMEM((19, 1, rows, LANES), F32),
        pltpu.VMEM((20, 64, LANES), F32),
        pltpu.VMEM((2 * LANES, LANES), BF16),
        pltpu.VMEM((2 * LANES, LANES), BF16),
    )


def last_cycle_kernel(g, zpost, state, means, far_first, far_coarse, matrices):
    row0, n = ROW0[3], OWN[3]

    @pl.when(lax.axis_index("level") == 2)
    def _():
        for k, (q, c) in enumerate(FLOW_CHUNKS):
            matrices[:, pl.ds(k * LANES, LANES)] = flow_chunk(q, c)
        for half in range(2):
            for c in range(2):
                matrices[:, pl.ds((LATE_AT + 2 * half + c) * LANES, LANES)] = late_chunk(half, c)
            matrices[:, pl.ds((LATE_AT + 4 + half) * LANES, LANES)] = late_mean_matrix(half, False)

    @pl.when(lax.axis_index("level") == 1)
    def _():
        for half in range(2):
            matrices[:, pl.ds(2 * half * LANES, 2 * LANES)] = late_back_chunk(half)

    @pl.when(lax.axis_index("level") == 0)
    def _():
        matrices[:, pl.ds(0, LANES)] = mean_back_matrix()
        matrices[:, pl.ds(LANES, 4 * LANES)] = spread_covered_matrix()

    @pl.when(lax.axis_index("level") == 3)
    def _():
        def scoped(pa, pb, wide, flat, spread, out, pairs, value, scratch, widen3):
            _, rim = zone_masks(2, 0)

            widen3[...] = widen_matrix(3)
            interface_values(zpost, None, rim, widen3, wide)
            finest_cycle(g, pa, pb, wide, PAD + 8, 10)

            def step_out(row):
                v = pulled(pb, 3, row, [0])[0]
                for q in range(19):
                    out[q, 0, pl.ds(row - row0, 8), :] = v[q]

            row_loop(row0, n // 8, step_out)
            for q in range(19):
                flat[q, pl.ds(0, 32), :] = (
                    out[q, 0, pl.ds(0, 32, stride=2), :] + out[q, 0, pl.ds(1, 32, stride=2), :]
                )
            total = None
            for i in range(4):
                part = jnp.concatenate(
                    [flat[q, pl.ds(8 * i, 8), :] for q in range(19)] + [jnp.zeros((8, LANES), F32)], axis=0
                )
                part = moved(part, compact_chunk(i))
                total = part if total is None else total + part
            scale = child_scale(3)
            v = relax([total[8 * q : 8 * q + 8] for q in range(19)], 1.0 - scale, scale)
            for q in range(19):
                means[pl.ds(8 * q, 8), :] = v[q]
            means[pl.ds(152, 8), :] = jnp.zeros((8, LANES), F32)
            pairs[...] = jnp.zeros(pairs.shape, F32)
            for q in range(19):
                pairs[pl.ds(4 * q, 4), :] = (
                    means[pl.ds(8 * q, 4, stride=2), :] + means[pl.ds(8 * q + 1, 4, stride=2), :]
                )
            for odd in range(2):
                scratch[pl.ds(0, 80), :] = moved(pairs[...], deep_matrix(odd))
                for q in range(19):
                    value[pl.ds(8 * q + 4 * odd, 4), :] = scratch[pl.ds(4 * q, 4), :]
            scale = child_scale(2)
            v = relax([value[pl.ds(8 * q, 8), :] for q in range(19)], 1.0 - scale, scale)
            deep = deep_late(lanes() & 63)
            for q in range(19):
                value[pl.ds(8 * q, 8), :] = jnp.where(deep, v[q], 0.0)
            value[pl.ds(152, 8), :] = jnp.zeros((8, LANES), F32)
            lane = lanes()
            for plane in range(3):
                total = jnp.zeros((8, LANES), F32)
                for k in range(8):
                    q = 8 * plane + k
                    if q < 19:
                        part = pltpu.roll(value[pl.ds(8 * q, 8), :], (8 * k - 4) % LANES, 1)
                        total = jnp.where(((lane & 63) >> 3) == k, part, total)
                far_first[pl.ds(8 * plane, 8), :] = total
            late_means(value, [late_mean_matrix(half, True) for half in range(2)], flat.at[:, pl.ds(0, 8)], spread.at[pl.ds(0, 20), pl.ds(0, 8)])
            packed_planes([flat[q, pl.ds(0, 8), :] for q in range(19)], far_coarse, 32)
            store_level(3, out, 0, state)

        rows = ROWS[3]
        pl.run_scoped(
            scoped,
            pltpu.VMEM((19, 1, rows, LANES), F32),
            pltpu.VMEM((19, 1, rows, LANES), F32),
            pltpu.VMEM((19, 1, rows, LANES), F32),
            pltpu.VMEM((19, 48, LANES), F32),
            pltpu.VMEM((20, 48, LANES), F32),
            pltpu.VMEM((19, 1, n, LANES), F32),
            pltpu.VMEM((80, LANES), F32),
            pltpu.VMEM((160, LANES), F32),
            pltpu.VMEM((80, LANES), F32),
            pltpu.VMEM((2 * LANES, LANES), BF16),
        )


def restrict_pairs(level, g, first, count, skip, flat):
    flat[...] = jnp.zeros(flat.shape, F32)
    for q in range(19):
        for c in range(CHUNKS[level]):
            flat[q, c, pl.ds(skip, count), :] = (
                g[q, c, pl.ds(first, count, stride=2), :] + g[q, c, pl.ds(first + 1, count, stride=2), :]
            )
    rows = flat.shape[2]
    total = None
    for c in range(CHUNKS[level]):
        part = moved(flat[:, c].reshape(flat.shape[0] * rows, LANES), restrict_chunk(level, c))
        total = part if total is None else total + part
    return total.reshape(flat.shape[0], rows, LANES)


def second_role(own, flags, low, high, center, left, right, keep_post, keep_wide, early, ring):
    level, row0 = 2, ROW0[2]
    first = row0 - 8

    def scoped(g, wide, zone, zpost, conv, spread, flat):
        load_level(level, own, flags, low, high, g)
        load_zone(1, zone, 16, center, left, right, 8, 32)
        covered, rim = zone_masks(1, 0)
        keep_post[19] = g[19]
        convert_zone(1, zone, 8, 4, rim, conv)
        widen(conv, widen_matrix(2), 2, 4, 24, wide, spread, first)
        collide_rows(level, g, g, wide, keep_post, first, 6)
        pull_rows(level, keep_post, g, first, 6)
        collide_rows(level, g, g, wide, keep_post, first, 6)
        pull_rows(level, keep_post, g, first, 6)
        spread[...] = restrict_pairs(level, g, first, 24, 4, flat)
        scale = child_scale(2)

        def restrict(i):
            row = pl.multiple_of(8 * i, 8)
            v = relax([spread[q, pl.ds(row, 8), :] for q in range(19)], 1.0 - scale, scale)
            v = [jnp.where(covered, v[q], zone[q, pl.ds(8 + row, 8), :]) for q in range(19)]
            post = collided(v, zone[19, pl.ds(8 + row, 8), :], 1)
            for q in range(19):
                zpost[q, pl.ds(8 + row, 8), :] = post[q]

        loop(4, restrict)

        def zone_pull(row):
            v = zone_pulled(zpost, 1, row)
            for q in range(19):
                zone[q, pl.ds(row, 8), :] = v[q]

        row_loop(8, 4, zone_pull)
        convert_zone(1, zone, 8, 4, rim, conv)
        widen(conv, widen_matrix(2), 2, 4, 24, keep_wide, spread, first)
        near, _ = zone_masks(1, 1)
        for q in range(19):
            for i in range(2):
                rows = pl.ds(8 * i, 8)
                early[q, rows, :] = jnp.where(near, zone[q, pl.ds(16 + 8 * i, 8), :], 0.0)
        mean = moved(early[...].reshape(19 * 16, LANES), mean_ring_matrix())
        spread[:, pl.ds(0, 16), :] = mean.reshape(19, 16, LANES)
        for q in range(19):
            ring[q] = spread[q, pl.ds(0, 8, stride=2), :] + spread[q, pl.ds(1, 8, stride=2), :]

    pl.run_scoped(
        scoped,
        pltpu.VMEM((20, 2, ROWS[2], LANES), F32),
        pltpu.VMEM((19, 2, ROWS[2], LANES), F32),
        pltpu.VMEM((20, 48, LANES), F32),
        pltpu.VMEM((19, 48, LANES), F32),
        pltpu.VMEM((19, 32, LANES), F32),
        pltpu.VMEM((19, 32, LANES), F32),
        pltpu.VMEM((19, 2, 32, LANES), F32),
    )


def first_role(own, flags, low, high, center, left, right, state, early):
    level, row0, n = 1, ROW0[1], OWN[1]
    first = row0 - 8

    def scoped(g, post, wide, zone, conv, spread, flat):
        load_level(level, own, flags, low, high, g)
        load_zone(0, zone, 12, center, left, right, 8, 16)
        y, z = zone_cell(0, lanes())
        convert_zone(0, zone, 8, 2, (z == 7) | (y == Y_LOW) | (y == Y_HIGH), conv)
        widen(conv, widen_matrix(1), 1, 0, 16, wide, spread, first)
        collide_rows(level, g, g, wide, post, first, 4)
        pull_rows(level, post, g, first, 4)
        collide_rows(level, g, g, wide, post, first, 4)
        pull_rows(level, post, g, row0, n // 8)
        store_level(level, g, row0, state)
        total = None
        for c in range(CHUNKS[1]):
            part = moved(g[pl.ds(0, 19), c, pl.ds(row0, n), :].reshape(19 * n, LANES), mean_chunk(c))
            total = part if total is None else total + part
        flat[...] = total.reshape(19, n, LANES)
        for q in range(19):
            early[q, pl.ds(0, 8), :] = flat[q, pl.ds(0, 8, stride=2), :] + flat[q, pl.ds(1, 8, stride=2), :]

    pl.run_scoped(
        scoped,
        pltpu.VMEM((20, 4, ROWS[1], LANES), F32),
        pltpu.VMEM((19, 4, ROWS[1], LANES), F32),
        pltpu.VMEM((19, 4, ROWS[1], LANES), F32),
        pltpu.VMEM((20, 32, LANES), F32),
        pltpu.VMEM((19, 16, LANES), F32),
        pltpu.VMEM((19, 16, LANES), F32),
        pltpu.VMEM((19, n, LANES), F32),
    )


def coarse_role(own, flags, low, high, state):
    level, row0 = 0, ROW0[0]

    def scoped(g, post):
        load_level(level, own, flags, low, high, g)
        collide_rows(level, g, g, None, post, row0 - 8, 3)
        pull_rows(level, post, g, row0, 1)
        store_level(level, g, row0, state)

    pl.run_scoped(
        scoped,
        pltpu.VMEM((20, 8, ROWS[0], LANES), F32),
        pltpu.VMEM((19, 8, ROWS[0], LANES), F32),
    )


def main_kernel(
    own, flags, low, high, center, left, right,
    state, fine, fine_post, flows, keep_post, keep_wide, early, ring,
):
    me = lax.axis_index("level")
    arrived = (own, flags, low, high, center, left, right)

    @pl.when(me == 3)
    def _():
        finest_role(*arrived, fine, fine_post, flows)

    @pl.when(me == 2)
    def _():
        second_role(*arrived, keep_post, keep_wide, early, ring)

    @pl.when(me == 1)
    def _():
        first_role(*arrived, state, early)

    @pl.when(me == 0)
    def _():
        coarse_role(own, flags, low, high, state)


def flow_kernel(flows, keep_post, keep_wide, ring, matrices, result, late, late_mean):
    level, row0 = 2, ROW0[2]
    first = row0 - 8

    @pl.when(lax.axis_index("level") == 2)
    def _():
        def scoped(other, post, override, flat, value, scratch):
            total = moved(flows[...], matrices[:, pl.ds(0, LATE_AT * LANES)])
            for k in range(len(FLOW_CHUNKS)):
                override[k] = total[:, k * LANES : (k + 1) * LANES]
            outward = []
            for q, c in FLOW_CHUNKS:
                y, z = cell_of(2, lanes() + c * LANES)
                outward.append(flow_mask(q, y, z))

            def overridden(c, row, cycle, v):
                v = list(v)
                for k, (q, chunk) in enumerate(FLOW_CHUNKS):
                    if chunk == c:
                        value = override[k, pl.ds(48 * cycle + row - first, 8), :]
                        v[q] = jnp.where(outward[k], value, v[q])
                return v

            masks = [interface_mask(level, c) for c in range(2)]

            def begin(row):
                for c in range(2):
                    v = overridden(c, row, 0, [keep_post[q, c, pl.ds(row, 8), :] for q in range(19)])
                    for q in range(19):
                        post[q, c, pl.ds(row, 8), :] = v[q]

            row_loop(first, 6, begin)
            for cycle, source, dest in ((1, post, other), (2, other, post)):

                def body(row, cycle=cycle, source=source, dest=dest):
                    for c, v in enumerate(pulled(source, level, row, range(2))):
                        v = [jnp.where(masks[c], keep_wide[q, c, pl.ds(row, 8), :], v[q]) for q in range(19)]
                        v = collided(v, keep_post[19, c, pl.ds(row, 8), :], level)
                        v = overridden(c, row, cycle, v)
                        for q in range(19):
                            dest[q, c, pl.ds(row, 8), :] = v[q]

                row_loop(first, 6, body)

            def last(row):
                for c, v in enumerate(pulled(post, level, row, range(2))):
                    for q in range(19):
                        result[q, c, pl.ds(row - row0, 8), :] = v[q]

            row_loop(row0, 4, last)
            for q in range(19):
                for c in range(2):
                    flat[c, q] = result[q, c, pl.ds(0, 16, stride=2), :] + result[q, c, pl.ds(1, 16, stride=2), :]
            flat[:, 19] = jnp.zeros((2, 16, LANES), F32)
            total = None
            for half in range(2):
                for c in range(2):
                    part = moved(
                        flat[c, :, pl.ds(8 * half, 8), :].reshape(160, LANES),
                        matrices[:, pl.ds((LATE_AT + 2 * half + c) * LANES, LANES)],
                    )
                    total = part if total is None else total + part
            scale = child_scale(2)
            v = relax([total[8 * q : 8 * q + 8] for q in range(19)], 1.0 - scale, scale)
            for q in range(19):
                late[pl.ds(8 * q, 8), :] = v[q]
            late[pl.ds(152, 8), :] = jnp.zeros((8, LANES), F32)
            late_means(
                late, [matrices[:, pl.ds((LATE_AT + 4 + half) * LANES, LANES)] for half in range(2)], value, scratch
            )
            packed_planes([value[q] + ring[q] for q in range(19)], late_mean, 32)

        pl.run_scoped(
            scoped,
            pltpu.VMEM((19, 2, ROWS[2], LANES), F32),
            pltpu.VMEM((19, 2, ROWS[2], LANES), F32),
            pltpu.VMEM((len(FLOW_CHUNKS), 144, LANES), F32),
            pltpu.VMEM((2, 20, 16, LANES), F32),
            pltpu.VMEM((19, 8, LANES), F32),
            pltpu.VMEM((20, 8, LANES), F32),
        )


def prepare_kernel(early, far, far_coarse, means, matrices, covered, near):
    me = lax.axis_index("level")

    @pl.when(me == 2)
    def _():
        for i in range(4):
            total = moved(means[...], spread_chunk(i))
            for c in range(2):
                covered[2 * i + c] = total[:, c * LANES : (c + 1) * LANES]

    @pl.when(me == 1)
    def _():
        total = moved(early[...].reshape(19 * 16, LANES), spread_zone_matrix())
        for c in range(4):
            near[c] = total[:, c * LANES : (c + 1) * LANES]

    @pl.when(me == 0)
    def _():
        def scoped(value):
            lane = lanes()
            for q in range(19):
                rows = pl.ds(8 * (q // 4), 8)
                part = far[rows, :] + far_coarse[rows, :]
                if q % 4:
                    part = pltpu.roll(part, LANES - 32 * (q % 4), 1)
                value[q] = jnp.where(lane < 32, part, 0.0)
            value[19] = jnp.zeros((8, LANES), F32)
            total = moved(value[...].reshape(160, LANES), matrices[:, pl.ds(0, LANES)])
            scale = child_scale(1)
            v = relax(
                [early[q, pl.ds(0, 8), :] + total[8 * q : 8 * q + 8] for q in range(19)],
                1.0 - scale,
                scale,
            )
            for q in range(19):
                value[q] = v[q]
            total = moved(value[...].reshape(160, LANES), matrices[:, pl.ds(LANES, 4 * LANES)])
            for c in range(4):
                covered[c] = total[:, c * LANES : (c + 1) * LANES]

        pl.run_scoped(scoped, pltpu.VMEM((20, 8, LANES), F32))


def finish_kernel(old_state, result, third_state, late, far, covered_values, near, matrices, state):
    me = lax.axis_index("level")

    @pl.when(me == 3)
    def _():
        state[...] = third_state[...]

    @pl.when(me == 2)
    def _():
        def scoped(g):
            for c in range(2):
                y, z = cell_of(2, lanes() + c * LANES)
                covered = (y >= Y_LOW) & (y <= Y_HIGH) & (z <= 1)

                def insert(q, c=c, covered=covered):
                    for i in range(4):
                        rows = pl.ds(8 * i, 8)
                        value = covered_values[2 * i + c, pl.ds(pl.multiple_of(8 * q, 8), 8), :]
                        g[q, c, rows, :] = jnp.where(covered, value, result[q, c, rows, :])

                loop(19, insert, 19)
            store_level(2, g, 0, state)

        pl.run_scoped(scoped, pltpu.VMEM((19, 2, OWN[2], LANES), F32))

    @pl.when(me == 1)
    def _():
        def scoped(inner, value):
            lane = lanes()
            deep = deep_late(lane & 63)
            for q in range(19):
                part = pltpu.roll(far[pl.ds(8 * (q // 8), 8), :], (4 - 8 * (q % 8)) % LANES, 1)
                value[pl.ds(8 * q, 8), :] = jnp.where(deep, part, late[pl.ds(8 * q, 8), :])
            value[pl.ds(152, 8), :] = jnp.zeros((8, LANES), F32)
            for half in range(2):
                total = moved(value[...], matrices[:, pl.ds(2 * half * LANES, 2 * LANES)])
                for c in range(2):
                    part = total[:, c * LANES : (c + 1) * LANES].reshape(20, 8, LANES)
                    inner[c, :, pl.ds(8 * half, 8), :] = part

            def one(q):
                for j in range(8):
                    c = j % 4
                    y, z = cell_of(1, lanes() + c * LANES)
                    columns = pl.ds(j * LANES, LANES)
                    rows = pl.ds(j // 4, 8, stride=2)
                    ring = near[c, pl.ds(16 * q + j // 4, 8, stride=2), :]
                    value = jnp.where(near_first(y, z), ring, old_state[q, :, columns])
                    if c in (1, 2):
                        value = jnp.where(covered_first(y, z), inner[c - 1, q, rows, :], value)
                    state[q, :, columns] = value

            loop(19, one)

        pl.run_scoped(
            scoped,
            pltpu.VMEM((2, 20, 16, LANES), F32),
            pltpu.VMEM((160, LANES), F32),
        )

    @pl.when(me == 0)
    def _():
        covered = (lanes() & 31) < 8

        def one(q):
            rows = pl.ds(pl.multiple_of(8 * q, 8), 8)
            for j in range(8):
                columns = pl.ds(j * LANES, LANES)
                value = old_state[q, :, columns]
                if 2 <= j < 6:
                    value = jnp.where(covered, covered_values[j - 2, rows, :], value)
                state[q, :, columns] = value

        loop(19, one, 19)


def call(kernel, shapes, args, micros):
    return pl.pallas_call(
        kernel,
        out_shape=[
            jax.ShapeDtypeStruct(s[:-1], BF16) if s[-1] is BF16 else jax.ShapeDtypeStruct(s, F32) for s in shapes
        ],
        in_specs=[pl.BlockSpec(memory_space=pltpu.VMEM)] * len(args),
        out_specs=[pl.BlockSpec(memory_space=pltpu.VMEM)] * len(shapes),
        cost_estimate=pl.CostEstimate(
            flops=int(micros * 1e9), bytes_accessed=int(micros * 3.6e6), transcendentals=0
        ),
        compiler_params=pltpu.CompilerParams(vmem_limit_bytes=24 * 1024 * 1024),
    )(*args)


def shards(populations, solid):
    if populations.shape[1:] != (19, SLAB, NY * NZ):
        raise ValueError("unexpected slab")
    own, flags = populations[0], solid[0].astype(F32)
    blocks = lax.axis_size("blocks")
    forward = [(i, (i + 1) % blocks) for i in range(blocks)]
    backward = [(i, (i - 1) % blocks) for i in range(blocks)]
    down = [(i, i + 1) for i in range(LEVELS - 1)]

    def diagonal(step):
        return [
            (level * blocks + b, (level + 1) * blocks + (b + step) % blocks)
            for level in range(LEVELS - 1)
            for b in range(blocks)
        ]

    both = ("level", "blocks")
    to_right, to_left, center, zone_right, zone_left = call(
        start_kernel,
        [(20, 16, LANES), (20, 16, LANES), (CENTER_ROWS, LANES), (PLANES + 1, 8, LANES), (PLANES + 1, 8, LANES)],
        [own, flags],
        1.5,
    )
    center = lax.ppermute(center, "level", down)
    left = lax.ppermute(zone_right, both, diagonal(1))
    right = lax.ppermute(zone_left, both, diagonal(-1))
    low = lax.ppermute(to_right, "blocks", forward)
    high = lax.ppermute(to_left, "blocks", backward)

    full = (19, SLAB, NY * NZ)
    state, fine, fine_post, flows, keep_post, keep_wide, early, ring = call(
        main_kernel,
        [
            full,
            (20, 1, ROWS[3], LANES),
            (19, 64, LANES),
            (144, LANES),
            (20, 2, ROWS[2], LANES),
            (19, 2, ROWS[2], LANES),
            (19, 16, LANES),
            (19, 8, LANES),
        ],
        [own, flags, low, high, center, left, right],
        8.0,
    )
    flows = lax.ppermute(flows, "level", [(3, 2)])
    early = lax.ppermute(early, "level", [(2, 1), (1, 0)])
    third_state, means, far_first, far_coarse, matrices = call(
        last_cycle_kernel,
        [full, (160, LANES), (40, LANES), (40, LANES), (2 * LANES, (LATE_AT + 6) * LANES, BF16)],
        [fine, fine_post],
        4.0,
    )
    far_coarse = lax.ppermute(far_coarse, "level", [(3, 0)])
    means = lax.ppermute(means, "level", [(3, 2)])
    result, late, late_mean = call(
        flow_kernel,
        [(19, 2, OWN[2], LANES), (160, LANES), (40, LANES)],
        [flows, keep_post, keep_wide, ring, matrices],
        2.5,
    )
    me = lax.axis_index("level")
    far = lax.ppermute(jnp.where(me == 3, far_first, late_mean), "level", [(3, 1), (2, 0)])
    late = lax.ppermute(late, "level", [(2, 1)])
    covered, near = call(
        prepare_kernel, [(8, 160, LANES), (4, 304, LANES)], [early, far, far_coarse, means, matrices], 4.0
    )
    (state,) = call(
        finish_kernel, [full], [state, result, third_state, late, far, covered, near, matrices], 1.0
    )
    return state[None]


def solution(mesh):
    in_specs = (P("level", None, "blocks", None), P("level", "blocks", None))
    out_specs = P("level", None, "blocks", None)
    return jax.shard_map(shards, mesh=mesh, in_specs=in_specs, out_specs=out_specs, check_vma=False)
```

```python
import jax
import jax.numpy as jnp
from jax import lax
from jax.experimental import pallas as pl
from jax.experimental.pallas import tpu as pltpu
from jax.sharding import PartitionSpec as P

NY = 32
NZ = 32
LEVELS = 4
SLAB = 8
LANES = 128
VELOCITY = (
    (0, 0, 0),
    (1, 0, 0),
    (-1, 0, 0),
    (0, 1, 0),
    (0, -1, 0),
    (0, 0, 1),
    (0, 0, -1),
    (1, 1, 0),
    (-1, -1, 0),
    (1, -1, 0),
    (-1, 1, 0),
    (1, 0, 1),
    (-1, 0, -1),
    (1, 0, -1),
    (-1, 0, 1),
    (0, 1, 1),
    (0, -1, -1),
    (0, 1, -1),
    (0, -1, 1),
)
OPPOSITE = (0, 2, 1, 4, 3, 6, 5, 8, 7, 10, 9, 12, 11, 14, 13, 16, 15, 18, 17)
TAU_BASE = 1.0
F32 = jnp.float32
BF16 = jnp.bfloat16

PAD = 8
MARGIN = (8, 8, 8, 16)
FACTOR = (1, 2, 4, 8)
CHUNKS = (8, 4, 2, 1)
DEPTH = (32, 16, 8, 4)
OWN = tuple(SLAB * f for f in FACTOR)
ROW0 = tuple(PAD + m for m in MARGIN)
ROWS = tuple(OWN[l] + 2 * ROW0[l] for l in range(LEVELS))

Y_LOW = NY // 4
Y_HIGH = 3 * NY // 4 - 1


def zone_lane(level, y, z):
    if level == 0:
        return (y - 8) * 8 + z
    if level == 1:
        return z * 20 + y - 6
    return z * 25 + y - 4


ZONE_PITCH = (None, 20, 25)


def level_lane(level, y, z):
    return y * DEPTH[level] + z


def made(columns, weight, holds):
    row = lax.broadcasted_iota(jnp.int32, (LANES, columns), 0)
    column = lax.broadcasted_iota(jnp.int32, (LANES, columns), 1)
    matrix = jnp.where(holds(row, column), weight, 0.0).astype(BF16)
    return jnp.concatenate([matrix, matrix], axis=0)


def cell_of(level, lane):
    return lane >> (DEPTH[level].bit_length() - 1), lane & (DEPTH[level] - 1)


def message_cell(level, y, z):
    if level == 0:
        side = (z < 7) & ((y == 8) | (y == 23))
        top = (z == 7) & (y >= 8) & (y <= 23)
        return jnp.where(z == 7, y - 8, 16 + 2 * z + (y == 23).astype(jnp.int32)), side | top
    if level == 1:
        outer = ((y >= 6) & (y <= 8)) | ((y >= 23) & (y <= 25))
        side = (z < 3) & outer
        top = (z >= 3) & (z <= 5) & (y >= 6) & (y <= 25)
        return jnp.where(z >= 3, (z - 3) * 20 + y - 6, 60 + z * 6 + jnp.where(y < 9, y - 6, y - 20)), side | top
    outer = ((y >= 5) & (y <= 8)) | ((y >= 23) & (y <= 26))
    side = (z == 0) & outer
    top = (z >= 1) & (z <= 4) & (y >= 5) & (y <= 26)
    return jnp.where(z >= 1, (z - 1) * 22 + y - 5, 88 + jnp.where(y < 9, y - 5, y - 19)), side | top


def pack_chunk(level, c):
    def holds(row, column):
        y, z = cell_of(level, row + c * LANES)
        lane, sent = message_cell(level, y, z)
        return sent & (column == lane)

    return made(LANES, 1.0, holds)


def flag_chunk(level, c):
    def holds(row, column):
        y, z = cell_of(level, row + c * LANES)
        if level == 0:
            inside = (y >= 8) & (y <= 23) & (z <= 7)
        elif level == 1:
            inside = (y >= 6) & (y <= 25) & (z <= 5)
        else:
            inside = (y >= 5) & (y <= 26) & (z <= 4)
        return inside & (column == zone_lane(level, y, z))

    return made(LANES, 1.0, holds)


def fold_chunk(level, c):
    def holds(row, column):
        y, z = cell_of(level, row + c * LANES)
        lane, sent = message_cell(level, y, z)
        return sent & ((column & (LANES - 1)) == 96 + (lane & 31)) & ((column >> 7) == (lane >> 5))

    return made(3 * LANES, 1.0, holds)


def unpack_matrix(level, k):
    def holds(row, column):
        y, z = zone_cell(level, column & (LANES - 1))
        lane, sent = message_cell(level, y, z)
        folded = (row == 96 + (lane & 31)) & ((lane >> 5) == k)
        own = row == lane
        return sent & (((column < LANES) & own) | ((column >= LANES) & folded))

    return made(2 * LANES, 1.0, holds)


def widen_matrix(child):
    def holds(row, column):
        y, z = cell_of(child, column)
        edge = (y == 0) | (y == NY - 1) | (z == DEPTH[child] - 1)
        return edge & (row == zone_lane(child - 1, 8 + (y >> 1), z >> 1))

    return made(CHUNKS[child] * LANES, 1.0, holds)


def restrict_chunk(child, c):
    def holds(row, column):
        y, z = cell_of(child, row + c * LANES)
        return column == zone_lane(child - 1, 8 + (y >> 1), z >> 1)

    return made(LANES, 0.125, holds)


def compact_chunk(i):
    def holds(row, column):
        y, z = cell_of(3, row)
        return column == 32 * i + (y >> 1) * 2 + (z >> 1)

    return made(LANES, 0.125, holds)


def spread_chunk(i):
    def holds(row, column):
        y, z = cell_of(2, column)
        return (y >= Y_LOW) & (y <= Y_HIGH) & (z <= 1) & (row == 32 * i + (y - Y_LOW) * 2 + z)

    return made(2 * LANES, 1.0, holds)


def near_first(y, z):
    return (y >= Y_LOW - 1) & (y <= Y_HIGH + 1) & (z <= 4)


def mean_chunk(c):
    def holds(row, column):
        y, z = cell_of(1, row + c * LANES)
        return jnp.logical_not(near_first(y, z)) & (column == zone_lane(0, 8 + (y >> 1), z >> 1))

    return made(LANES, 0.125, holds)


def zone_cell(level, lane):
    if level == 0:
        return 8 + (lane >> 3), lane & 7
    pitch, first = ZONE_PITCH[level], 6 if level == 1 else 4
    z = sum((lane >= pitch * k).astype(jnp.int32) for k in range(1, 7))
    return lane - pitch * z + first, z


def covered_first(y, z):
    return (y >= Y_LOW) & (y <= Y_HIGH) & (z <= 3)


def mean_lane(y, z):
    return y - 11 + 10 * z


def mean_ring_matrix():
    def holds(row, column):
        y, z = zone_cell(1, row)
        ring = near_first(y, z) & jnp.logical_not(covered_first(y, z))
        return ring & (column == mean_lane(8 + (y >> 1), z >> 1))

    return made(LANES, 0.125, holds)


def late_chunk(half, c):
    def holds(row, column):
        y, z = cell_of(2, row + c * LANES)
        return column == 64 * half + (z >> 1) * 16 + (y >> 1)

    return made(LANES, 0.125, holds)


def late_back_chunk(half):
    def holds(row, column):
        y, z = cell_of(1, column + LANES)
        return covered_first(y, z) & (row == 64 * half + z * 16 + y - Y_LOW)

    return made(2 * LANES, 1.0, holds)


def deep_late(cell):
    return (cell >= 4) & (cell < 12)


def late_mean_matrix(half, deep):
    def holds(row, column):
        cell = row - 64 * half
        inside = (cell >= 0) & (cell < 64)
        inside = inside & (deep_late(cell) if deep else jnp.logical_not(deep_late(cell)))
        return inside & (column == mean_lane(12 + ((cell & 15) >> 1), cell >> 5))

    return made(LANES, 0.125, holds)


def deep_matrix(odd):
    def holds(row, column):
        i, y = row >> 5, (row & 31) >> 1
        return ((i & 1) == odd) & (column == 64 * (i >> 1) + 4 + (y >> 1))

    return made(LANES, 0.125, holds)


def mean_back_matrix():
    def holds(row, column):
        z = (row >= 10).astype(jnp.int32) + (row >= 20).astype(jnp.int32)
        return (row < 30) & (column == zone_lane(0, row - 10 * z + 11, z))

    return made(LANES, 1.0, holds)


def packed_planes(source, out, width):
    lane = lanes()
    per = LANES // width
    for plane in range(-(-19 // per)):
        total = jnp.zeros((8, LANES), F32)
        for k in range(per):
            q = per * plane + k
            if q < 19:
                part = source[q] if k == 0 else pltpu.roll(source[q], width * k, 1)
                total = jnp.where((lane >= width * k) & (lane < width * (k + 1)), part, total)
        out[pl.ds(8 * plane, 8), :] = total


def late_means(late, weights, value, scratch):
    for half in range(2):
        scratch[...] = moved(late[...], weights[half]).reshape(20, 8, LANES)
        for q in range(19):
            value[q, pl.ds(4 * half, 4), :] = (
                scratch[q, pl.ds(0, 4, stride=2), :] + scratch[q, pl.ds(1, 4, stride=2), :]
            )


def spread_zone_matrix():
    def holds(row, column):
        y, z = cell_of(1, column)
        return near_first(y, z) & (row == zone_lane(1, y, z))

    return made(4 * LANES, 1.0, holds)


def spread_covered_matrix():
    def holds(row, column):
        y, z = cell_of(0, column + 2 * LANES)
        return (z < 8) & (row == zone_lane(0, y, z))

    return made(4 * LANES, 1.0, holds)


Z_OUT = (5, 11, 14, 15, 18)
Y_DOWN = (4, 8, 9, 16, 18)
Y_UP = (3, 7, 10, 15, 17)
FLOW_DIRECTIONS = tuple(sorted(set(Z_OUT + Y_DOWN + Y_UP)))


def flow_mask(q, y, z):
    mask = None
    if q in Z_OUT:
        mask = (z == 1) & (y >= Y_LOW) & (y <= Y_HIGH)
    for group, edge in ((Y_DOWN, Y_LOW), (Y_UP, Y_HIGH)):
        if q in group:
            cells = (y == edge) & (z <= 1)
            mask = cells if mask is None else mask | cells
    return mask


FLOW_CHUNKS = tuple(
    (q, c) for q in FLOW_DIRECTIONS for c in range(2) if q in Z_OUT or q in (Y_DOWN, Y_UP)[c]
)


LATE_AT = len(FLOW_CHUNKS)


def flow_chunk(q, c):
    def holds(row, column):
        y, z = cell_of(2, column + c * LANES)
        source = None
        if q in Y_DOWN:
            source = 80 + Y_DOWN.index(q) + 25 * z
        if q in Y_UP:
            source = 85 + Y_UP.index(q) + 25 * z
        if q in Z_OUT:
            over = 16 * Z_OUT.index(q) + y - Y_LOW
            source = over if source is None else jnp.where(z == 1, over, source)
        return flow_mask(q, y, z) & (row == source)

    return made(LANES, 1.0, holds)


def relaxation(level_id):
    return 2.0**level_id * (TAU_BASE - 0.5) + 0.5


def parent_scale(child):
    return relaxation(child) / (2.0 * relaxation(child - 1))


def child_scale(child):
    return 2.0 * relaxation(child - 1) / relaxation(child)


def relax(v, a, b):
    s = [None] + [v[2 * k - 1] + v[2 * k] for k in range(1, 10)]
    d = [None] + [v[2 * k - 1] - v[2 * k] for k in range(1, 10)]
    rho = (
        (1.0 / 3.0) * v[0]
        + (1.0 / 18.0) * (s[1] + s[2] + s[3])
        + (1.0 / 36.0) * ((s[4] + s[5]) + (s[6] + s[7]) + (s[8] + s[9]))
    )
    mx = (1.0 / 18.0) * d[1] + (1.0 / 36.0) * ((d[4] + d[5]) + (d[6] + d[7]))
    my = (1.0 / 18.0) * d[2] + (1.0 / 36.0) * ((d[4] - d[5]) + (d[8] + d[9]))
    mz = (1.0 / 18.0) * d[3] + (1.0 / 36.0) * ((d[6] - d[7]) + (d[8] - d[9]))
    inv = 1.0 / rho
    ux, uy, uz = mx * inv, my * inv, mz * inv
    ra = a * rho
    base = ra - (1.5 * ra) * (ux * ux + uy * uy + uz * uz)
    r45 = 4.5 * ra
    ra3 = 3.0 * ra

    def kept(q):
        return v[q] if b == 1.0 else b * v[q]

    out = [base if b == 0.0 else base + kept(0)]
    cus = (ux, uy, uz, ux + uy, ux - uy, ux + uz, ux - uz, uy + uz, uy - uz)
    for k in range(1, 10):
        cu = cus[k - 1]
        even = base + r45 * (cu * cu)
        odd = ra3 * cu
        plus, minus = even + odd, even - odd
        if b != 0.0:
            plus, minus = plus + kept(2 * k - 1), minus + kept(2 * k)
        out += [plus, minus]
    return out


def collided(v, solid, level):
    inv_tau = 1.0 / relaxation(level)
    relaxed = relax(v, inv_tau, 1.0 - inv_tau)
    flag = solid != 0.0
    return [jnp.where(flag, v[OPPOSITE[q]], relaxed[q]) for q in range(19)]


def lanes():
    return lax.broadcasted_iota(jnp.int32, (8, LANES), 1)


def interface_mask(level, c):
    lane = lanes()
    nz = DEPTH[level]
    mask = (lane & (nz - 1)) == nz - 1
    if c == 0:
        mask = mask | (lane < nz)
    if c == CHUNKS[level] - 1:
        mask = mask | (lane >= LANES - nz)
    return mask


def pulled(post, level, row, chunks, interface_next=False):
    lane = lanes()
    nz, count = DEPTH[level], CHUNKS[level]
    out = [[] for _ in chunks]
    for q in range(19):
        cx, cy, cz = VELOCITY[q]
        shift = cy * nz + cz
        rolled = {}

        def moved_chunk(c):
            if c not in rolled:
                value = post[q, c, pl.ds(row - cx, 8), :]
                rolled[c] = pltpu.roll(value, shift % LANES, 1) if shift != 0 else value
            return rolled[c]

        for place, c in enumerate(chunks):
            value = moved_chunk(c)
            outside = None
            if cy == 1:
                if c > 0:
                    value = jnp.where(lane < shift, moved_chunk(c - 1), value)
                else:
                    outside = lane < nz
            if cy == -1:
                if c < count - 1:
                    value = jnp.where(lane >= LANES + shift, moved_chunk(c + 1), value)
                else:
                    outside = lane >= LANES - nz
            if cz != 0:
                edge = (lane & (nz - 1)) == (0 if cz == 1 else nz - 1)
                outside = edge if outside is None else outside | edge
            if interface_next:
                outside = (lane & (nz - 1)) == 0 if cz == 1 else None
            if outside is not None:
                value = jnp.where(outside, post[OPPOSITE[q], c, pl.ds(row, 8), :], value)
            out[place].append(value)
    return out


def zone_pulled(post, level, row):
    lane = lanes()
    pitch = ZONE_PITCH[level]
    out = []
    for q in range(19):
        cx, cy, cz = VELOCITY[q]
        shift = cz * pitch + cy
        value = post[q, pl.ds(row - cx, 8), :]
        if shift != 0:
            value = pltpu.roll(value, shift % LANES, 1)
            if cz == 1:
                value = jnp.where(lane < pitch, post[OPPOSITE[q], pl.ds(row, 8), :], value)
        out.append(value)
    return out


def zone_masks(level, reach):
    lane = lanes()
    pitch, first = ZONE_PITCH[level], 6 if level == 1 else 4
    top = DEPTH[level] // 4 - 1
    inside = None
    rim = None
    for z in range(top + reach + 1):
        start = z * pitch - first
        row = (lane >= start + Y_LOW - reach) & (lane <= start + Y_HIGH + reach)
        inside = row if inside is None else inside | row
        if z < top:
            row = (lane == start + Y_LOW) | (lane == start + Y_HIGH)
        elif z == top:
            row = (lane >= start + Y_LOW) & (lane <= start + Y_HIGH)
        else:
            continue
        rim = row if rim is None else rim | row
    return inside, rim


def loop(count, body, unroll=None):
    def step(i, carry):
        body(i)
        return carry

    if unroll is None:
        unroll = max(u for u in range(1, 13) if count % u == 0)
    lax.fori_loop(0, count, step, 0, unroll=unroll)


def row_loop(start, count, body):
    loop(count, lambda i: body(pl.multiple_of(start + 8 * i, 8)))


def moved(value, matrix):
    high = value.astype(BF16)
    low = (value - high.astype(F32)).astype(BF16)
    return jnp.dot(jnp.concatenate([high, low], axis=1), matrix, preferred_element_type=F32)


def load_level(level, own, flags, low, high, buf):
    factor, count, row0 = FACTOR[level], CHUNKS[level], ROW0[level]
    n = OWN[level]

    def one(q, source):
        for j in range(8):
            buf[q, j % count, pl.ds(row0 + j // count, 8, stride=factor), :] = source(j)
        if low is not None:
            for c in range(count):
                rows = pl.ds(c, 2 * factor, stride=count) if count > 1 else pl.ds(0, 2 * factor)
                buf[q, c, pl.ds(row0 - 2 * factor, 2 * factor), :] = low[q, rows, :]
                buf[q, c, pl.ds(row0 + n, 2 * factor), :] = high[q, rows, :]

    loop(19, lambda q: one(q, lambda j: own[q, :, pl.ds(j * LANES, LANES)]))
    one(19, lambda j: flags[:, pl.ds(j * LANES, LANES)])


def store_level(level, buf, row0, out):
    factor, count = FACTOR[level], CHUNKS[level]

    def one(q):
        for j in range(8):
            out[q, :, pl.ds(j * LANES, LANES)] = buf[
                q, j % count, pl.ds(row0 + j // count, 8, stride=factor), :
            ]

    loop(19, one)


def collide_rows(level, source, solid, wide, dest, start, groups):
    masks = [interface_mask(level, c) for c in range(CHUNKS[level])]

    def body(row):
        for c in range(CHUNKS[level]):
            v = [source[q, c, pl.ds(row, 8), :] for q in range(19)]
            if wide is not None:
                v = [jnp.where(masks[c], wide[q, c, pl.ds(row, 8), :], v[q]) for q in range(19)]
            post = collided(v, solid[19, c, pl.ds(row, 8), :], level)
            for q in range(19):
                dest[q, c, pl.ds(row, 8), :] = post[q]

    row_loop(start, groups, body)


def pull_rows(level, post, dest, start, groups):
    def body(row):
        step = min(2, CHUNKS[level])
        for first in range(0, CHUNKS[level], step):
            chunks = range(first, first + step)
            for c, v in zip(chunks, pulled(post, level, row, chunks)):
                for q in range(19):
                    dest[q, c, pl.ds(row, 8), :] = v[q]

    row_loop(start, groups, body)


PLANES = 15
CENTER_ROWS = (PLANES + 1) * (OWN[2] + 2)


def load_zone(level, zone, zero_row, center, left, right, start, rows):
    n = OWN[level]

    def scoped(planes):
        planes[...] = jnp.zeros(planes.shape, F32)
        for p in range(PLANES + 1):
            planes[p, pl.ds(zero_row - 1, n + 2), :] = center[pl.ds(p * (OWN[2] + 2), n + 2), :]
            planes[p, pl.ds(zero_row - 7, 8), :] += left[p]
            planes[p, pl.ds(zero_row + n - 1, 8), :] += right[p]
        folded = None
        for k in range(3):
            part = jnp.concatenate([planes[3 * j + k, pl.ds(start, rows), :] for j in range(5)], axis=0)
            total = moved(part, unpack_matrix(level, k))
            for j in range(5):
                zone[3 * j + k, pl.ds(start, rows), :] = total[rows * j : rows * (j + 1), :LANES]
            folded = total[:, LANES:] if folded is None else folded + total[:, LANES:]
        for j in range(4):
            zone[PLANES + j, pl.ds(start, rows), :] = folded[rows * j : rows * (j + 1)]
        zone[19, pl.ds(start, rows), :] = planes[PLANES, pl.ds(start, rows), :]

    pl.run_scoped(scoped, pltpu.VMEM((PLANES + 1, *zone.shape[1:]), F32))


def convert_zone(level, zone, start, groups, rim, out):
    scale = parent_scale(level + 1)

    def body(i):
        row = pl.multiple_of(8 * i, 8)
        v = [zone[q, pl.ds(start + row, 8), :] for q in range(19)]
        v = relax(v, 1.0 - scale, scale)
        for q in range(19):
            out[q, pl.ds(row, 8), :] = v[q] if rim is None else jnp.where(rim, v[q], 0.0)

    loop(groups, body)


def widen(converted, matrix, child, skip, count, wide, spread, first):
    rows = converted.shape[1]
    value = moved(converted[...].reshape(19 * rows, LANES), matrix)
    for c in range(CHUNKS[child]):
        part = value[:, c * LANES : (c + 1) * LANES].reshape(19, rows, LANES)
        if count < rows:
            spread[pl.ds(0, 19)] = part
        for q in range(19):
            t = part[q] if count == rows else spread[q, pl.ds(skip, count), :]
            wide[q, c, pl.ds(first, count, stride=2), :] = t
            wide[q, c, pl.ds(first + 1, count, stride=2), :] = t


def start_kernel(own, flags, to_right, to_left, center, to_zone_right, to_zone_left):
    me = lax.axis_index("level")

    def halo(q, source):
        for j in range(8):
            to_left[q, pl.ds(j, 2, stride=8), :] = source(pl.ds(0, 2), j)
            to_right[q, pl.ds(j, 2, stride=8), :] = source(pl.ds(SLAB - 2, 2), j)

    loop(19, lambda q: halo(q, lambda rows, j: own[q, rows, pl.ds(j * LANES, LANES)]))
    halo(19, lambda rows, j: flags[rows, pl.ds(j * LANES, LANES)])

    for level in range(3):

        def push(level=level):
            n, row0, count, rows = OWN[level], ROW0[level], CHUNKS[level], ROWS[level]
            span = max(n + 16, 32)

            def scoped(buf, post, packed):
                post[...] = jnp.zeros(post.shape, F32)
                buf[19] = jnp.zeros(buf.shape[1:], F32)
                load_level(level, own, flags, None, None, buf)
                collide_rows(level, buf, buf, None, post, row0, n // 8)
                pull_rows(level, post, buf, row0 - 8, n // 8 + 2)
                def spanned(first, many, c):
                    return buf[pl.ds(first, many), c, pl.ds(row0 - 8, span), :].reshape(many * span, LANES)

                main = folded = solid = None
                for c in range(count):
                    part = moved(spanned(0, PLANES, c), pack_chunk(level, c))
                    main = part if main is None else main + part
                    part = moved(spanned(PLANES, 4, c), fold_chunk(level, c))
                    folded = part if folded is None else folded + part
                    part = moved(spanned(19, 1, c), flag_chunk(level, c))
                    solid = part if solid is None else solid + part
                for p in range(PLANES):
                    j, k = divmod(p, 3)
                    part = main[span * p : span * (p + 1)]
                    if j < 4:
                        part = part + folded[span * j : span * (j + 1), LANES * k : LANES * (k + 1)]
                    packed[p] = part
                packed[PLANES] = solid
                for p in range(PLANES + 1):
                    center[pl.ds(p * (OWN[2] + 2), n + 2), :] = packed[p, pl.ds(7, n + 2), :]
                    to_zone_right[p] = packed[p, pl.ds(n + 1, 8), :]
                    to_zone_left[p] = packed[p, pl.ds(7, 8), :]

            pl.run_scoped(
                scoped,
                pltpu.VMEM((20, count, rows, LANES), F32),
                pltpu.VMEM((19, count, rows, LANES), F32),
                pltpu.VMEM((PLANES + 1, span, LANES), F32),
            )

        pl.when(me == level)(push)


FLOW_SPANS = ((5, 38), (54, 36), (103, 34))
FLOW_ROWS = 112


def pack_flows(post, out, row):
    lane = lanes()
    total = jnp.zeros((8, LANES), F32)
    for k, q in enumerate(Z_OUT):
        v = pltpu.roll(post[q], (16 * k - zone_lane(2, 8, 1)) % LANES, 1)
        total = jnp.where((lane >= 16 * k) & (lane < 16 * k + 16), v, total)
    for group, y, base in ((Y_DOWN, 8, 80), (Y_UP, 23, 85)):
        for k, q in enumerate(group):
            lane0 = base + k
            v = pltpu.roll(post[q], (lane0 - zone_lane(2, y, 0)) % LANES, 1)
            total = jnp.where((lane == lane0) | (lane == lane0 + 25), v, total)
    out[pl.ds(row, 8), :] = total


def interface_values(zpost, zone, rim, matrix, wide):
    scale = parent_scale(3)
    for i in range(3):
        halves = []
        for half in range(2):
            rows = pl.ds(8 + 16 * i + 8 * half, 8)
            if zpost is None:
                v = [zone[q, rows, :] for q in range(19)]
            else:
                v = zone_pulled(zpost, 2, 8 + 16 * i + 8 * half)
                if zone is not None:
                    for q in range(19):
                        zone[q, rows, :] = v[q]
            v = relax(v, 1.0 - scale, scale)
            halves.append([jnp.where(rim, v[q], 0.0) for q in range(19)])
        part = jnp.concatenate([halves[half][q] for q in range(19) for half in range(2)], axis=0)
        total = moved(part, matrix[...])
        for q in range(19):
            t = total[16 * q : 16 * q + 16]
            wide[q, 0, pl.ds(PAD + 32 * i, 16, stride=2), :] = t
            wide[q, 0, pl.ds(PAD + 32 * i + 1, 16, stride=2), :] = t


def restrict_and_collide(g, zone, covered, matrix, zpost, flows, first):
    scale = child_scale(3)
    for i in range(3):
        even, odd = pl.ds(PAD + 32 * i, 16, stride=2), pl.ds(PAD + 32 * i + 1, 16, stride=2)
        part = jnp.concatenate([g[q, 0, even, :] + g[q, 0, odd, :] for q in range(19)], axis=0)
        total = moved(part, matrix[...])
        for half in range(2):
            rows = pl.ds(8 + 16 * i + 8 * half, 8)
            v = relax([total[16 * q + 8 * half : 16 * q + 8 * half + 8] for q in range(19)], 1.0 - scale, scale)
            v = [jnp.where(covered, v[q], zone[q, rows, :]) for q in range(19)]
            post = collided(v, zone[19, rows, :], 2)
            for q in range(19):
                zpost[q, rows, :] = post[q]
            pack_flows(post, flows, first + 16 * i + 8 * half)


def finest_cycle(g, pa, pb, wide, first, groups):
    mask = interface_mask(3, 0)

    def substep(v, row, dest):
        v = [jnp.where(mask, wide[q, 0, pl.ds(row, 8), :], v[q]) for q in range(19)]
        post = collided(v, g[19, 0, pl.ds(row, 8), :], 3)
        for q in range(19):
            dest[q, 0, pl.ds(row, 8), :] = post[q]

    row_loop(first, groups, lambda row: substep([g[q, 0, pl.ds(row, 8), :] for q in range(19)], row, pa))
    row_loop(first, groups, lambda row: substep(pulled(pa, 3, row, [0], True)[0], row, pb))


def finest_role(own, flags, low, high, center, left, right, g, zpost, flows):
    def scoped(pa, pb, wide, zone, widen3, restrict3, all_flows):
        widen3[...] = widen_matrix(3)
        restrict3[...] = restrict_chunk(3, 0)
        load_level(3, own, flags, low, high, g)
        load_zone(2, zone, 16, center, left, right, 8, 48)
        covered, rim = zone_masks(2, 0)
        interface_values(None, zone, rim, widen3, wide)
        for cycle in range(3):
            first, groups = (PAD, 12) if cycle < 2 else (PAD + 8, 10)

            def step_out(row):
                v = pulled(pb, 3, row, [0])[0]
                for q in range(19):
                    g[q, 0, pl.ds(row, 8), :] = v[q]

            finest_cycle(g, pa, pb, wide, first, groups)
            row_loop(first, groups, step_out)
            restrict_and_collide(g, zone, covered, restrict3, zpost, all_flows, 48 * cycle)
            if cycle < 2:
                interface_values(zpost, zone, rim, widen3, wide)
        at = 0
        for first, count in FLOW_SPANS:
            flows[pl.ds(at, count), :] = all_flows[pl.ds(first, count), :]
            at += count
        flows[pl.ds(at, FLOW_ROWS - at), :] = jnp.zeros((FLOW_ROWS - at, LANES), F32)

    rows = ROWS[3]
    pl.run_scoped(
        scoped,
        pltpu.VMEM((19, 1, rows, LANES), F32),
        pltpu.VMEM((19, 1, rows, LANES), F32),
        pltpu.VMEM((19, 1, rows, LANES), F32),
        pltpu.VMEM((20, 64, LANES), F32),
        pltpu.VMEM((2 * LANES, LANES), BF16),
        pltpu.VMEM((2 * LANES, LANES), BF16),
        pltpu.VMEM((144, LANES), F32),
    )


def last_cycle_kernel(g, zpost, state, means, far_first, far_coarse, matrices):
    row0, n = ROW0[3], OWN[3]

    @pl.when(lax.axis_index("level") == 2)
    def _():
        for k, (q, c) in enumerate(FLOW_CHUNKS):
            matrices[:, pl.ds(k * LANES, LANES)] = flow_chunk(q, c)
        for half in range(2):
            for c in range(2):
                matrices[:, pl.ds((LATE_AT + 2 * half + c) * LANES, LANES)] = late_chunk(half, c)
            matrices[:, pl.ds((LATE_AT + 4 + half) * LANES, LANES)] = late_mean_matrix(half, False)

    @pl.when(lax.axis_index("level") == 1)
    def _():
        for half in range(2):
            matrices[:, pl.ds(2 * half * LANES, 2 * LANES)] = late_back_chunk(half)

    @pl.when(lax.axis_index("level") == 0)
    def _():
        matrices[:, pl.ds(0, LANES)] = mean_back_matrix()
        matrices[:, pl.ds(LANES, 4 * LANES)] = spread_covered_matrix()

    @pl.when(lax.axis_index("level") == 3)
    def _():
        def scoped(pa, pb, wide, flat, spread, out, pairs, value, scratch, widen3):
            _, rim = zone_masks(2, 0)

            widen3[...] = widen_matrix(3)
            interface_values(zpost, None, rim, widen3, wide)
            finest_cycle(g, pa, pb, wide, PAD + 8, 10)

            def step_out(row):
                v = pulled(pb, 3, row, [0])[0]
                for q in range(19):
                    out[q, 0, pl.ds(row - row0, 8), :] = v[q]

            row_loop(row0, n // 8, step_out)
            for q in range(19):
                flat[q, pl.ds(0, 32), :] = (
                    out[q, 0, pl.ds(0, 32, stride=2), :] + out[q, 0, pl.ds(1, 32, stride=2), :]
                )
            total = None
            for i in range(4):
                part = jnp.concatenate(
                    [flat[q, pl.ds(8 * i, 8), :] for q in range(19)] + [jnp.zeros((8, LANES), F32)], axis=0
                )
                part = moved(part, compact_chunk(i))
                total = part if total is None else total + part
            scale = child_scale(3)
            v = relax([total[8 * q : 8 * q + 8] for q in range(19)], 1.0 - scale, scale)
            for q in range(19):
                means[pl.ds(8 * q, 8), :] = v[q]
            means[pl.ds(152, 8), :] = jnp.zeros((8, LANES), F32)
            pairs[...] = jnp.zeros(pairs.shape, F32)
            for q in range(19):
                pairs[pl.ds(4 * q, 4), :] = (
                    means[pl.ds(8 * q, 4, stride=2), :] + means[pl.ds(8 * q + 1, 4, stride=2), :]
                )
            for odd in range(2):
                scratch[pl.ds(0, 80), :] = moved(pairs[...], deep_matrix(odd))
                for q in range(19):
                    value[pl.ds(8 * q + 4 * odd, 4), :] = scratch[pl.ds(4 * q, 4), :]
            scale = child_scale(2)
            v = relax([value[pl.ds(8 * q, 8), :] for q in range(19)], 1.0 - scale, scale)
            deep = deep_late(lanes() & 63)
            for q in range(19):
                value[pl.ds(8 * q, 8), :] = jnp.where(deep, v[q], 0.0)
            value[pl.ds(152, 8), :] = jnp.zeros((8, LANES), F32)
            lane = lanes()
            for plane in range(3):
                total = jnp.zeros((8, LANES), F32)
                for k in range(8):
                    q = 8 * plane + k
                    if q < 19:
                        part = pltpu.roll(value[pl.ds(8 * q, 8), :], (8 * k - 4) % LANES, 1)
                        total = jnp.where(((lane & 63) >> 3) == k, part, total)
                far_first[pl.ds(8 * plane, 8), :] = total
            late_means(value, [late_mean_matrix(half, True) for half in range(2)], flat.at[:, pl.ds(0, 8)], spread.at[pl.ds(0, 20), pl.ds(0, 8)])
            packed_planes([flat[q, pl.ds(0, 8), :] for q in range(19)], far_coarse, 32)
            store_level(3, out, 0, state)

        rows = ROWS[3]
        pl.run_scoped(
            scoped,
            pltpu.VMEM((19, 1, rows, LANES), F32),
            pltpu.VMEM((19, 1, rows, LANES), F32),
            pltpu.VMEM((19, 1, rows, LANES), F32),
            pltpu.VMEM((19, 48, LANES), F32),
            pltpu.VMEM((20, 48, LANES), F32),
            pltpu.VMEM((19, 1, n, LANES), F32),
            pltpu.VMEM((80, LANES), F32),
            pltpu.VMEM((160, LANES), F32),
            pltpu.VMEM((80, LANES), F32),
            pltpu.VMEM((2 * LANES, LANES), BF16),
        )


def restrict_pairs(level, g, first, count, skip, flat):
    flat[...] = jnp.zeros(flat.shape, F32)
    for q in range(19):
        for c in range(CHUNKS[level]):
            flat[q, c, pl.ds(skip, count), :] = (
                g[q, c, pl.ds(first, count, stride=2), :] + g[q, c, pl.ds(first + 1, count, stride=2), :]
            )
    rows = flat.shape[2]
    total = None
    for c in range(CHUNKS[level]):
        part = moved(flat[:, c].reshape(flat.shape[0] * rows, LANES), restrict_chunk(level, c))
        total = part if total is None else total + part
    return total.reshape(flat.shape[0], rows, LANES)


def second_role(own, flags, low, high, center, left, right, keep_post, keep_wide, early, ring):
    level, row0 = 2, ROW0[2]
    first = row0 - 8

    def scoped(g, wide, zone, zpost, conv, spread, flat):
        load_level(level, own, flags, low, high, g)
        load_zone(1, zone, 16, center, left, right, 8, 32)
        covered, rim = zone_masks(1, 0)
        keep_post[19] = g[19]
        convert_zone(1, zone, 8, 4, rim, conv)
        widen(conv, widen_matrix(2), 2, 4, 24, wide, spread, first)
        collide_rows(level, g, g, wide, keep_post, first, 6)
        pull_rows(level, keep_post, g, first, 6)
        collide_rows(level, g, g, wide, keep_post, first, 6)
        pull_rows(level, keep_post, g, first, 6)
        spread[...] = restrict_pairs(level, g, first, 24, 4, flat)
        scale = child_scale(2)

        def restrict(i):
            row = pl.multiple_of(8 * i, 8)
            v = relax([spread[q, pl.ds(row, 8), :] for q in range(19)], 1.0 - scale, scale)
            v = [jnp.where(covered, v[q], zone[q, pl.ds(8 + row, 8), :]) for q in range(19)]
            post = collided(v, zone[19, pl.ds(8 + row, 8), :], 1)
            for q in range(19):
                zpost[q, pl.ds(8 + row, 8), :] = post[q]

        loop(4, restrict)

        def zone_pull(row):
            v = zone_pulled(zpost, 1, row)
            for q in range(19):
                zone[q, pl.ds(row, 8), :] = v[q]

        row_loop(8, 4, zone_pull)
        convert_zone(1, zone, 8, 4, rim, conv)
        widen(conv, widen_matrix(2), 2, 4, 24, keep_wide, spread, first)
        near, _ = zone_masks(1, 1)
        for q in range(19):
            for i in range(2):
                rows = pl.ds(8 * i, 8)
                early[q, rows, :] = jnp.where(near, zone[q, pl.ds(16 + 8 * i, 8), :], 0.0)
        mean = moved(early[...].reshape(19 * 16, LANES), mean_ring_matrix())
        spread[:, pl.ds(0, 16), :] = mean.reshape(19, 16, LANES)
        for q in range(19):
            ring[q] = spread[q, pl.ds(0, 8, stride=2), :] + spread[q, pl.ds(1, 8, stride=2), :]

    pl.run_scoped(
        scoped,
        pltpu.VMEM((20, 2, ROWS[2], LANES), F32),
        pltpu.VMEM((19, 2, ROWS[2], LANES), F32),
        pltpu.VMEM((20, 48, LANES), F32),
        pltpu.VMEM((19, 48, LANES), F32),
        pltpu.VMEM((19, 32, LANES), F32),
        pltpu.VMEM((19, 32, LANES), F32),
        pltpu.VMEM((19, 2, 32, LANES), F32),
    )


def first_role(own, flags, low, high, center, left, right, state, early):
    level, row0, n = 1, ROW0[1], OWN[1]
    first = row0 - 8

    def scoped(g, post, wide, zone, conv, spread, flat):
        load_level(level, own, flags, low, high, g)
        load_zone(0, zone, 12, center, left, right, 8, 16)
        y, z = zone_cell(0, lanes())
        convert_zone(0, zone, 8, 2, (z == 7) | (y == Y_LOW) | (y == Y_HIGH), conv)
        widen(conv, widen_matrix(1), 1, 0, 16, wide, spread, first)
        collide_rows(level, g, g, wide, post, first, 4)
        pull_rows(level, post, g, first, 4)
        collide_rows(level, g, g, wide, post, first, 4)
        pull_rows(level, post, g, row0, n // 8)
        store_level(level, g, row0, state)
        total = None
        for c in range(CHUNKS[1]):
            part = moved(g[pl.ds(0, 19), c, pl.ds(row0, n), :].reshape(19 * n, LANES), mean_chunk(c))
            total = part if total is None else total + part
        flat[...] = total.reshape(19, n, LANES)
        for q in range(19):
            early[q, pl.ds(0, 8), :] = flat[q, pl.ds(0, 8, stride=2), :] + flat[q, pl.ds(1, 8, stride=2), :]

    pl.run_scoped(
        scoped,
        pltpu.VMEM((20, 4, ROWS[1], LANES), F32),
        pltpu.VMEM((19, 4, ROWS[1], LANES), F32),
        pltpu.VMEM((19, 4, ROWS[1], LANES), F32),
        pltpu.VMEM((20, 32, LANES), F32),
        pltpu.VMEM((19, 16, LANES), F32),
        pltpu.VMEM((19, 16, LANES), F32),
        pltpu.VMEM((19, n, LANES), F32),
    )


def coarse_role(own, flags, low, high, state):
    level, row0 = 0, ROW0[0]

    def scoped(g, post):
        load_level(level, own, flags, low, high, g)
        collide_rows(level, g, g, None, post, row0 - 8, 3)
        pull_rows(level, post, g, row0, 1)
        store_level(level, g, row0, state)

    pl.run_scoped(
        scoped,
        pltpu.VMEM((20, 8, ROWS[0], LANES), F32),
        pltpu.VMEM((19, 8, ROWS[0], LANES), F32),
    )


def main_kernel(
    own, flags, low, high, center, left, right,
    state, fine, fine_post, flows, keep_post, keep_wide, early, ring,
):
    me = lax.axis_index("level")
    arrived = (own, flags, low, high, center, left, right)

    @pl.when(me == 3)
    def _():
        finest_role(*arrived, fine, fine_post, flows)

    @pl.when(me == 2)
    def _():
        second_role(*arrived, keep_post, keep_wide, early, ring)

    @pl.when(me == 1)
    def _():
        first_role(*arrived, state, early)

    @pl.when(me == 0)
    def _():
        coarse_role(own, flags, low, high, state)


def flow_kernel(flows, keep_post, keep_wide, ring, matrices, result, late, late_mean):
    level, row0 = 2, ROW0[2]
    first = row0 - 8

    @pl.when(lax.axis_index("level") == 2)
    def _():
        def scoped(other, post, override, flat, value, scratch, all_flows):
            all_flows[...] = jnp.zeros(all_flows.shape, F32)
            at = 0
            for start, count in FLOW_SPANS:
                all_flows[pl.ds(start, count), :] = flows[pl.ds(at, count), :]
                at += count
            total = moved(all_flows[...], matrices[:, pl.ds(0, LATE_AT * LANES)])
            for k in range(len(FLOW_CHUNKS)):
                override[k] = total[:, k * LANES : (k + 1) * LANES]
            outward = []
            for q, c in FLOW_CHUNKS:
                y, z = cell_of(2, lanes() + c * LANES)
                outward.append(flow_mask(q, y, z))

            def overridden(c, row, cycle, v):
                v = list(v)
                for k, (q, chunk) in enumerate(FLOW_CHUNKS):
                    if chunk == c:
                        value = override[k, pl.ds(48 * cycle + row - first, 8), :]
                        v[q] = jnp.where(outward[k], value, v[q])
                return v

            masks = [interface_mask(level, c) for c in range(2)]

            def begin(row):
                for c in range(2):
                    v = overridden(c, row, 0, [keep_post[q, c, pl.ds(row, 8), :] for q in range(19)])
                    for q in range(19):
                        post[q, c, pl.ds(row, 8), :] = v[q]

            row_loop(first, 6, begin)
            for cycle, source, dest in ((1, post, other), (2, other, post)):

                def body(row, cycle=cycle, source=source, dest=dest):
                    for c, v in enumerate(pulled(source, level, row, range(2))):
                        v = [jnp.where(masks[c], keep_wide[q, c, pl.ds(row, 8), :], v[q]) for q in range(19)]
                        v = collided(v, keep_post[19, c, pl.ds(row, 8), :], level)
                        v = overridden(c, row, cycle, v)
                        for q in range(19):
                            dest[q, c, pl.ds(row, 8), :] = v[q]

                row_loop(first, 6, body)

            def last(row):
                for c, v in enumerate(pulled(post, level, row, range(2))):
                    for q in range(19):
                        result[q, c, pl.ds(row - row0, 8), :] = v[q]

            row_loop(row0, 4, last)
            for q in range(19):
                for c in range(2):
                    flat[c, q] = result[q, c, pl.ds(0, 16, stride=2), :] + result[q, c, pl.ds(1, 16, stride=2), :]
            flat[:, 19] = jnp.zeros((2, 16, LANES), F32)
            total = None
            for half in range(2):
                for c in range(2):
                    part = moved(
                        flat[c, :, pl.ds(8 * half, 8), :].reshape(160, LANES),
                        matrices[:, pl.ds((LATE_AT + 2 * half + c) * LANES, LANES)],
                    )
                    total = part if total is None else total + part
            scale = child_scale(2)
            v = relax([total[8 * q : 8 * q + 8] for q in range(19)], 1.0 - scale, scale)
            for q in range(19):
                late[pl.ds(8 * q, 8), :] = v[q]
            late[pl.ds(152, 8), :] = jnp.zeros((8, LANES), F32)
            late_means(
                late, [matrices[:, pl.ds((LATE_AT + 4 + half) * LANES, LANES)] for half in range(2)], value, scratch
            )
            packed_planes([value[q] + ring[q] for q in range(19)], late_mean, 32)

        pl.run_scoped(
            scoped,
            pltpu.VMEM((19, 2, ROWS[2], LANES), F32),
            pltpu.VMEM((19, 2, ROWS[2], LANES), F32),
            pltpu.VMEM((len(FLOW_CHUNKS), 144, LANES), F32),
            pltpu.VMEM((2, 20, 16, LANES), F32),
            pltpu.VMEM((19, 8, LANES), F32),
            pltpu.VMEM((20, 8, LANES), F32),
            pltpu.VMEM((144, LANES), F32),
        )


def prepare_kernel(early, far, far_coarse, means, matrices, covered, near):
    me = lax.axis_index("level")

    @pl.when(me == 2)
    def _():
        for i in range(4):
            total = moved(means[...], spread_chunk(i))
            for c in range(2):
                covered[2 * i + c] = total[:, c * LANES : (c + 1) * LANES]

    @pl.when(me == 1)
    def _():
        total = moved(early[...].reshape(19 * 16, LANES), spread_zone_matrix())
        for c in range(4):
            near[c] = total[:, c * LANES : (c + 1) * LANES]

    @pl.when(me == 0)
    def _():
        def scoped(value):
            lane = lanes()
            for q in range(19):
                rows = pl.ds(8 * (q // 4), 8)
                part = far[rows, :] + far_coarse[rows, :]
                if q % 4:
                    part = pltpu.roll(part, LANES - 32 * (q % 4), 1)
                value[q] = jnp.where(lane < 32, part, 0.0)
            value[19] = jnp.zeros((8, LANES), F32)
            total = moved(value[...].reshape(160, LANES), matrices[:, pl.ds(0, LANES)])
            scale = child_scale(1)
            v = relax(
                [early[q, pl.ds(0, 8), :] + total[8 * q : 8 * q + 8] for q in range(19)],
                1.0 - scale,
                scale,
            )
            for q in range(19):
                value[q] = v[q]
            total = moved(value[...].reshape(160, LANES), matrices[:, pl.ds(LANES, 4 * LANES)])
            for c in range(4):
                covered[c] = total[:, c * LANES : (c + 1) * LANES]

        pl.run_scoped(scoped, pltpu.VMEM((20, 8, LANES), F32))


def finish_kernel(old_state, result, third_state, late, far, covered_values, near, matrices, state):
    me = lax.axis_index("level")

    @pl.when(me == 3)
    def _():
        state[...] = third_state[...]

    @pl.when(me == 2)
    def _():
        def scoped(g):
            for c in range(2):
                y, z = cell_of(2, lanes() + c * LANES)
                covered = (y >= Y_LOW) & (y <= Y_HIGH) & (z <= 1)

                def insert(q, c=c, covered=covered):
                    for i in range(4):
                        rows = pl.ds(8 * i, 8)
                        value = covered_values[2 * i + c, pl.ds(pl.multiple_of(8 * q, 8), 8), :]
                        g[q, c, rows, :] = jnp.where(covered, value, result[q, c, rows, :])

                loop(19, insert, 19)
            store_level(2, g, 0, state)

        pl.run_scoped(scoped, pltpu.VMEM((19, 2, OWN[2], LANES), F32))

    @pl.when(me == 1)
    def _():
        def scoped(inner, value):
            lane = lanes()
            deep = deep_late(lane & 63)
            for q in range(19):
                part = pltpu.roll(far[pl.ds(8 * (q // 8), 8), :], (4 - 8 * (q % 8)) % LANES, 1)
                value[pl.ds(8 * q, 8), :] = jnp.where(deep, part, late[pl.ds(8 * q, 8), :])
            value[pl.ds(152, 8), :] = jnp.zeros((8, LANES), F32)
            for half in range(2):
                total = moved(value[...], matrices[:, pl.ds(2 * half * LANES, 2 * LANES)])
                for c in range(2):
                    part = total[:, c * LANES : (c + 1) * LANES].reshape(20, 8, LANES)
                    inner[c, :, pl.ds(8 * half, 8), :] = part

            def one(q):
                for j in range(8):
                    c = j % 4
                    y, z = cell_of(1, lanes() + c * LANES)
                    columns = pl.ds(j * LANES, LANES)
                    rows = pl.ds(j // 4, 8, stride=2)
                    ring = near[c, pl.ds(16 * q + j // 4, 8, stride=2), :]
                    value = jnp.where(near_first(y, z), ring, old_state[q, :, columns])
                    if c in (1, 2):
                        value = jnp.where(covered_first(y, z), inner[c - 1, q, rows, :], value)
                    state[q, :, columns] = value

            loop(19, one)

        pl.run_scoped(
            scoped,
            pltpu.VMEM((2, 20, 16, LANES), F32),
            pltpu.VMEM((160, LANES), F32),
        )

    @pl.when(me == 0)
    def _():
        covered = (lanes() & 31) < 8

        def one(q):
            rows = pl.ds(pl.multiple_of(8 * q, 8), 8)
            for j in range(8):
                columns = pl.ds(j * LANES, LANES)
                value = old_state[q, :, columns]
                if 2 <= j < 6:
                    value = jnp.where(covered, covered_values[j - 2, rows, :], value)
                state[q, :, columns] = value

        loop(19, one, 19)


def call(kernel, shapes, args, micros):
    return pl.pallas_call(
        kernel,
        out_shape=[
            jax.ShapeDtypeStruct(s[:-1], BF16) if s[-1] is BF16 else jax.ShapeDtypeStruct(s, F32) for s in shapes
        ],
        in_specs=[pl.BlockSpec(memory_space=pltpu.VMEM)] * len(args),
        out_specs=[pl.BlockSpec(memory_space=pltpu.VMEM)] * len(shapes),
        cost_estimate=pl.CostEstimate(
            flops=int(micros * 1e9), bytes_accessed=int(micros * 3.6e6), transcendentals=0
        ),
        compiler_params=pltpu.CompilerParams(vmem_limit_bytes=24 * 1024 * 1024),
    )(*args)


def shards(populations, solid):
    if populations.shape[1:] != (19, SLAB, NY * NZ):
        raise ValueError("unexpected slab")
    own, flags = populations[0], solid[0].astype(F32)
    blocks = lax.axis_size("blocks")
    forward = [(i, (i + 1) % blocks) for i in range(blocks)]
    backward = [(i, (i - 1) % blocks) for i in range(blocks)]
    down = [(i, i + 1) for i in range(LEVELS - 1)]

    def diagonal(step):
        return [
            (level * blocks + b, (level + 1) * blocks + (b + step) % blocks)
            for level in range(LEVELS - 1)
            for b in range(blocks)
        ]

    both = ("level", "blocks")
    to_right, to_left, center, zone_right, zone_left = call(
        start_kernel,
        [(20, 16, LANES), (20, 16, LANES), (CENTER_ROWS, LANES), (PLANES + 1, 8, LANES), (PLANES + 1, 8, LANES)],
        [own, flags],
        1.5,
    )
    center = lax.ppermute(center, "level", down)
    left = lax.ppermute(zone_right, both, diagonal(1))
    right = lax.ppermute(zone_left, both, diagonal(-1))
    low = lax.ppermute(to_right, "blocks", forward)
    high = lax.ppermute(to_left, "blocks", backward)

    full = (19, SLAB, NY * NZ)
    state, fine, fine_post, flows, keep_post, keep_wide, early, ring = call(
        main_kernel,
        [
            full,
            (20, 1, ROWS[3], LANES),
            (19, 64, LANES),
            (FLOW_ROWS, LANES),
            (20, 2, ROWS[2], LANES),
            (19, 2, ROWS[2], LANES),
            (19, 16, LANES),
            (19, 8, LANES),
        ],
        [own, flags, low, high, center, left, right],
        8.0,
    )
    flows = lax.ppermute(flows, "level", [(3, 2)])
    early = lax.ppermute(early, "level", [(2, 1), (1, 0)])
    third_state, means, far_first, far_coarse, matrices = call(
        last_cycle_kernel,
        [full, (160, LANES), (40, LANES), (40, LANES), (2 * LANES, (LATE_AT + 6) * LANES, BF16)],
        [fine, fine_post],
        4.0,
    )
    far_coarse = lax.ppermute(far_coarse, "level", [(3, 0)])
    means = lax.ppermute(means, "level", [(3, 2)])
    result, late, late_mean = call(
        flow_kernel,
        [(19, 2, OWN[2], LANES), (160, LANES), (40, LANES)],
        [flows, keep_post, keep_wide, ring, matrices],
        2.5,
    )
    me = lax.axis_index("level")
    far = lax.ppermute(jnp.where(me == 3, far_first, late_mean), "level", [(3, 1), (2, 0)])
    late = lax.ppermute(late, "level", [(2, 1)])
    covered, near = call(
        prepare_kernel, [(8, 160, LANES), (4, 304, LANES)], [early, far, far_coarse, means, matrices], 4.0
    )
    (state,) = call(
        finish_kernel, [full], [state, result, third_state, late, far, covered, near, matrices], 1.0
    )
    return state[None]


def solution(mesh):
    in_specs = (P("level", None, "blocks", None), P("level", "blocks", None))
    out_specs = P("level", None, "blocks", None)
    return jax.shard_map(shards, mesh=mesh, in_specs=in_specs, out_specs=out_specs, check_vma=False)
```
